128 devices in a mesh: seq: 64 (over y, x, z), wt: 2 (over core).
Axes of the slice: x: 4, y: 4, z: 4, core: 2. Of those that a mesh axis runs over, the one named last changes fastest.
Arguments:
- block_in: bfloat16 [8192, 1600], P('seq'), may hold values from -6 to 6
- in_gain: bfloat16 [1600], P('seq'), may hold values from 0.5 to 1.5
- w_query: bfloat16 [1600, 1600], P('seq'), may hold values from -0.15625 to 0.15625
- w_keyval: bfloat16 [1600, 2, 320], P('seq'), may hold values from -0.15625 to 0.15625
- w_out: bfloat16 [1600, 1600], P(None, 'seq'), may hold values from -0.15625 to 0.15625
- attn_gain: bfloat16 [1600], P('seq'), may hold values from 0.5 to 1.5
- ssm_gain: bfloat16 [1600], P('seq'), may hold values from 0.5 to 1.5
- inner_weight: bfloat16 [1600, 2, 3200], P(None, None, ('seq', 'wt')), may hold values from -0.15625 to 0.15625
- conv_weight: bfloat16 [4, 3200], P(None, ('seq', 'wt')), may hold values from -3 to 3
- conv_bias: bfloat16 [3200], P(('seq', 'wt')), may hold values from -3 to 3
- w_xproj: bfloat16 [3200, 132], P(('seq', 'wt')), may hold values from -0.109375 to 0.109375
- w_delta: bfloat16 [100, 3200], P(None, ('seq', 'wt')), may hold values from -0.625 to 0.625
- delta_bias: bfloat16 [3200], P(('seq', 'wt')), may hold values from -6 to -3
- log_decay: bfloat16 [16, 3200], P(None, ('seq', 'wt')), may hold values from -9 to 2.796875
- skip_gain: bfloat16 [3200], P(('seq', 'wt')), may hold values from 0.5 to 1.5
- w_ssmout: bfloat16 [3200, 1600], P(('seq', 'wt')), may hold values from -0.109375 to 0.109375
- mlp_gain: bfloat16 [1600], P('seq'), may hold values from 0.5 to 1.5
- w_gateup: bfloat16 [1600, 2, 5504], P('seq', None, 'wt'), may hold values from -0.15625 to 0.15625
- w_down: bfloat16 [5504, 1600], P('wt', 'seq'), may hold values from -0.078125 to 0.078125
- cotangent: bfloat16 [8192, 1600], P('seq'), may hold values from -6 to 6
Outputs:
- block_out: bfloat16 [8192, 1600], P('seq')
- grad_in: float32 [8192, 1600], P('seq')
- grad_in_gain: float32 [1600], P('seq')
- grad_w_query: float32 [1600, 1600], P('seq')
- grad_w_keyval: float32 [1600, 2, 320], P('seq')
- grad_w_out: float32 [1600, 1600], P(None, 'seq')
- grad_attn_gain: float32 [1600], P('seq')
- grad_ssm_gain: float32 [1600], P('seq')
- grad_w_inner: float32 [1600, 2, 3200], P(None, None, ('seq', 'wt'))
- grad_conv_weight: float32 [4, 3200], P(None, ('seq', 'wt'))
- grad_conv_bias: float32 [3200], P(('seq', 'wt'))
- grad_w_xproj: float32 [3200, 132], P(('seq', 'wt'))
- grad_w_delta: float32 [100, 3200], P(None, ('seq', 'wt'))
- grad_delta_bias: float32 [3200], P(('seq', 'wt'))
- grad_log_decay: float32 [16, 3200], P(None, ('seq', 'wt'))
- grad_skip_gain: float32 [3200], P(('seq', 'wt'))
- grad_w_ssmout: float32 [3200, 1600], P(('seq', 'wt'))
- grad_mlp_gain: float32 [1600], P('seq')
- derivative_switch_lift_matrix: float32 [1600, 2, 5504], P('seq', None, 'wt')
- grad_w_down: float32 [5504, 1600], P('wt', 'seq')
The draws below stay inside these ranges and needn't reach their ends.
All inputs are finite; a program needn't handle non-finite values.
Results may differ from the reference program's by a relative error of at most 0.019.
Values may be sent and summed in bfloat16 or wider, within the bound.
No kernel may reach another device: no remote copies, remote signals or barrier semaphores. Data moves between devices by JAX's collectives and lax.ppermute only.
A program may use at most 384 MiB of HBM per device.

```python
import math
import jax
import jax.numpy as jnp
from jax import lax

D = 1600
HEADS = 25
KV_HEADS = 5
HEAD = 64
INNER = 3200
STATE = 16
DTR = 100
CONV = 4
FF = 5504
WINDOW = 1024
TOKENS = 8192
QW = 1600
KVW = 320
XW = 132


def levels(rng, dims, pieces, low, top_value):
    def one(axis_at, blocks):
        steps = jax.random.uniform(jax.random.fold_in(jax.random.fold_in(rng, 6), axis_at), (blocks,), jnp.float32, low / len(pieces), top_value / len(pieces))
        return jnp.repeat(jnp.exp(steps), dims[axis_at] // blocks).reshape((-1,) + (1,) * (len(dims) - axis_at - 1))

    loudness = one(*pieces[0])
    for cut in pieces[1:]:
        loudness = loudness * one(*cut)
    return loudness


def bell_draw(own_key, dims, width, reach, cuts=(), kind=jnp.bfloat16):
    entries = jax.random.normal(own_key, dims, jnp.float32) * width
    if len(cuts) > 0:
        entries = levels(own_key, dims, cuts, -0.22, 0.18) * entries
    return jnp.clip(entries, min=-reach, max=reach).astype(kind)


def setup_inputs(seed: int = 0) -> dict:
    streams_of = jax.random.split(jax.random.key(seed), 21)
    block_in = bell_draw(streams_of[0], (TOKENS, D), 1.0, 6.0, ((0, 64),))
    in_gain = jnp.clip(1.0 + 0.1 * jax.random.normal(streams_of[1], (D,), jnp.float32), 0.5, 1.5).astype(jnp.bfloat16)
    w_query = bell_draw(streams_of[2], (D, QW), D ** -0.5, 0.15625, ((0, 64),))
    w_keyval = bell_draw(streams_of[3], (D, 2, KVW), D ** -0.5, 0.15625, ((0, 64),))
    w_out = bell_draw(streams_of[4], (QW, D), QW ** -0.5, 0.15625, ((1, 64),))
    attn_gain = jnp.clip(1.0 + 0.1 * jax.random.normal(streams_of[5], (D,), jnp.float32), 0.5, 1.5).astype(jnp.bfloat16)
    ssm_gain = jnp.clip(1.0 + 0.1 * jax.random.normal(streams_of[6], (D,), jnp.float32), 0.5, 1.5).astype(jnp.bfloat16)
    inner_weight = bell_draw(streams_of[7], (D, 2, INNER), D ** -0.5, 0.15625, ((2, 128),))
    conv_weight = bell_draw(streams_of[8], (CONV, INNER), 0.5, 3.0, ((1, 128),))
    conv_bias = bell_draw(streams_of[9], (INNER,), 0.5, 3.0, ((0, 128),))
    w_xproj = bell_draw(streams_of[10], (INNER, XW), INNER ** -0.5, 0.109375, ((0, 128),))
    w_delta = bell_draw(streams_of[11], (DTR, INNER), DTR ** -0.5, 0.625, ((1, 128),))
    delta_bias = jnp.clip(-6.0 + 3.0 * jax.random.uniform(streams_of[12], (INNER,), jnp.float32) ** levels(streams_of[12], (INNER,), ((0, 128),), -0.2, 0.2), -6.0, -3.0).astype(jnp.bfloat16)
    log_decay = jnp.clip(-9.0 + 11.796875 * jax.random.uniform(streams_of[13], (STATE, INNER), jnp.float32) ** levels(streams_of[13], (STATE, INNER), ((1, 128),), -0.2, 0.2), -9.0, 2.796875).astype(jnp.bfloat16)
    skip_gain = jnp.clip(0.5 + 1.0 * jax.random.uniform(streams_of[14], (INNER,), jnp.float32) ** levels(streams_of[14], (INNER,), ((0, 128),), -0.2, 0.2), 0.5, 1.5).astype(jnp.bfloat16)
    w_ssmout = bell_draw(streams_of[15], (INNER, D), INNER ** -0.5, 0.109375, ((0, 128),))
    mlp_gain = jnp.clip(1.0 + 0.1 * jax.random.normal(streams_of[16], (D,), jnp.float32), 0.5, 1.5).astype(jnp.bfloat16)
    w_gateup = bell_draw(streams_of[17], (D, 2, FF), D ** -0.5, 0.15625, ((0, 64), (2, 2)))
    w_down = bell_draw(streams_of[18], (FF, D), FF ** -0.5, 0.078125, ((0, 2), (1, 64)))
    cotangent = bell_draw(streams_of[19], (TOKENS, D), 1.0, 6.0, ((0, 64),))
    return dict(block_in=block_in, in_gain=in_gain, w_query=w_query, w_keyval=w_keyval, w_out=w_out, attn_gain=attn_gain, ssm_gain=ssm_gain, inner_weight=inner_weight, conv_weight=conv_weight, conv_bias=conv_bias, w_xproj=w_xproj, w_delta=w_delta, delta_bias=delta_bias, log_decay=log_decay, skip_gain=skip_gain, w_ssmout=w_ssmout, mlp_gain=mlp_gain, w_gateup=w_gateup, w_down=w_down, cotangent=cotangent)


EPS = 1e-06
PRECISE_MODE = lax.Precision.HIGHEST

@jax.custom_vjp
def reduced_precision(v):
    return lax.optimization_barrier(v.astype(jnp.bfloat16)).astype(jnp.float32)

@jax.custom_vjp
def reduced_backward(v):
    return v

def low_keep(v):
    return (reduced_precision(v), None)

def low_pass(kept, grad):
    return (grad,)

def back_keep(v):
    return (v, None)

def back_low(kept, grad):
    return (reduced_precision(grad),)
reduced_precision.defvjp(low_keep, low_pass)
reduced_backward.defvjp(back_keep, back_low)

def matmul(left, right):
    return jnp.dot(left, right, precision=PRECISE_MODE, preferred_element_type=jnp.float32)

def root_square_normalizer(value, gain):
    return value * lax.rsqrt(lax.optimization_barrier(jnp.mean(value * value, axis=-1, keepdims=True)) + EPS) * gain

def attend_block(queries, keyrows, start):
    rows = queries.shape[0]
    keys = keyrows[:, 0].reshape(-1, KV_HEADS, HEAD)
    values = keyrows[:, 1].reshape(-1, KV_HEADS, HEAD)
    scores = reduced_backward(jnp.einsum('tkgd,skd->kgts', queries, keys, precision=PRECISE_MODE) * HEAD ** (-0.5))
    qpos = start + jnp.arange(rows, dtype=jnp.int32)
    kpos = start - WINDOW + jnp.arange(WINDOW + rows, dtype=jnp.int32)
    gap = qpos[:, None] - kpos[None, :]
    allowed = (gap >= 0) & (gap < WINDOW) & (kpos[None, :] >= 0)
    scores = jnp.where(allowed, scores, -1e+30)
    total = jax.nn.logsumexp(scores, axis=-1, keepdims=True)
    probs = reduced_precision(jnp.exp(scores - total))
    return jnp.einsum('kgts,skd->tkgd', probs, values, precision=PRECISE_MODE)

def attention(query, keyval):
    group = HEADS // KV_HEADS
    block = 512 if TOKENS % 512 == 0 else TOKENS
    grouped = query.reshape(TOKENS, KV_HEADS, group, HEAD)
    padded = jnp.concatenate([jnp.zeros((WINDOW, 2, KV_HEADS * HEAD), jnp.float32), keyval], 0)

    def one_block(start):
        queries = lax.dynamic_slice_in_dim(grouped, start, block, 0)
        keyrows = lax.dynamic_slice_in_dim(padded, start, WINDOW + block, 0)
        return jax.checkpoint(attend_block)(queries, keyrows, start)
    starts = jnp.arange(TOKENS // block, dtype=jnp.int32) * block
    return lax.map(one_block, starts).reshape(TOKENS, HEADS * HEAD)

def selective_scan(step, mixer_in, in_mix, combined_result_matrix, rate):
    span = math.gcd(TOKENS, 128)
    count = TOKENS // span

    def one_token(state, inputs):
        delta, value, in_row, out_row = inputs
        state = jnp.exp(delta[None, :] * rate) * state + (delta * value)[None, :] * in_row[:, None]
        return (state, lax.optimization_barrier(jnp.sum(out_row[:, None] * state, axis=0)))

    def one_block(state, inputs):
        return lax.scan(one_token, state, inputs)

    def split(array):
        return array.reshape(count, span, array.shape[1])
    start_state = jnp.zeros((STATE, INNER), jnp.float32)
    _, outputs = lax.scan(jax.checkpoint(one_block), start_state, (split(step), split(mixer_in), split(in_mix), split(combined_result_matrix)))
    return outputs.reshape(TOKENS, INNER)

def forward(block_in, in_gain, w_query, w_keyval, w_out, attn_gain, ssm_gain, inner_weight, conv_weight, conv_bias, w_xproj, w_delta, delta_bias, log_decay, skip_gain, w_ssmout, mlp_gain, w_gateup, w_down):
    first_residual = reduced_precision(root_square_normalizer(block_in, in_gain))
    query = reduced_backward(reduced_precision(matmul(first_residual, w_query)))
    keyval = reduced_backward(reduced_precision(jnp.einsum('td,dck->tck', first_residual, w_keyval, precision=PRECISE_MODE)))
    attended = reduced_backward(reduced_precision(attention(query, keyval)))
    attn_out = reduced_backward(matmul(attended, w_out))
    inner_projection = reduced_backward(reduced_precision(jnp.einsum('yn,nhb->yhb', first_residual, inner_weight, precision=PRECISE_MODE)))
    conv_in = inner_projection[:, 0]
    gate_z = inner_projection[:, 1]
    padded_in = jnp.concatenate([jnp.zeros((CONV - 1, INNER), jnp.float32), conv_in], 0)
    conv_out = conv_bias + jnp.zeros((TOKENS, INNER), jnp.float32)
    for tap in range(CONV):
        conv_out = conv_out + conv_weight[tap] * padded_in[tap:tap + TOKENS]
    mixer_in = reduced_precision(jax.nn.silu(conv_out))
    xproj = reduced_backward(matmul(mixer_in, w_xproj))
    step_low = reduced_precision(xproj[:, :DTR])
    in_mix = xproj[:, DTR:DTR + STATE]
    combined_result_matrix = xproj[:, DTR + STATE:]
    step = jax.nn.softplus(reduced_backward(matmul(step_low, w_delta)) + delta_bias)
    ssm_y = selective_scan(step, mixer_in, in_mix, combined_result_matrix, -jnp.exp(log_decay)) + skip_gain * mixer_in
    mixer_act = reduced_precision(ssm_y * jax.nn.silu(gate_z))
    mixer_out = reduced_backward(matmul(mixer_act, w_ssmout))
    hidden = block_in + 0.5 * (root_square_normalizer(attn_out, attn_gain) + root_square_normalizer(mixer_out, ssm_gain))
    x_two = reduced_precision(root_square_normalizer(hidden, mlp_gain))
    gate_up = reduced_backward(reduced_precision(jnp.einsum('td,dcf->tcf', x_two, w_gateup, precision=PRECISE_MODE)))
    mlp_act = reduced_precision(jax.nn.silu(gate_up[:, 0]) * gate_up[:, 1])
    return hidden + matmul(mlp_act, w_down)

def reference(block_in, in_gain, w_query, w_keyval, w_out, attn_gain, ssm_gain, inner_weight, conv_weight, conv_bias, w_xproj, w_delta, delta_bias, log_decay, skip_gain, w_ssmout, mlp_gain, w_gateup, w_down, cotangent):
    values = [item.astype(jnp.float32) for item in (block_in, in_gain, w_query, w_keyval, w_out, attn_gain, ssm_gain, inner_weight, conv_weight, conv_bias, w_xproj, w_delta, delta_bias, log_decay, skip_gain, w_ssmout, mlp_gain, w_gateup, w_down)]
    result, pullback = jax.vjp(forward, *values)
    grads = pullback(cotangent.astype(jnp.float32))
    return (result.astype(jnp.bfloat16), grads[0], grads[1], grads[2], grads[3], grads[4], grads[5], grads[6], grads[7], grads[8], grads[9], grads[10], grads[11], grads[12], grads[13], grads[14], grads[15], grads[16], grads[17], grads[18])
```

```python
import functools
import math

import jax
import jax.numpy as jnp
from jax import lax
from jax.experimental import pallas as pl
from jax.experimental.pallas import tpu as pltpu
from jax.sharding import Mesh
from jax.sharding import PartitionSpec as P

F32 = jnp.float32
BF16 = jnp.bfloat16

HEADS = 25
KV_HEADS = 5
GROUP = HEADS // KV_HEADS
HEAD = 64
STATE = 16
DTR = 100
CONV = 4
WINDOW = 1024
D = 1600
QW = GROUP * HEAD
EPS = 1e-06
LOG2E = math.log2(math.e)

YX = ("y", "x")
SEQ = ("y", "x", "z")
RING = 4
LINES = 16
PIECE = 25
ROWS = RING * PIECE
ROWS_PAD = 104
DP = LINES * ROWS_PAD
CH_PAD = 32
CH = LINES * CH_PAD
SPAN = 64
CHUNKS = 8
TOK = SPAN * CHUNKS
FF_PIECE = 688
FF_PAD = 768
ATT_COLS = 768
RANK_PAD = 104
XROWS = RANK_PAD + 2 * STATE
SMALL = 128
SMALL_USED = CONV + 3 + STATE
COLS = (0, DP, 2 * DP, 3 * DP, 3 * DP + 256, 3 * DP + 384, 3 * DP + 512)


def dot(left, right, dims):
    return lax.dot_general(left, right, (dims, ((), ())), preferred_element_type=F32)


def nn(left, right):
    return dot(left, right, ((1,), (0,)))


def nt(left, right):
    return dot(left, right, ((1,), (1,)))


def tn(left, right):
    return dot(left, right, ((0,), (0,)))


def low(value):
    return value.astype(BF16)


def pad_features(value):
    lead = value.shape[:-1]
    value = value.reshape(lead + (LINES, ROWS))
    value = jnp.pad(value, [(0, 0)] * (len(lead) + 1) + [(0, ROWS_PAD - ROWS)])
    return value.reshape(lead + (DP,))


def drop_features(value):
    lead = value.shape[:-1]
    return value.reshape(lead + (LINES, ROWS_PAD))[..., :ROWS].reshape(lead + (D,))


def step_to(axis, distance):
    return [(i, (i + distance) % RING) for i in range(RING)]


def around(value, axis):
    return [value] + [lax.ppermute(value, axis, step_to(axis, RING - d)) for d in range(1, RING)]


def in_order(blocks, axis):
    twice = jnp.stack(blocks + blocks[: RING - 1])
    first = (RING - lax.axis_index(axis)) % RING
    return lax.dynamic_slice_in_dim(twice, first, RING, 0)


def swap_core(value):
    return lax.ppermute(value, "wt", [(0, 1), (1, 0)])


def exchange(pieces, axis):
    here = lax.axis_index(axis)
    got = [lax.dynamic_index_in_dim(pieces, here, 0, False)]
    for d in range(1, RING):
        piece = lax.dynamic_index_in_dim(pieces, (here + RING - d) % RING, 0, False)
        got.append(lax.ppermute(piece, axis, step_to(axis, RING - d)))
    return in_order(got, axis)


def gather_tokens(own, ordered):
    blocks = around(own, "z")
    if ordered:
        mine = in_order(blocks, "z")
        other = swap_core(mine)
        first = lax.axis_index("wt") == 0
        both = jnp.stack([jnp.where(first, mine, other), jnp.where(first, other, mine)], axis=1)
        return both.reshape((TOK,) + own.shape[1:])
    mine = jnp.concatenate(blocks, 0)
    return jnp.concatenate([mine, swap_core(mine)], 0)


def scatter_tokens(partial, ordered):
    wide = partial.shape[1]
    if ordered:
        core = lax.axis_index("wt")
        parts = partial.reshape(RING, 2, SPAN, wide)
        mine = lax.dynamic_index_in_dim(parts, core, 1, False)
        theirs = lax.dynamic_index_in_dim(parts, 1 - core, 1, False)
    else:
        parts = partial.reshape(2, RING, SPAN, wide)
        mine, theirs = parts[0], parts[1]
    mine = mine + swap_core(low(theirs)).astype(F32)
    here = lax.axis_index("z")
    total = None
    for d in range(RING):
        if ordered:
            piece = lax.dynamic_index_in_dim(mine, (here + d) % RING, 0, False)
        else:
            piece = mine[d]
        if d:
            piece = lax.ppermute(low(piece), "z", step_to("z", d)).astype(F32)
        total = piece if total is None else total + piece
    return total


def sum_line(value):
    value = value + swap_core(value)
    half = value.shape[1] // 2
    core = lax.axis_index("wt")
    mine = lax.dynamic_slice_in_dim(value, core * half, half, 1)
    blocks = around(mine, "z")
    mine = (blocks[0] + blocks[2]) + (blocks[1] + blocks[3])
    other = swap_core(mine)
    first = core == 0
    return jnp.concatenate([jnp.where(first, mine, other), jnp.where(first, other, mine)], 1)


def sum_all(value):
    value = value + swap_core(value)
    for axis in SEQ:
        blocks = around(value, axis)
        value = (blocks[0] + blocks[2]) + (blocks[1] + blocks[3])
    return value


def line_shift(value, distance):
    route = [(i, i + distance) for i in range(LINES) if 0 <= i + distance < LINES]
    return lax.ppermute(value, YX, route)


def rms(value, gain):
    scale = lax.rsqrt(jnp.sum(value * value, axis=-1, keepdims=True) / D + EPS)
    return value * scale * gain


def rms_back(value, gain, dy):
    r = lax.rsqrt(jnp.sum(value * value, axis=-1, keepdims=True) / D + EPS)
    inner = jnp.sum(value * gain * dy, axis=-1, keepdims=True) / D
    return r * gain * dy - value * (r * r * r) * inner, jnp.sum(value * r * dy, axis=0)


def silu_grad(value):
    sig = jax.nn.sigmoid(value)
    return sig * (1.0 + value * (1.0 - sig))


def rows_at(ref, tau):
    return ref[pl.ds(tau, CHUNKS, stride=SPAN), :]


def spread(rows):
    rows = jnp.transpose(rows.reshape(STATE, CHUNKS, SPAN), (2, 0, 1))
    return jnp.broadcast_to(rows[..., None], (SPAN, STATE, CHUNKS, 128))


def rate_rows(rate_ref):
    return [jnp.broadcast_to(rate_ref[n : n + 1, :], (CHUNKS, 128)) for n in range(STATE)]


def zeros():
    return jnp.zeros((CHUNKS, 128), F32)


def ends_kernel(step_ref, in_ref, b_ref, rate_ref, end_ref, span_ref):
    rates = rate_rows(rate_ref)

    def token(tau, carry):
        states, total = carry
        step = rows_at(step_ref, tau)
        push = step * rows_at(in_ref, tau)
        states = [jnp.exp2(step * rates[n]) * states[n] + push * b_ref[tau, n] for n in range(STATE)]
        return states, total + step

    states, total = lax.fori_loop(0, SPAN, token, ([zeros()] * STATE, zeros()), unroll=8)
    for n in range(STATE):
        end_ref[n] = states[n]
    span_ref[...] = total


def outputs_kernel(step_ref, in_ref, b_ref, c_ref, rate_ref, init_ref, y_ref):
    rates = rate_rows(rate_ref)

    def token(tau, states):
        step = rows_at(step_ref, tau)
        push = step * rows_at(in_ref, tau)
        states = [jnp.exp2(step * rates[n]) * states[n] + push * b_ref[tau, n] for n in range(STATE)]
        y_ref[pl.ds(tau, CHUNKS, stride=SPAN), :] = sum(c_ref[tau, n] * states[n] for n in range(STATE))
        return states

    lax.fori_loop(0, SPAN, token, [init_ref[n] for n in range(STATE)], unroll=8)


def heads_kernel(step_ref, dy_ref, c_ref, rate_ref, head_ref):
    rates = rate_rows(rate_ref)

    def token(back, carry):
        tau = SPAN - 1 - back
        step = rows_at(step_ref, tau)
        dy = rows_at(dy_ref, tau)
        return [jnp.exp2(step * rates[n]) * (c_ref[tau, n] * dy + carry[n]) for n in range(STATE)]

    carry = lax.fori_loop(0, SPAN, token, [zeros()] * STATE, unroll=8)
    for n in range(STATE):
        head_ref[n] = carry[n]


def backward_kernel(
    step_ref, in_ref, dy_ref, b_ref, c_ref, rate_ref, init_ref, lam_ref,
    dstep_ref, lamb_ref, ddecay_ref, dmix_ref,
    a_ref, h_ref, din_ref, dout_ref,
):
    rates = rate_rows(rate_ref)

    @pl.when(pl.program_id(0) == 0)
    def _():
        @pl.loop(0, SPAN)
        def _(tau):
            din_ref[tau] = jnp.zeros((STATE, CHUNKS, 128), F32)
            dout_ref[tau] = jnp.zeros((STATE, CHUNKS, 128), F32)

    for n in range(STATE):
        h_ref[0, n] = init_ref[n]

    def forth(tau, states):
        step = rows_at(step_ref, tau)
        push = step * rows_at(in_ref, tau)
        states = list(states)
        for n in range(STATE):
            decay = jnp.exp2(step * rates[n])
            a_ref[tau, n] = decay
            states[n] = decay * states[n] + push * b_ref[tau, n]
            h_ref[tau + 1, n] = states[n]
        return states

    lax.fori_loop(0, SPAN, forth, [init_ref[n] for n in range(STATE)], unroll=4)

    def back(backwards, carry):
        tau = SPAN - 1 - backwards
        lams, decays = list(carry[0]), list(carry[1])
        step = rows_at(step_ref, tau)
        push = step * rows_at(in_ref, tau)
        dy = rows_at(dy_ref, tau)
        dstep, lamb = zeros(), zeros()
        for n in range(STATE):
            lam = c_ref[tau, n] * dy + lams[n]
            lams[n] = a_ref[tau, n] * lam
            along = lams[n] * h_ref[tau, n]
            dstep = dstep + along * rates[n]
            lamb = lamb + lam * b_ref[tau, n]
            decays[n] = decays[n] + along * step
            din_ref[tau, n] += lam * push
            dout_ref[tau, n] += dy * h_ref[tau + 1, n]
        dstep_ref[pl.ds(tau, CHUNKS, stride=SPAN), :] = dstep * (1.0 / LOG2E)
        lamb_ref[pl.ds(tau, CHUNKS, stride=SPAN), :] = lamb
        return lams, decays

    start = ([lam_ref[n] for n in range(STATE)], [zeros()] * STATE)
    _, decays = lax.fori_loop(0, SPAN, back, start, unroll=4)
    for n in range(STATE):
        ddecay_ref[n] = decays[n]

    @pl.when(pl.program_id(0) == pl.num_programs(0) - 1)
    def _():
        lane = lax.broadcasted_iota(jnp.int32, (CHUNKS, 128), 1)

        def fold(tau, carry):
            rows = zeros()
            for n in range(STATE):
                rows = jnp.where(lane == n, jnp.sum(din_ref[tau, n], axis=1, keepdims=True), rows)
                total = jnp.sum(dout_ref[tau, n], axis=1, keepdims=True)
                rows = jnp.where(lane == STATE + n, total, rows)
            dmix_ref[pl.ds(tau, CHUNKS, stride=SPAN), :] = rows
            return carry

        lax.fori_loop(0, SPAN, fold, 0, unroll=8)


def cost(micros):
    return pl.CostEstimate(flops=int(micros * 1e9), bytes_accessed=int(micros * 3e6), transcendentals=0)


def scan_call(kernel, ins, outs, scratch, micros):
    wide = (SPAN, STATE, CHUNKS, 128)
    once = pl.BlockSpec(wide, lambda i: (0, 0, 0, 0), pipeline_mode=pl.Buffered(1))
    kinds = {
        "tok": ((TOK, CH), pl.BlockSpec((TOK, 128), lambda i: (0, i))),
        "mix": ((TOK, 128), pl.BlockSpec((TOK, 128), lambda i: (0, 0))),
        "rate": ((STATE, CH), pl.BlockSpec((STATE, 128), lambda i: (0, i))),
        "state": ((STATE, CHUNKS, CH), pl.BlockSpec((STATE, CHUNKS, 128), lambda i: (0, 0, i))),
        "chunk": ((CHUNKS, CH), pl.BlockSpec((CHUNKS, 128), lambda i: (0, i))),
        "wide": (wide, once),
    }
    return pl.pallas_call(
        kernel,
        grid=(CH // 128,),
        in_specs=[kinds[kind][1] for kind in ins],
        out_specs=[kinds[kind][1] for kind in outs],
        out_shape=[jax.ShapeDtypeStruct(kinds[kind][0], F32) for kind in outs],
        scratch_shapes=[pltpu.VMEM((SPAN + extra, STATE, CHUNKS, 128), F32) for extra in scratch],
        compiler_params=pltpu.CompilerParams(
            dimension_semantics=("arbitrary",), vmem_limit_bytes=36 * 1024 * 1024
        ),
        cost_estimate=cost(micros),
    )


def scan_ends(*args):
    return scan_call(ends_kernel, ("tok", "tok", "wide", "rate"), ("state", "chunk"), (), 5)(*args)


def scan_outputs(*args):
    ins = ("tok", "tok", "wide", "wide", "rate", "state")
    return scan_call(outputs_kernel, ins, ("tok",), (), 7)(*args)[0]


def scan_heads(*args):
    return scan_call(heads_kernel, ("tok", "tok", "wide", "rate"), ("state",), (), 5)(*args)[0]


def scan_backward(*args):
    ins = ("tok", "tok", "tok", "wide", "wide", "rate", "state", "state")
    outs = ("tok", "tok", "state", "mix")
    return scan_call(backward_kernel, ins, outs, (0, 1, 0, 0), 24)(*args)


def chunk_starts(start, ends, decays, backward):
    order = range(CHUNKS)
    state, starts = start, [None] * CHUNKS
    for chunk in reversed(order) if backward else order:
        starts[chunk] = state
        state = decays[:, chunk] * state + ends[:, chunk]
    return jnp.stack(starts, 1), state


def entering_state(rate2, span, end, backward):
    sign = -1 if backward else 1

    def fold(items, here, ordered):
        state, total = jnp.zeros_like(end), jnp.zeros_like(span)
        for keep, (item_span, item_end) in items:
            state = jnp.where(keep, jnp.exp2(rate2 * item_span) * state + item_end, state)
            total = jnp.where(keep, total + item_span, total)
        return state, total

    def apart(block):
        return block[STATE : STATE + 1], block[:STATE]

    x, y = lax.axis_index("x"), lax.axis_index("y")
    row = in_order(around(jnp.concatenate([end, span], 0), "x"), "x")
    order = range(RING)[::sign]
    before, before_span = fold([((x - k) * sign > 0, apart(row[k])) for k in order], x, True)
    whole, whole_span = fold([(True, apart(row[k])) for k in order], x, True)
    rows = in_order(around(jnp.concatenate([whole, whole_span], 0), "y"), "y")
    above, _ = fold([((y - k) * sign > 0, apart(rows[k])) for k in order], y, True)
    return jnp.exp2(rate2 * before_span) * above + before


QBLOCK = 128
SEEN = WINDOW + QBLOCK
HEAD_COLS = GROUP * 128


def head_cols(g):
    return slice(128 * g, 128 * g + 128)


def fill_bias(first_ref, bias_ref):
    row = lax.broadcasted_iota(jnp.int32, (QBLOCK, SEEN), 0)
    col = lax.broadcasted_iota(jnp.int32, (QBLOCK, SEEN), 1)
    first = first_ref[0] - pl.program_id(0) * QBLOCK
    bias_ref[...] = jnp.where((col > row) & (col <= row + WINDOW) & (col >= first), 0.0, -1e30)


def attend_kernel(first_ref, q_ref, kv_ref, out_ref, lse_ref, bias_ref):
    fill_bias(first_ref, bias_ref)
    keyval = kv_ref[pl.ds(pl.program_id(0) * QBLOCK, SEEN), :]
    lane = lax.broadcasted_iota(jnp.int32, (QBLOCK, 128), 1)
    lses = jnp.zeros((QBLOCK, 128), F32)
    for g in range(GROUP):
        scores = nt(q_ref[:, head_cols(g)], keyval) + bias_ref[...]
        peak = jnp.max(scores, axis=1, keepdims=True)
        probs = jnp.exp(scores - peak)
        total = jnp.sum(probs, axis=1, keepdims=True)
        out_ref[:, head_cols(g)] = low(nn(low(probs), keyval) / total)
        lses = jnp.where(lane == g, peak + jnp.log(total), lses)
    lse_ref[...] = lses


def attend_back_kernel(
    first_ref, q_ref, kv_ref, dout_ref, lse_ref, dq_ref, dkv_ref, bias_ref, probs_ref, dscores_ref
):
    block = pl.program_id(0)
    fill_bias(first_ref, bias_ref)

    @pl.when(block == 0)
    def _():
        dkv_ref[...] = jnp.zeros(dkv_ref.shape, F32)

    here = pl.ds(block * QBLOCK, SEEN)
    keyval = kv_ref[here, :]
    lses = lse_ref[...]
    for g in range(GROUP):
        rows = slice(g * QBLOCK, (g + 1) * QBLOCK)
        probs = jnp.exp(nt(q_ref[:, head_cols(g)], keyval) + bias_ref[...] - lses[:, g : g + 1])
        weighted = probs * nt(dout_ref[:, head_cols(g)], keyval)
        d_scores = low(weighted - probs * jnp.sum(weighted, axis=1, keepdims=True))
        probs_ref[rows, :] = low(probs)
        dscores_ref[rows, :] = d_scores
        dq_ref[:, head_cols(g)] = low(nn(d_scores, keyval) * HEAD ** (-0.5))
    queries = jnp.concatenate([q_ref[:, head_cols(g)] for g in range(GROUP)], 0)
    d_outs = jnp.concatenate([dout_ref[:, head_cols(g)] for g in range(GROUP)], 0)
    dkv_ref[here, :] += tn(dscores_ref[...], queries) + tn(probs_ref[...], d_outs)


def attention_call(kernel, ins, outs, scratch, micros):
    kinds = {
        "first": pl.BlockSpec(memory_space=pltpu.SMEM),
        "heads": pl.BlockSpec((QBLOCK, HEAD_COLS), lambda i: (i, 0)),
        "keys": pl.BlockSpec((WINDOW + TOK, 128), lambda i: (0, 0)),
        "lse": pl.BlockSpec((QBLOCK, 128), lambda i: (i, 0)),
    }
    shapes = {"heads": ((TOK, HEAD_COLS), BF16), "keys": ((WINDOW + TOK, 128), F32), "lse": ((TOK, 128), F32)}
    return pl.pallas_call(
        kernel,
        grid=(TOK // QBLOCK,),
        in_specs=[kinds[kind] for kind in ins],
        out_specs=[kinds[kind] for kind in outs],
        out_shape=[jax.ShapeDtypeStruct(*shapes[kind]) for kind in outs],
        scratch_shapes=[pltpu.VMEM((QBLOCK, SEEN), F32)] + [pltpu.VMEM((GROUP * QBLOCK, SEEN), BF16)] * scratch,
        compiler_params=pltpu.CompilerParams(
            dimension_semantics=("arbitrary",), vmem_limit_bytes=28 * 1024 * 1024
        ),
        cost_estimate=cost(micros),
    )


def widen(heads, front):
    heads = heads.reshape(TOK, GROUP, HEAD)
    heads = jnp.pad(heads, ((0, 0), (0, 0), (front, 128 - HEAD - front)))
    return heads.reshape(TOK, HEAD_COLS)


def narrow(wide, first):
    return wide.reshape(TOK, GROUP, 128)[:, :, first : first + HEAD].reshape(TOK, QW)


def first_key(line):
    return (WINDOW - line * TOK).reshape(1).astype(jnp.int32)


def attention_forward(query_wide, keyval, line):
    call = attention_call(attend_kernel, ("first", "heads", "keys"), ("heads", "lse"), 0, 9)
    out, lse = call(first_key(line), query_wide, keyval)
    return narrow(out, HEAD), lse


def attention_backward(query_wide, keyval, lse, d_out, line):
    ins = ("first", "heads", "keys", "heads", "lse")
    call = attention_call(attend_back_kernel, ins, ("heads", "keys"), 2, 14)
    d_query, d_keyval = call(first_key(line), query_wide, keyval, widen(d_out, HEAD), lse)
    return narrow(d_query, 0), d_keyval


def by_group(pieces):
    rows, _, cols = pieces.shape
    pieces = jnp.pad(pieces, ((0, 0), (0, 2 * RING - KV_HEADS), (0, 0)))
    pieces = pieces.reshape(rows, RING, 2, cols)
    mine = lax.dynamic_index_in_dim(pieces, lax.axis_index("wt"), 2, False)
    return jnp.swapaxes(mine, 0, 1)


def gather_lines(block):
    return lax.all_gather(block, YX, axis=0, tiled=True)


def gather_by_steps(block):
    half = block.shape[1] // 2
    first, second = block[:, :half], block[:, half:]
    first = in_order(around(in_order(around(first, "x"), "x"), "y"), "y")
    second = jnp.swapaxes(in_order(around(in_order(around(second, "y"), "y"), "x"), "x"), 0, 1)
    return jnp.concatenate([first, second], 3).reshape(-1, 2 * half)


def reduce_lines(grads):
    rows = grads.shape[0] // LINES
    blocks = jnp.pad(low(grads).reshape(LINES, rows, -1), ((0, 0), (0, -rows % 32), (0, 0)))
    return lax.psum_scatter(blocks.reshape(-1, grads.shape[1]), YX, scatter_dimension=0, tiled=True)


def reduce_by_steps(grads):
    half = grads.shape[1] // 2
    blocks = grads.reshape(RING, RING, -1, 2 * half)

    def one_axis(parts, axis, dim):
        here, total = lax.axis_index(axis), None
        for d in range(RING):
            part = lax.dynamic_index_in_dim(parts, (here + d) % RING, dim, False)
            if d:
                part = lax.ppermute(low(part), axis, step_to(axis, d))
            part = part.astype(F32)
            total = part if total is None else total + part
        return total

    first = one_axis(one_axis(blocks[..., :half], "y", 0), "x", 0)
    second = one_axis(one_axis(blocks[..., half:], "x", 1), "y", 0)
    return jnp.concatenate([first, second], 1)


def per_device(
    block_in, in_gain, w_query, w_keyval, w_out, attn_gain, ssm_gain, inner_weight, conv_weight, conv_bias,
    w_xproj, w_delta, delta_bias, log_decay, skip_gain, w_ssmout, mlp_gain, w_gateup, w_down, cotangent,
):
    core = lax.axis_index("wt")
    depth = lax.axis_index("z")
    line = lax.axis_index("y") * RING + lax.axis_index("x")

    attn_piece = jnp.concatenate(
        [
            by_group(w_query.reshape(PIECE, KV_HEADS, QW)),
            by_group(w_keyval[:, 0].reshape(PIECE, KV_HEADS, HEAD)),
            by_group(w_keyval[:, 1].reshape(PIECE, KV_HEADS, HEAD)),
            by_group(w_out.T.reshape(PIECE, KV_HEADS, QW)),
        ],
        2,
    )
    gains = jnp.concatenate([in_gain, attn_gain, ssm_gain, mlp_gain])
    gains = jnp.broadcast_to(jnp.pad(gains, (0, ATT_COLS - 4 * PIECE)), (RING, 1, ATT_COLS))
    attn_piece = exchange(jnp.concatenate([attn_piece, gains], 1), "z")
    gains = attn_piece[:, PIECE, : 4 * PIECE].reshape(RING, 4, PIECE)
    gains = jnp.swapaxes(gains, 0, 1).reshape(4, ROWS)
    gains = jnp.pad(gains, ((0, 0), (0, ATT_COLS - ROWS)))
    attn_piece = jnp.concatenate([attn_piece[:, :PIECE].reshape(ROWS, ATT_COLS), gains], 0)

    ff_piece = jnp.concatenate([w_gateup, w_down.T[:, None]], 1).reshape(PIECE, 3, RING, FF_PIECE)
    ff_piece = jnp.pad(ff_piece, ((0, 0), (0, 0), (0, 0), (0, FF_PAD - FF_PIECE)))
    ff_piece = jnp.transpose(ff_piece, (2, 0, 1, 3)).reshape(RING, PIECE, 3 * FF_PAD)
    ff_piece = exchange(ff_piece, "z").reshape(ROWS, 3 * FF_PAD)
    ff_piece = jnp.pad(ff_piece, ((0, ROWS_PAD - ROWS), (0, 0)))

    inner_rows = jnp.transpose(inner_weight, (2, 1, 0))
    small = jnp.concatenate(
        [conv_weight.T, conv_bias[:, None], delta_bias[:, None], skip_gain[:, None], log_decay.T], 1
    )
    channel = jnp.concatenate(
        [
            pad_features(inner_rows).reshape(PIECE, 2 * DP),
            pad_features(w_ssmout),
            jnp.pad(w_xproj[:, :DTR], ((0, 0), (0, RANK_PAD - DTR))),
            jnp.pad(w_xproj[:, DTR:], ((0, 0), (0, 256 - XROWS))),
            jnp.pad(w_delta.T, ((0, 0), (0, 128 - DTR))),
            jnp.pad(small, ((0, 0), (0, SMALL - SMALL_USED))),
        ],
        1,
    )
    channel = jnp.pad(channel, ((0, CH_PAD - PIECE), (0, 0)))

    with jax.named_scope("gather_attention"):
        w_attn = gather_by_steps(attn_piece)
    with jax.named_scope("gather_channels"):
        channel = gather_lines(channel)
    with jax.named_scope("gather_ff"):
        w_ff = gather_lines(ff_piece)

    w_conv, w_gate, w_so = channel[:, :DP], channel[:, COLS[1] : COLS[2]], channel[:, COLS[2] : COLS[3]]
    w_x = channel[:, COLS[3] : COLS[3] + XROWS]
    w_d = channel[:, COLS[4] : COLS[4] + DTR]
    small = channel[:, COLS[5] : COLS[6]].astype(F32)
    small_rows = small[:, :32].T
    taps, c_bias, d_bias, skip = small_rows[:CONV], small_rows[4:5], small_rows[5:6], small_rows[6:7]
    rate2 = -jnp.exp(small_rows[7 : 7 + STATE]) * LOG2E
    gains = w_attn.reshape(LINES, ROWS_PAD, ATT_COLS)[:, ROWS:, :ROWS].astype(F32)
    gains = jnp.pad(jnp.swapaxes(gains, 0, 1), ((0, 0), (0, 0), (0, ROWS_PAD - ROWS))).reshape(4, DP)
    in_g, attn_g, ssm_g, mlp_g = (gains[k : k + 1] for k in range(4))

    own_in = lax.dynamic_slice_in_dim(pad_features(block_in), core * SPAN, SPAN, 0)
    own_cot = lax.dynamic_slice_in_dim(pad_features(cotangent), core * SPAN, SPAN, 0)
    line_in = gather_tokens(own_in, True)
    line_cot = gather_tokens(own_cot, False)
    own_in = own_in.astype(F32)
    x1 = low(rms(line_in.astype(F32), in_g))

    qkv = low(nn(x1, w_attn[:, : QW + 2 * HEAD]))
    query, keyval = qkv[:, :QW], qkv[:, QW:]
    keyval = jnp.concatenate([line_shift(keyval, 2), line_shift(keyval, 1), keyval], 0)
    query_wide = widen(query * BF16(HEAD ** (-0.5)), 0)
    attended, lse = attention_forward(query_wide, keyval, line)
    w_o = w_attn[:, QW + 2 * HEAD :]
    attn_out = scatter_tokens(nt(attended, w_o), True)

    conv_in = low(nt(x1, w_conv))
    gate_z = low(nt(x1, w_gate)).astype(F32)
    edge = line_shift(conv_in[TOK - (CONV - 1) :], 1)
    padded_in = jnp.concatenate([edge, conv_in], 0).astype(F32)
    conv_out = c_bias
    for tap in range(CONV):
        conv_out = conv_out + taps[tap : tap + 1] * padded_in[tap : tap + TOK]
    mixer_low = low(jax.nn.silu(conv_out))
    mixer_in = mixer_low.astype(F32)
    xproj = sum_line(dot(w_x, mixer_low, ((0,), (1,))))
    step_low = low(xproj[:DTR])
    in_mix, out_mix = spread(xproj[RANK_PAD : RANK_PAD + STATE]), spread(xproj[RANK_PAD + STATE :])
    step_pre = dot(step_low, w_d, ((0,), (1,))) + d_bias
    step = jax.nn.softplus(step_pre)
    ends, spans = scan_ends(step, mixer_in, in_mix, rate2)
    span = jnp.sum(spans, axis=0, keepdims=True)
    decays = jnp.exp2(rate2[:, None] * spans[None])
    _, end = chunk_starts(jnp.zeros_like(rate2), ends, decays, False)
    starts, _ = chunk_starts(entering_state(rate2, span, end, False), ends, decays, False)
    ssm_y = scan_outputs(step, mixer_in, in_mix, out_mix, rate2, starts) + skip * mixer_in
    silu_z = jax.nn.silu(gate_z)
    mixer_act = low(ssm_y * silu_z)
    mixer_out = scatter_tokens(nn(mixer_act, w_so), True)

    hidden = own_in + 0.5 * (rms(attn_out, attn_g) + rms(mixer_out, ssm_g))
    x2 = gather_tokens(low(rms(hidden, mlp_g)), False)
    w_gu, w_dn = w_ff[:, : 2 * FF_PAD], w_ff[:, 2 * FF_PAD :]
    gate_up = low(nn(x2, w_gu)).astype(F32)
    gate, upper = gate_up[:, :FF_PAD], gate_up[:, FF_PAD:]
    silu_gate = jax.nn.silu(gate)
    mlp_act = low(silu_gate * upper)
    d_act = nn(line_cot, w_dn)
    d_gate_up = low(jnp.concatenate([d_act * upper * silu_grad(gate), d_act * silu_gate], 1))
    d_x2 = scatter_tokens(nt(d_gate_up, w_gu), False)
    mlp_out = scatter_tokens(nt(mlp_act, w_dn), False)
    grad_ff = low(jnp.concatenate([tn(x2, d_gate_up), tn(line_cot, mlp_act)], 1))
    block_out = low(hidden + mlp_out)

    d_norm, d_mlp_g = rms_back(hidden, mlp_g, d_x2)
    d_hidden = own_cot.astype(F32) + d_norm
    d_attn, d_attn_g = rms_back(attn_out, attn_g, 0.5 * d_hidden)
    d_mixer, d_ssm_g = rms_back(mixer_out, ssm_g, 0.5 * d_hidden)
    d_mixer = gather_tokens(low(d_mixer), True)
    d_attn = gather_tokens(low(d_attn), True)

    d_mact = nt(d_mixer, w_so)
    grad_so = tn(mixer_act, d_mixer)
    dy = d_mact * silu_z
    d_gate_low = low(d_mact * ssm_y * silu_grad(gate_z))
    grad_early = jnp.concatenate([low(tn(d_gate_low, x1)), low(grad_so)], 1)
    heads = scan_heads(step, dy, out_mix, rate2)
    _, head = chunk_starts(jnp.zeros_like(rate2), heads, decays, True)
    lams, _ = chunk_starts(entering_state(rate2, span, head, True), heads, decays, True)
    d_step, lam_b, d_decay, d_mixes = scan_backward(step, mixer_in, dy, in_mix, out_mix, rate2, starts, lams)
    grad_decay = rate2 * (1.0 / LOG2E) * jnp.sum(d_decay, axis=1)
    d_step_pre = (d_step + lam_b * mixer_in) * jax.nn.sigmoid(step_pre)
    d_step_low = low(d_step_pre)
    grad_d = tn(d_step_low, step_low.T)
    d_rank = dot(w_d, d_step_low, ((0,), (1,)))
    d_xproj = jnp.concatenate([jnp.pad(d_rank, ((0, RANK_PAD - DTR), (0, 0))), d_mixes[:, : 2 * STATE].T], 0)
    d_xproj = low(sum_line(d_xproj))
    grad_x = dot(mixer_low, d_xproj, ((0,), (1,)))
    d_mixer_in = dy * skip + step * lam_b + dot(d_xproj, w_x, ((0,), (1,)))
    d_conv_out = d_mixer_in * silu_grad(conv_out)
    d_after = jnp.concatenate([d_conv_out, line_shift(d_conv_out[: CONV - 1], -1)], 0)
    d_conv_in = sum(taps[k : k + 1] * d_after[CONV - 1 - k : CONV - 1 - k + TOK] for k in range(CONV))
    small_grads = jnp.stack(
        [jnp.sum(d_conv_out * padded_in[tap : tap + TOK], axis=0) for tap in range(CONV)]
        + [jnp.sum(d_conv_out, axis=0), jnp.sum(d_step_pre, axis=0), jnp.sum(dy * mixer_in, axis=0)],
        0,
    )
    small_grads = jnp.concatenate([small_grads, grad_decay], 0).T
    d_conv_low = low(d_conv_in)
    grad_late = jnp.concatenate(
        [
            tn(d_conv_low, x1),
            jnp.pad(grad_x, ((0, 0), (0, 256 - XROWS))),
            jnp.pad(grad_d, ((0, 0), (0, 128 - DTR))),
            jnp.pad(small_grads, ((0, 0), (0, SMALL - SMALL_USED))),
        ],
        1,
    )

    d_attended = low(nn(d_attn, w_o))
    d_query, d_keyval = attention_backward(query_wide, keyval, lse, d_attended, line)
    d_keyval = (
        d_keyval[2 * TOK :]
        + line_shift(low(d_keyval[TOK : 2 * TOK]), -1).astype(F32)
        + line_shift(low(d_keyval[:TOK]), -2).astype(F32)
    )
    d_qkv = jnp.concatenate([d_query, low(d_keyval)], 1)
    grad_attn = low(jnp.concatenate([tn(x1, d_qkv), tn(d_attn, attended)], 1))
    d_x1 = nt(d_qkv, w_attn[:, : QW + 2 * HEAD]) + nn(d_conv_low, w_conv) + nn(d_gate_low, w_gate)
    d_x1 = scatter_tokens(d_x1, True)
    d_norm, d_in_g = rms_back(own_in, in_g, d_x1)
    grad_in = d_hidden + d_norm

    first = core == 0

    def both_cores(own):
        other = swap_core(own)
        return jnp.concatenate([jnp.where(first, own, other), jnp.where(first, other, own)], 0)

    block_out = drop_features(both_cores(block_out))
    grad_in = drop_features(both_cores(grad_in))

    with jax.named_scope("reduce_ff"):
        grad_ff = reduce_lines(grad_ff)
    with jax.named_scope("reduce_channels"):
        grad_early, _ = lax.optimization_barrier((grad_early, grad_ff[:8, :128]))
        grad_early = reduce_lines(grad_early).astype(F32)
    with jax.named_scope("reduce_attention"):
        grad_attn = reduce_by_steps(grad_attn)
    with jax.named_scope("reduce_late"):
        grad_late = reduce_by_steps(grad_late)

    def to_owner(grads):
        return exchange(low(grads[:ROWS]).reshape(RING, PIECE, grads.shape[1]), "z").astype(F32)

    grad_ff = to_owner(grad_ff).reshape(RING, PIECE, 3, FF_PAD)[..., :FF_PIECE]
    grad_ff = jnp.transpose(grad_ff, (1, 2, 0, 3)).reshape(PIECE, 3, RING * FF_PIECE)
    grad_gateup, grad_down = grad_ff[:, :2], grad_ff[:, 2].T

    grad_attn = to_owner(grad_attn)
    other = swap_core(grad_attn)
    grad_attn = jnp.stack([jnp.where(first, grad_attn, other), jnp.where(first, other, grad_attn)], 1)
    grad_attn = jnp.transpose(grad_attn, (2, 0, 1, 3)).reshape(PIECE, 2 * RING, ATT_COLS)[:, :KV_HEADS]
    grad_query = grad_attn[..., :QW].reshape(PIECE, HEADS * HEAD)
    grad_keyval = grad_attn[..., QW : QW + 2 * HEAD].reshape(PIECE, KV_HEADS, 2, HEAD)
    grad_keyval = jnp.swapaxes(grad_keyval, 1, 2).reshape(PIECE, 2, KV_HEADS * HEAD)
    grad_out = grad_attn[..., QW + 2 * HEAD :].reshape(PIECE, HEADS * HEAD).T

    grad_early, grad_late = grad_early[:PIECE], grad_late[:PIECE]
    grad_inner = jnp.stack([grad_late[:, :DP], grad_early[:, :DP]], 1)
    grad_inner = jnp.transpose(drop_features(grad_inner), (2, 1, 0))
    grad_ssmout = drop_features(grad_early[:, DP:])
    grad_xproj = grad_late[:, DP : DP + XROWS]
    grad_xproj = jnp.concatenate([grad_xproj[:, :DTR], grad_xproj[:, RANK_PAD:]], 1)
    grad_delta = grad_late[:, DP + 256 : DP + 256 + DTR].T
    small_grads = grad_late[:, DP + 384 : DP + 384 + SMALL_USED].T

    gain_grads = sum_all(jnp.stack([d_in_g, d_attn_g, d_ssm_g, d_mlp_g]))
    gain_grads = lax.dynamic_slice_in_dim(gain_grads, line * ROWS_PAD, ROWS_PAD, 1)
    gain_grads = lax.dynamic_slice_in_dim(gain_grads, depth * PIECE, PIECE, 1)

    return (
        block_out, grad_in, gain_grads[0], grad_query, grad_keyval, grad_out, gain_grads[1], gain_grads[2],
        grad_inner, small_grads[:CONV], small_grads[4], grad_xproj, grad_delta, small_grads[5],
        small_grads[7 : 7 + STATE], small_grads[6], grad_ssmout, gain_grads[3], grad_gateup, grad_down,
    )


def solution(mesh):
    fine = Mesh(mesh.devices.reshape(RING, RING, RING, 2), ("y", "x", "z", "wt"))
    both = SEQ + ("wt",)
    weights = (
        P(SEQ),
        P(SEQ, None),
        P(SEQ, None, None),
        P(None, SEQ),
        P(SEQ),
        P(SEQ),
        P(None, None, both),
        P(None, both),
        P(both),
        P(both, None),
        P(None, both),
        P(both),
        P(None, both),
        P(both),
        P(both, None),
        P(SEQ),
        P(SEQ, None, "wt"),
        P("wt", SEQ),
    )
    rows = P(SEQ, None)
    return jax.shard_map(
        per_device, mesh=fine, in_specs=(rows,) + weights + (rows,), out_specs=(rows, rows) + weights, check_vma=False
    )
```

```python
import functools
import math

import jax
import jax.numpy as jnp
from jax import lax
from jax.experimental import pallas as pl
from jax.experimental.pallas import tpu as pltpu
from jax.sharding import Mesh
from jax.sharding import PartitionSpec as P

F32 = jnp.float32
BF16 = jnp.bfloat16

HEADS = 25
KV_HEADS = 5
GROUP = HEADS // KV_HEADS
HEAD = 64
STATE = 16
DTR = 100
CONV = 4
WINDOW = 1024
D = 1600
QW = GROUP * HEAD
EPS = 1e-06
LOG2E = math.log2(math.e)

YX = ("y", "x")
SEQ = ("y", "x", "z")
RING = 4
LINES = 16
PIECE = 25
ROWS = RING * PIECE
ROWS_PAD = 104
DP = LINES * ROWS_PAD
CH_PAD = 32
CH = LINES * CH_PAD
SPAN = 64
CHUNKS = 8
TOK = SPAN * CHUNKS
FF_PIECE = 688
FF_PAD = 768
ATT_COLS = 768
RANK_PAD = 104
XROWS = RANK_PAD + 2 * STATE
PAY = STATE + 8
SMALL = 128
SMALL_USED = CONV + 3 + STATE
GAIN_AT = SMALL - ROWS
COLS = (0, DP, 2 * DP, 2 * DP + 256, 2 * DP + 384, 2 * DP + 512)


def dot(left, right, dims):
    return lax.dot_general(left, right, (dims, ((), ())), preferred_element_type=F32)


def nn(left, right):
    return dot(left, right, ((1,), (0,)))


def nt(left, right):
    return dot(left, right, ((1,), (1,)))


def tn(left, right):
    return dot(left, right, ((0,), (0,)))


def low(value):
    return value.astype(BF16)


def pad_features(value):
    lead = value.shape[:-1]
    value = value.reshape(lead + (LINES, ROWS))
    value = jnp.pad(value, [(0, 0)] * (len(lead) + 1) + [(0, ROWS_PAD - ROWS)])
    return value.reshape(lead + (DP,))


def drop_features(value):
    lead = value.shape[:-1]
    return value.reshape(lead + (LINES, ROWS_PAD))[..., :ROWS].reshape(lead + (D,))


def step_to(axis, distance):
    return [(i, (i + distance) % RING) for i in range(RING)]


def around(value, axis):
    return [value] + [lax.ppermute(value, axis, step_to(axis, RING - d)) for d in range(1, RING)]


def copy_kernel(plan, count, *refs):
    ins, outs, sems = refs[:count], refs[count:-1], refs[-1]
    copies = [pltpu.make_async_copy(src, dst, sems.at[k]) for k, (src, dst) in enumerate(plan(ins, outs))]
    for copy in copies:
        copy.start()
    for copy in copies:
        copy.wait()


def copy_call(plan, number, arrays, shapes):
    anywhere = pl.BlockSpec(memory_space=pl.ANY)
    return pl.pallas_call(
        functools.partial(copy_kernel, plan, len(arrays)),
        in_specs=[anywhere] * len(arrays),
        out_specs=[anywhere] * len(shapes),
        out_shape=[jax.ShapeDtypeStruct(shape, arrays[0].dtype) for shape in shapes],
        scratch_shapes=[pltpu.SemaphoreType.DMA((number,))],
        compiler_params=pltpu.CompilerParams(vmem_limit_bytes=8 * 1024 * 1024),
        cost_estimate=cost(1),
    )(*arrays)


def spot(axis, k):
    return lax.rem(lax.axis_index(axis) + k, RING)


def in_order(blocks, axis):
    def plan(ins, outs):
        return [(block, outs[0].at[spot(axis, k)]) for k, block in enumerate(ins)]

    return copy_call(plan, RING, blocks, [(RING,) + blocks[0].shape])[0]


def swap_core(value):
    return lax.ppermute(value, "wt", [(0, 1), (1, 0)])


def sent_along(pieces, axis):
    here = lax.axis_index(axis)
    got = [lax.dynamic_index_in_dim(pieces, here, 0, False)]
    for d in range(1, RING):
        piece = lax.dynamic_index_in_dim(pieces, (here + RING - d) % RING, 0, False)
        got.append(lax.ppermute(piece, axis, step_to(axis, RING - d)))
    return got


def exchange(pieces, axis):
    return in_order(sent_along(pieces, axis), axis)


def gather_tokens(own):
    return merge_cores(in_order(around(own, "z"), "z"))


def merge_cores(mine):
    wide, rows = mine.shape[2], pl.ds(0, SPAN)

    def plan(ins, outs):
        core = lax.axis_index("wt")
        return [(part.at[:, rows], outs[0].at[:, place]) for place, part in ((core, ins[0]), (1 - core, ins[1]))]

    return copy_call(plan, 2, [mine, swap_core(mine)], [(RING, 2, SPAN, wide)])[0].reshape(TOK, wide)


def add_cores(partial):
    core = lax.axis_index("wt")
    parts = partial.reshape(RING, 2, SPAN, partial.shape[1])
    mine = lax.dynamic_index_in_dim(parts, core, 1, False)
    theirs = lax.dynamic_index_in_dim(parts, 1 - core, 1, False)
    return mine.astype(F32) + swap_core(theirs).astype(F32)


def add_ring(mine):
    here = lax.axis_index("z")
    total, parts = lax.dynamic_index_in_dim(mine, here, 0, False), []
    for d in range(1, RING):
        piece = lax.dynamic_index_in_dim(mine, (here + d) % RING, 0, False)
        parts.append(lax.ppermute(low(piece), "z", step_to("z", d)))
        total = total + parts[-1].astype(F32)
    return total, parts[0]


def scatter_tokens(partial):
    return add_ring(add_cores(partial))


def sum_line(value):
    value = value + swap_core(value)
    parts = around(low(value), "z")
    return value + (parts[1].astype(F32) + parts[2].astype(F32) + parts[3].astype(F32))


def line_shift(value, distance):
    route = [(i, i + distance) for i in range(LINES) if 0 <= i + distance < LINES]
    return lax.ppermute(value, YX, route)


def rms(value, gain):
    scale = lax.rsqrt(jnp.sum(value * value, axis=-1, keepdims=True) / D + EPS)
    return value * scale * gain


def rms_back(value, gain, dy):
    r = lax.rsqrt(jnp.sum(value * value, axis=-1, keepdims=True) / D + EPS)
    inner = jnp.sum(value * gain * dy, axis=-1, keepdims=True) / D
    return r * gain * dy - value * (r * r * r) * inner, jnp.sum(value * r * dy, axis=0)


def silu_grad(value):
    sig = jax.nn.sigmoid(value)
    return sig * (1.0 + value * (1.0 - sig))


def rows_at(ref, tau):
    return ref[pl.ds(tau, CHUNKS, stride=SPAN), :]


def spread(rows):
    rows = jnp.transpose(rows.reshape(STATE, CHUNKS, SPAN), (2, 0, 1))
    return jnp.broadcast_to(rows[..., None], (SPAN, STATE, CHUNKS, 128))


def rate_rows(rate_ref):
    return [jnp.broadcast_to(rate_ref[n : n + 1, :], (CHUNKS, 128)) for n in range(STATE)]


def zeros():
    return jnp.zeros((CHUNKS, 128), F32)


def walk(start, ends_ref, spans_ref, rate_ref, starts_ref=None, backward=False):
    state, order = start, range(CHUNKS)
    for chunk in reversed(order) if backward else order:
        rows = pl.ds(chunk, STATE, stride=CHUNKS)
        if starts_ref is not None:
            starts_ref[rows, :] = state
        state = jnp.exp2(rate_ref[...] * spans_ref[chunk : chunk + 1, :]) * state + ends_ref[rows, :]
    return state


def chunk_rows(n):
    return slice(CHUNKS * n, CHUNKS * n + CHUNKS)


def report(pay_ref, state, spans_ref):
    pay_ref[:STATE, :] = state
    total = jnp.sum(spans_ref[...], axis=0, keepdims=True)
    pay_ref[STATE:, :] = jnp.broadcast_to(total, (PAY - STATE, 128))


def ends_kernel(step_ref, in_ref, b_ref, rate_ref, end_ref, span_ref, pay_ref):
    rates = rate_rows(rate_ref)

    def token(tau, carry):
        states, total = carry
        step = rows_at(step_ref, tau)
        push = step * rows_at(in_ref, tau)
        states = [jnp.exp2(step * rates[n]) * states[n] + push * b_ref[tau, n] for n in range(STATE)]
        return states, total + step

    states, total = lax.fori_loop(0, SPAN, token, ([zeros()] * STATE, zeros()), unroll=8)
    for n in range(STATE):
        end_ref[chunk_rows(n), :] = states[n]
    span_ref[...] = total
    report(pay_ref, walk(jnp.zeros((STATE, 128), F32), end_ref, span_ref, rate_ref), span_ref)


def outputs_kernel(step_ref, in_ref, b_ref, c_ref, rate_ref, end_ref, span_ref, enter_ref, y_ref, init_ref):
    rates = rate_rows(rate_ref)
    walk(enter_ref[...], end_ref, span_ref, rate_ref, init_ref)

    def token(tau, states):
        step = rows_at(step_ref, tau)
        push = step * rows_at(in_ref, tau)
        states = [jnp.exp2(step * rates[n]) * states[n] + push * b_ref[tau, n] for n in range(STATE)]
        y_ref[pl.ds(tau, CHUNKS, stride=SPAN), :] = sum(c_ref[tau, n] * states[n] for n in range(STATE))
        return states

    lax.fori_loop(0, SPAN, token, [init_ref[chunk_rows(n), :] for n in range(STATE)], unroll=8)


def heads_kernel(step_ref, dy_ref, c_ref, rate_ref, span_ref, head_ref, pay_ref):
    rates = rate_rows(rate_ref)

    def token(back, carry):
        tau = SPAN - 1 - back
        step = rows_at(step_ref, tau)
        dy = rows_at(dy_ref, tau)
        return [jnp.exp2(step * rates[n]) * (c_ref[tau, n] * dy + carry[n]) for n in range(STATE)]

    carry = lax.fori_loop(0, SPAN, token, [zeros()] * STATE, unroll=8)
    for n in range(STATE):
        head_ref[chunk_rows(n), :] = carry[n]
    state = walk(jnp.zeros((STATE, 128), F32), head_ref, span_ref, rate_ref, backward=True)
    report(pay_ref, state, span_ref)


def backward_kernel(
    step_ref, in_ref, dy_ref, b_ref, c_ref, rate_ref, end_ref, span_ref, enter_ref, head_ref, enter_back_ref,
    dstep_ref, lamb_ref, ddecay_ref, dmix_ref,
    a_ref, h_ref, din_ref, dout_ref, init_ref, lam_ref,
):
    rates = rate_rows(rate_ref)

    @pl.when(pl.program_id(0) == 0)
    def _():
        @pl.loop(0, SPAN)
        def _(tau):
            din_ref[tau] = jnp.zeros((STATE, CHUNKS, 128), F32)
            dout_ref[tau] = jnp.zeros((STATE, CHUNKS, 128), F32)

    walk(enter_ref[...], end_ref, span_ref, rate_ref, init_ref)
    walk(enter_back_ref[...], head_ref, span_ref, rate_ref, lam_ref, backward=True)
    for n in range(STATE):
        h_ref[0, n] = init_ref[chunk_rows(n), :]

    def forth(tau, states):
        step = rows_at(step_ref, tau)
        push = step * rows_at(in_ref, tau)
        states = list(states)
        for n in range(STATE):
            decay = jnp.exp2(step * rates[n])
            a_ref[tau, n] = decay
            states[n] = decay * states[n] + push * b_ref[tau, n]
            h_ref[tau + 1, n] = states[n]
        return states

    lax.fori_loop(0, SPAN, forth, [init_ref[chunk_rows(n), :] for n in range(STATE)], unroll=4)

    def back(backwards, carry):
        tau = SPAN - 1 - backwards
        lams, decays = list(carry[0]), list(carry[1])
        step = rows_at(step_ref, tau)
        push = step * rows_at(in_ref, tau)
        dy = rows_at(dy_ref, tau)
        dstep, lamb = zeros(), zeros()
        for n in range(STATE):
            lam = c_ref[tau, n] * dy + lams[n]
            lams[n] = a_ref[tau, n] * lam
            along = lams[n] * h_ref[tau, n]
            dstep = dstep + along * rates[n]
            lamb = lamb + lam * b_ref[tau, n]
            decays[n] = decays[n] + along * step
            din_ref[tau, n] += lam * push
            dout_ref[tau, n] += dy * h_ref[tau + 1, n]
        dstep_ref[pl.ds(tau, CHUNKS, stride=SPAN), :] = dstep * (1.0 / LOG2E)
        lamb_ref[pl.ds(tau, CHUNKS, stride=SPAN), :] = lamb
        return lams, decays

    start = ([lam_ref[chunk_rows(n), :] for n in range(STATE)], [zeros()] * STATE)
    _, decays = lax.fori_loop(0, SPAN, back, start, unroll=4)
    total = jnp.concatenate([jnp.sum(decays[n], axis=0, keepdims=True) for n in range(STATE)], 0)
    ddecay_ref[...] = total * rate_ref[...] * (1.0 / LOG2E)

    @pl.when(pl.program_id(0) == pl.num_programs(0) - 1)
    def _():
        lane = lax.broadcasted_iota(jnp.int32, (CHUNKS, 128), 1)

        def fold(tau, carry):
            rows = zeros()
            for n in range(STATE):
                rows = jnp.where(lane == n, jnp.sum(din_ref[tau, n], axis=1, keepdims=True), rows)
                total = jnp.sum(dout_ref[tau, n], axis=1, keepdims=True)
                rows = jnp.where(lane == STATE + n, total, rows)
            dmix_ref[pl.ds(tau, CHUNKS, stride=SPAN), :] = rows
            return carry

        lax.fori_loop(0, SPAN, fold, 0, unroll=8)


def cost(micros):
    return pl.CostEstimate(flops=int(micros * 1e9), bytes_accessed=int(micros * 3e6), transcendentals=0)


def scan_call(kernel, ins, outs, scratch, micros):
    wide = (SPAN, STATE, CHUNKS, 128)
    once = pl.BlockSpec(wide, lambda i: (0, 0, 0, 0), pipeline_mode=pl.Buffered(1))

    def lanes(rows):
        return (rows, CH), pl.BlockSpec((rows, 128), lambda i: (0, i))

    kinds = {
        "tok": lanes(TOK),
        "mix": ((TOK, 128), pl.BlockSpec((TOK, 128), lambda i: (0, 0))),
        "state": lanes(STATE),
        "states": lanes(STATE * CHUNKS),
        "chunk": lanes(CHUNKS),
        "pay": lanes(PAY),
        "wide": (wide, once),
    }
    return pl.pallas_call(
        kernel,
        grid=(CH // 128,),
        in_specs=[kinds[kind][1] for kind in ins],
        out_specs=[kinds[kind][1] for kind in outs],
        out_shape=[jax.ShapeDtypeStruct(kinds[kind][0], F32) for kind in outs],
        scratch_shapes=[pltpu.VMEM(shape, F32) for shape in scratch],
        compiler_params=pltpu.CompilerParams(
            dimension_semantics=("arbitrary",), vmem_limit_bytes=36 * 1024 * 1024
        ),
        cost_estimate=cost(micros),
    )


WALK = (STATE * CHUNKS, 128)


def scan_ends(*args):
    ins = ("tok", "tok", "wide", "state")
    return scan_call(ends_kernel, ins, ("states", "chunk", "pay"), (), 5)(*args)


def scan_outputs(*args):
    ins = ("tok", "tok", "wide", "wide", "state", "states", "chunk", "state")
    return scan_call(outputs_kernel, ins, ("tok",), (WALK,), 7)(*args)[0]


def scan_heads(*args):
    ins = ("tok", "tok", "wide", "state", "chunk")
    return scan_call(heads_kernel, ins, ("states", "pay"), (), 5)(*args)


def scan_backward(*args):
    ins = ("tok", "tok", "tok", "wide", "wide", "state", "states", "chunk", "state", "states", "state")
    outs = ("tok", "tok", "state", "mix")
    wide = [(SPAN + extra, STATE, CHUNKS, 128) for extra in (0, 1, 0, 0)]
    return scan_call(backward_kernel, ins, outs, wide + [WALK, WALK], 20)(*args)


def nearer(value, axis, backward):
    here = lax.axis_index(axis)
    if backward:
        here = RING - 1 - here
    steps = ((d, lax.ppermute(value, axis, step_to(axis, -d if backward else d))) for d in (3, 2, 1))
    return here, list(steps)


def fold(rate2, blocks, keep):
    state, span = jnp.zeros_like(rate2), jnp.zeros_like(rate2[:1])
    for d, block in blocks:
        block_span = block[STATE : STATE + 1]
        longer = jnp.exp2(rate2 * block_span) * state + block[:STATE]
        state = jnp.where(keep(d), longer, state)
        span = jnp.where(keep(d), span + block_span, span)
    return state, span


def state_along_x(rate2, pay, backward):
    here, blocks = nearer(pay, "x", backward)
    before = fold(rate2, blocks, lambda d: d <= here)
    after, after_span = fold(rate2, blocks, lambda d: d > here)
    own_span = pay[STATE : STATE + 1]
    whole = jnp.exp2(rate2 * own_span) * before[0] + pay[:STATE]
    whole = jnp.exp2(rate2 * after_span) * whole + after
    rows = jnp.concatenate([whole, jnp.broadcast_to(before[1] + own_span + after_span, (PAY - STATE, CH))], 0)
    return before, rows


def state_along_y(rate2, before, rows, backward):
    here, blocks = nearer(rows, "y", backward)
    above, _ = fold(rate2, blocks, lambda d: d <= here)
    return jnp.exp2(rate2 * before[1]) * above + before[0], blocks[-1][1]


QBLOCK = 128
SCALE = HEAD ** (-0.5)
SEEN = WINDOW + QBLOCK


def head_cols(g):
    return slice(HEAD * g, HEAD * g + HEAD)


def fill_bias(first_ref, bias_ref):
    row = lax.broadcasted_iota(jnp.int32, (QBLOCK, SEEN), 0)
    col = lax.broadcasted_iota(jnp.int32, (QBLOCK, SEEN), 1)
    first = first_ref[0] - pl.program_id(0) * QBLOCK
    bias_ref[...] = jnp.where((col > row) & (col <= row + WINDOW) & (col >= first), 0.0, -1e30)


def attend_kernel(first_ref, q_ref, kv_ref, out_ref, lse_ref, bias_ref):
    fill_bias(first_ref, bias_ref)
    keyval = kv_ref[pl.ds(pl.program_id(0) * QBLOCK, SEEN), :]
    keys = keyval[:, :HEAD]
    lane = lax.broadcasted_iota(jnp.int32, (QBLOCK, 128), 1)
    lses = jnp.zeros((QBLOCK, 128), F32)
    outs = []
    for g in range(GROUP):
        scores = nt(q_ref[:, head_cols(g)] * BF16(SCALE), keys) + bias_ref[...]
        peak = jnp.max(scores, axis=1, keepdims=True)
        probs = jnp.exp(scores - peak)
        total = jnp.sum(probs, axis=1, keepdims=True)
        outs.append(low(nn(low(probs), keyval)[:, HEAD:] / total))
        lses = jnp.where(lane == g, peak + jnp.log(total), lses)
    out_ref[...] = jnp.concatenate(outs, 1)
    lse_ref[...] = lses


def attend_back_kernel(
    first_ref, q_ref, kv_ref, dout_ref, lse_ref, dq_ref, dkv_ref, bias_ref, probs_ref, dscores_ref
):
    block = pl.program_id(0)
    fill_bias(first_ref, bias_ref)

    @pl.when(block == 0)
    def _():
        dkv_ref[...] = jnp.zeros(dkv_ref.shape, F32)

    here = pl.ds(block * QBLOCK, SEEN)
    keyval = kv_ref[here, :]
    keys, values = keyval[:, :HEAD], keyval[:, HEAD:]
    lses = lse_ref[...]
    queries = [q_ref[:, head_cols(g)] * BF16(SCALE) for g in range(GROUP)]
    d_outs = [dout_ref[:, head_cols(g)] for g in range(GROUP)]
    d_queries = []
    for g in range(GROUP):
        rows = slice(g * QBLOCK, (g + 1) * QBLOCK)
        probs = jnp.exp(nt(queries[g], keys) + bias_ref[...] - lses[:, g : g + 1])
        weighted = probs * nt(d_outs[g], values)
        d_scores = low(weighted - probs * jnp.sum(weighted, axis=1, keepdims=True))
        probs_ref[rows, :] = low(probs)
        dscores_ref[rows, :] = d_scores
        d_queries.append(low(nn(d_scores, keys) * SCALE))
    dq_ref[...] = jnp.concatenate(d_queries, 1)
    d_keys = tn(dscores_ref[...], jnp.concatenate(queries, 0))
    d_values = tn(probs_ref[...], jnp.concatenate(d_outs, 0))
    dkv_ref[here, :] += jnp.concatenate([d_keys, d_values], 1)


def attention_call(kernel, ins, outs, scratch, micros):
    kinds = {
        "first": pl.BlockSpec(memory_space=pltpu.SMEM),
        "heads": pl.BlockSpec((QBLOCK, QW), lambda i: (i, 0)),
        "keys": pl.BlockSpec((WINDOW + TOK, 128), lambda i: (0, 0)),
        "lse": pl.BlockSpec((QBLOCK, 128), lambda i: (i, 0)),
    }
    shapes = {"heads": ((TOK, QW), BF16), "keys": ((WINDOW + TOK, 128), F32), "lse": ((TOK, 128), F32)}
    return pl.pallas_call(
        kernel,
        grid=(TOK // QBLOCK,),
        in_specs=[kinds[kind] for kind in ins],
        out_specs=[kinds[kind] for kind in outs],
        out_shape=[jax.ShapeDtypeStruct(*shapes[kind]) for kind in outs],
        scratch_shapes=[pltpu.VMEM((QBLOCK, SEEN), F32)] + [pltpu.VMEM((GROUP * QBLOCK, SEEN), BF16)] * scratch,
        compiler_params=pltpu.CompilerParams(
            dimension_semantics=("arbitrary",), vmem_limit_bytes=28 * 1024 * 1024
        ),
        cost_estimate=cost(micros),
    )


def first_key(line):
    return (WINDOW - line * TOK).reshape(1).astype(jnp.int32)


def attention_forward(query, keyval, line):
    call = attention_call(attend_kernel, ("first", "heads", "keys"), ("heads", "lse"), 0, 9)
    return call(first_key(line), query, keyval)


def attention_backward(query, keyval, lse, d_out, line):
    ins = ("first", "heads", "keys", "heads", "lse")
    call = attention_call(attend_back_kernel, ins, ("heads", "keys"), 2, 14)
    return call(first_key(line), query, keyval, d_out, lse)


def by_group(pieces):
    rows, _, cols = pieces.shape
    pieces = jnp.pad(pieces, ((0, 0), (0, 2 * RING - KV_HEADS), (0, 0)))
    pieces = pieces.reshape(rows, RING, 2, cols)
    mine = lax.dynamic_index_in_dim(pieces, lax.axis_index("wt"), 2, False)
    return jnp.swapaxes(mine, 0, 1)


def gather_lines(block):
    return lax.all_gather(block, YX, axis=0, tiled=True)


def reduce_lines(grads):
    return lax.psum_scatter(grads, YX, scatter_dimension=0, tiled=True)


TURNED = ROWS_PAD * (LINES - 1) + 128


def turn_features(x_ref, out_ref, first):
    for tile in range(DP // 128):
        cols = slice(128 * tile, 128 * tile + 128)
        out_ref[cols, first : first + TOK] = x_ref[:, cols].T.astype(F32)
    out_ref[DP:, first : first + TOK] = jnp.zeros((TURNED - DP, TOK), F32)


def two_blocks(turned_ref, pair):
    starts = [pl.multiple_of(ROWS_PAD * (2 * pair + k), 8) for k in range(2)]
    return jnp.concatenate([low(turned_ref[pl.ds(start, 128), :]) for start in starts], 0)


def ff_grads_kernel(x2_ref, cot_ref, d_gu_ref, act_ref, done_ref, out_ref, turned_ref):
    part = pl.program_id(0)

    def fill(right_ref):
        @pl.loop(0, LINES // 2)
        def _(pair):
            rows = pl.ds(pl.multiple_of(256 * pair, 256), 256)
            out_ref[rows, :] = low(nn(two_blocks(turned_ref, pair), right_ref[...]))

    @pl.when(part == 0)
    def _():
        turn_features(x2_ref, turned_ref, 0)

    @pl.when(part < 2)
    def _():
        fill(d_gu_ref)

    @pl.when(part == 2)
    def _():
        turn_features(cot_ref, turned_ref, 0)
        fill(act_ref)


def ff_grads(x2, cot, d_gate_up, act, done):
    def whole(cols):
        return pl.BlockSpec((TOK, cols), lambda i: (0, 0))

    return pl.pallas_call(
        ff_grads_kernel,
        grid=(3,),
        in_specs=[
            whole(DP),
            whole(DP),
            pl.BlockSpec((TOK, FF_PAD), lambda i: (0, jnp.minimum(i, 1))),
            whole(FF_PAD),
            pl.BlockSpec(memory_space=pl.ANY),
        ],
        out_specs=pl.BlockSpec((LINES * 128, FF_PAD), lambda i: (0, i)),
        out_shape=pltpu.HBM((LINES * 128, 3 * FF_PAD), BF16),
        scratch_shapes=[pltpu.VMEM((TURNED, TOK), F32)],
        compiler_params=pltpu.CompilerParams(
            dimension_semantics=("arbitrary",), vmem_limit_bytes=36 * 1024 * 1024
        ),
        cost_estimate=cost(11),
    )(x2, cot, d_gate_up, act, done)


LATE = DP + 512
PARTS = (0, 2 * DP, 2 * DP + RING * ATT_COLS, 2 * DP + RING * ATT_COLS + LATE)


def put(source_ref, out_ref, part, sem):
    copy = pltpu.make_async_copy(source_ref, out_ref.at[:, PARTS[part] : PARTS[part + 1]], sem)
    copy.start()
    copy.wait()


def channel_grads_kernel(x1_ref, d_mixer_ref, d_gate_ref, act_ref, out_ref, left_ref, got_ref, sem):
    def channels(source_ref, right_ref, cols):
        left_ref[...] = source_ref[...].T

        @pl.loop(0, CH // 256)
        def _(part):
            rows = pl.ds(pl.multiple_of(256 * part, 256), 256)
            got_ref[rows, cols] = low(nn(left_ref[rows, :], right_ref[...]))

    channels(d_gate_ref, x1_ref, slice(0, DP))
    channels(act_ref, d_mixer_ref, slice(DP, 2 * DP))
    put(got_ref, out_ref, 0, sem)


def attention_grads_kernel(x1_ref, d_attn_ref, right_ref, grads_ref, out_ref, turned_ref, got_ref, sem):
    turn_features(x1_ref, turned_ref, 0)
    turn_features(d_attn_ref, turned_ref, TOK)

    @pl.loop(0, LINES // 2)
    def _(pair):
        got = low(nn(two_blocks(turned_ref, pair), right_ref[...]))
        for block in range(2):
            rows = pl.ds(pl.multiple_of((2 * pair + block) * CH_PAD, CH_PAD), CH_PAD)
            for q in range(RING):
                first = 128 * block + CH_PAD * q
                got_ref[rows, ATT_COLS * q : ATT_COLS * (q + 1)] = got[first : first + CH_PAD, :]

    put(got_ref, out_ref, 1, sem)


def late_grads_kernel(late_ref, grads_ref, out_ref, sem):
    put(late_ref, out_ref, 2, sem)


def grads_call(kernel, arrays, grads, scratch, micros):
    whole, far = pl.BlockSpec(memory_space=pltpu.VMEM), pl.BlockSpec(memory_space=pltpu.HBM)
    given = [] if grads is None else [grads]
    return pl.pallas_call(
        kernel,
        in_specs=[whole] * len(arrays) + [far] * len(given),
        out_specs=far,
        out_shape=pltpu.HBM((CH, PARTS[3]), BF16),
        input_output_aliases={len(arrays): 0} if given else {},
        scratch_shapes=scratch + [pltpu.SemaphoreType.DMA(())],
        compiler_params=pltpu.CompilerParams(vmem_limit_bytes=36 * 1024 * 1024),
        cost_estimate=cost(micros),
    )(*arrays, *given)


def channel_grads(x1, d_mixer, d_gate, act):
    scratch = [pltpu.VMEM((CH, TOK), BF16), pltpu.VMEM((CH, 2 * DP), BF16)]
    return grads_call(channel_grads_kernel, (x1, d_mixer, d_gate, act), None, scratch, 5)


def attention_grads(x1, d_attn, d_qkv, attended, grads):
    right = [jnp.pad(d_qkv, ((0, 0), (0, QW))), jnp.pad(attended, ((0, 0), (ATT_COLS - QW, 0)))]
    scratch = [pltpu.VMEM((TURNED, 2 * TOK), F32), pltpu.VMEM((CH, RING * ATT_COLS), BF16)]
    return grads_call(attention_grads_kernel, (x1, d_attn, jnp.concatenate(right, 0)), grads, scratch, 8)


def late_grads(late, grads):
    return grads_call(late_grads_kernel, (late,), grads, [], 2)


def nothing_kernel(value_ref, done_ref, out_ref):
    pass


def tie(value, done):
    anywhere = pl.BlockSpec(memory_space=pl.ANY)
    return pl.pallas_call(
        nothing_kernel,
        in_specs=[anywhere, anywhere],
        out_specs=anywhere,
        out_shape=jax.ShapeDtypeStruct(value.shape, value.dtype),
        input_output_aliases={0: 0},
        compiler_params=pltpu.CompilerParams(vmem_limit_bytes=8 * 1024 * 1024),
        cost_estimate=cost(0),
    )(value, done)


def per_device(
    block_in, in_gain, w_query, w_keyval, w_out, attn_gain, ssm_gain, inner_weight, conv_weight, conv_bias,
    w_xproj, w_delta, delta_bias, log_decay, skip_gain, w_ssmout, mlp_gain, w_gateup, w_down, cotangent,
):
    core = lax.axis_index("wt")
    depth = lax.axis_index("z")
    line = lax.axis_index("y") * RING + lax.axis_index("x")

    own_in = lax.dynamic_slice_in_dim(pad_features(block_in), core * SPAN, SPAN, 0)
    own_cot = lax.dynamic_slice_in_dim(pad_features(cotangent), core * SPAN, SPAN, 0)
    gains = jnp.concatenate([in_gain, attn_gain, ssm_gain, mlp_gain])
    gains = jnp.pad(gains.reshape(1, 4 * PIECE), ((0, 15), (0, DP - 4 * PIECE)))
    mine = in_order(around(jnp.concatenate([own_in, gains], 0), "z"), "z")
    line_in = merge_cores(mine)
    gains = jnp.swapaxes(mine[:, SPAN, : 4 * PIECE].reshape(RING, 4, PIECE), 0, 1).reshape(4, ROWS)
    gains = jnp.pad(gains, ((0, 12), (0, 128 - ROWS)))
    gains_rows = in_order(around(in_order(around(gains, "x"), "x"), "y"), "y")
    gains = gains_rows.reshape(LINES, 16, 128)[:, :4, :ROWS].astype(F32)
    gains = jnp.pad(jnp.swapaxes(gains, 0, 1), ((0, 0), (0, 0), (0, ROWS_PAD - ROWS))).reshape(4, DP)
    in_g, attn_g, ssm_g, mlp_g = (gains[k : k + 1] for k in range(4))
    own_in = own_in.astype(F32)
    x1 = low(rms(line_in.astype(F32), in_g))

    attn_piece = jnp.concatenate(
        [
            by_group(w_query.reshape(PIECE, KV_HEADS, QW)),
            by_group(w_keyval[:, 0].reshape(PIECE, KV_HEADS, HEAD)),
            by_group(w_keyval[:, 1].reshape(PIECE, KV_HEADS, HEAD)),
            by_group(w_out.T.reshape(PIECE, KV_HEADS, QW)),
        ],
        2,
    )
    ff_piece = jnp.concatenate([w_gateup, w_down.T[:, None]], 1).reshape(PIECE, 3, RING, FF_PIECE)
    ff_piece = jnp.pad(ff_piece, ((0, 0), (0, 0), (0, 0), (0, FF_PAD - FF_PIECE)))
    ff_piece = jnp.transpose(ff_piece, (2, 0, 1, 3)).reshape(RING, PIECE, 3 * FF_PAD)
    parts = jnp.pad(jnp.concatenate([attn_piece, ff_piece], 2), ((0, 0), (0, CH_PAD - PIECE), (0, 0)))
    halves = jnp.concatenate([own_cot[:CH_PAD], own_cot[CH_PAD:]], 1)
    parts = jnp.concatenate([parts, jnp.broadcast_to(halves, (RING,) + halves.shape)], 2)
    parts = sent_along(tie(parts, mine), "z")
    cols = ATT_COLS + 3 * FF_PAD

    def plan(ins, outs):
        pairs = []
        for k, part in enumerate(ins[:RING]):
            pairs.append((part.at[:, :cols], outs[0].at[spot("z", k)]))
            for half in range(2):
                source = part.at[:, cols + DP * half : cols + DP * (half + 1)]
                pairs.append((source, outs[1].at[spot("z", k), CH_PAD * half : CH_PAD * (half + 1)]))
        return pairs

    piece, mine_cot = copy_call(plan, 3 * RING, parts + [gains_rows], [(RING, CH_PAD, cols), (RING, SPAN, DP)])
    line_cot = merge_cores(mine_cot)
    piece = piece[:, :PIECE].reshape(ROWS, cols)
    piece = jnp.pad(piece, ((0, ROWS_PAD - ROWS), (0, 0)))
    attn_piece, ff_piece = piece[:, :ATT_COLS], piece[:, ATT_COLS:]
    out_piece = jnp.pad(pad_features(w_ssmout), ((0, CH_PAD - PIECE), (0, 0))).reshape(4, 8, DP // 128, 128)
    out_piece = jnp.transpose(out_piece, (2, 1, 0, 3)).reshape(ROWS_PAD, 512)
    attn_piece = jnp.concatenate([attn_piece, out_piece], 1)

    inner_rows = jnp.transpose(inner_weight, (2, 1, 0))
    small = jnp.concatenate(
        [conv_weight.T, conv_bias[:, None], delta_bias[:, None], skip_gain[:, None], log_decay.T], 1
    )
    channel = jnp.concatenate(
        [
            pad_features(inner_rows).reshape(PIECE, 2 * DP),
            jnp.pad(w_xproj[:, :DTR], ((0, 0), (0, RANK_PAD - DTR))),
            jnp.pad(w_xproj[:, DTR:], ((0, 0), (0, 256 - XROWS))),
            jnp.pad(w_delta.T, ((0, 0), (0, 128 - DTR))),
            jnp.pad(small, ((0, 0), (0, SMALL - SMALL_USED))),
        ],
        1,
    )
    channel = jnp.pad(channel, ((0, CH_PAD - PIECE), (0, 0)))

    with jax.named_scope("gather_channels"):
        channel = gather_lines(channel)
    with jax.named_scope("gather_attention"):
        w_attn = gather_lines(attn_piece)
    with jax.named_scope("gather_ff"):
        w_ff = gather_lines(ff_piece)
    w_so = w_attn[:, ATT_COLS:].reshape(LINES, DP // 128, 8, 4, 128)
    w_so = jnp.transpose(w_so, (0, 3, 2, 1, 4)).reshape(CH, DP)

    w_conv, w_gate = channel[:, :DP], channel[:, COLS[1] : COLS[2]]
    w_x = channel[:, COLS[2] : COLS[2] + XROWS]
    w_d = channel[:, COLS[3] : COLS[3] + DTR]
    small = channel[:, COLS[4] : COLS[5]].astype(F32)
    small_rows = small[:, :32].T
    taps, c_bias, d_bias, skip = small_rows[:CONV], small_rows[4:5], small_rows[5:6], small_rows[6:7]
    rate2 = -jnp.exp(small_rows[7 : 7 + STATE]) * LOG2E
    conv_in = low(nt(x1, w_conv))
    gate_z = low(nt(x1, w_gate)).astype(F32)
    edge = line_shift(conv_in[TOK - (CONV - 1) :], 1)
    padded_in = jnp.concatenate([edge, conv_in], 0).astype(F32)
    conv_out = c_bias
    for tap in range(CONV):
        conv_out = conv_out + taps[tap : tap + 1] * padded_in[tap : tap + TOK]
    mixer_low = low(jax.nn.silu(conv_out))
    mixer_in = mixer_low.astype(F32)
    xproj = sum_line(dot(w_x, mixer_low, ((0,), (1,))))
    step_low = low(xproj[:DTR])
    in_mix, out_mix = spread(xproj[RANK_PAD : RANK_PAD + STATE]), spread(xproj[RANK_PAD + STATE :])
    step_pre = dot(step_low, w_d, ((0,), (1,))) + d_bias
    step = jax.nn.softplus(step_pre)
    ends, spans, pay = scan_ends(step, mixer_in, in_mix, rate2)
    before, rows = state_along_x(rate2, pay, False)

    qkv = low(nn(x1, w_attn[:, : QW + 2 * HEAD]))
    enter, _ = state_along_y(rate2, before, rows, False)
    query, keyval = qkv[:, :QW], qkv[:, QW:]
    keyval = jnp.concatenate([line_shift(keyval, 2), line_shift(keyval, 1), keyval], 0)
    attended, lse = attention_forward(query, keyval, line)
    w_o = w_attn[:, QW + 2 * HEAD : ATT_COLS]
    attn_part = low(nt(attended, w_o))

    ssm_y = scan_outputs(step, mixer_in, in_mix, out_mix, rate2, ends, spans, enter) + skip * mixer_in
    silu_z = jax.nn.silu(gate_z)
    mixer_act = low(ssm_y * silu_z)
    branches, _ = scatter_tokens(jnp.concatenate([attn_part, low(nn(mixer_act, w_so))], 1))
    attn_out, mixer_out = branches[:, :DP], branches[:, DP:]

    hidden = own_in + 0.5 * (rms(attn_out, attn_g) + rms(mixer_out, ssm_g))
    x2 = gather_tokens(low(rms(hidden, mlp_g)))
    w_gu, w_dn = w_ff[:, : 2 * FF_PAD], w_ff[:, 2 * FF_PAD :]
    gate_up = low(nn(x2, w_gu)).astype(F32)
    gate, upper = gate_up[:, :FF_PAD], gate_up[:, FF_PAD:]
    silu_gate = jax.nn.silu(gate)
    mlp_act = low(silu_gate * upper)
    d_act = nn(line_cot, w_dn)
    d_gate_up = low(jnp.concatenate([d_act * upper * silu_grad(gate), d_act * silu_gate], 1))
    d_x2 = add_cores(low(nt(d_gate_up, w_gu)))
    d_x2, arrived = add_ring(d_x2)
    grad_ff = ff_grads(x2, line_cot, d_gate_up, mlp_act, arrived)
    with jax.named_scope("reduce_ff"):
        grad_ff = reduce_lines(grad_ff)

    d_norm, d_mlp_g = rms_back(hidden, mlp_g, d_x2)
    d_hidden = own_cot.astype(F32) + d_norm
    d_attn, d_attn_g = rms_back(attn_out, attn_g, 0.5 * d_hidden)
    d_mixer, d_ssm_g = rms_back(mixer_out, ssm_g, 0.5 * d_hidden)
    blocks = around(low(d_mixer), "z")
    d_mixer = merge_cores(in_order(blocks, "z"))
    blocks = around(tie(low(d_attn), blocks[2]), "z")
    d_attn = merge_cores(in_order(blocks, "z"))

    d_mact = nt(d_mixer, w_so)
    dy = d_mact * silu_z
    d_gate_low = low(d_mact * ssm_y * silu_grad(gate_z))
    heads, pay = scan_heads(step, dy, out_mix, tie(rate2, blocks[1]), spans)
    before, rows = state_along_x(rate2, pay, True)
    enter_back, arrived = state_along_y(rate2, before, rows, True)

    d_attended = low(nn(d_attn, w_o))
    d_query, d_keyval = attention_backward(query, keyval, tie(lse, arrived), d_attended, line)
    d_keyval = (
        d_keyval[2 * TOK :]
        + line_shift(low(d_keyval[TOK : 2 * TOK]), -1).astype(F32)
        + line_shift(low(d_keyval[:TOK]), -2).astype(F32)
    )
    d_qkv = jnp.concatenate([d_query, low(d_keyval)], 1)
    grads = channel_grads(x1, d_mixer, d_gate_low, mixer_act)
    grads = attention_grads(x1, d_attn, d_qkv, attended, grads)

    d_step, lam_b, grad_decay, d_mixes = scan_backward(
        step, mixer_in, dy, in_mix, out_mix, rate2, ends, spans, enter, heads, enter_back
    )
    d_step_pre = (d_step + lam_b * mixer_in) * jax.nn.sigmoid(step_pre)
    d_step_low = low(d_step_pre)
    grad_d = tn(d_step_low, step_low.T)
    d_rank = dot(w_d, d_step_low, ((0,), (1,)))
    d_xproj = jnp.concatenate([jnp.pad(d_rank, ((0, RANK_PAD - DTR), (0, 0))), d_mixes[:, : 2 * STATE].T], 0)
    d_xproj = low(sum_line(d_xproj))
    grad_x = dot(mixer_low, d_xproj, ((0,), (1,)))
    d_mixer_in = dy * skip + step * lam_b + dot(d_xproj, w_x, ((0,), (1,)))
    d_conv_out = d_mixer_in * silu_grad(conv_out)
    d_after = jnp.concatenate([d_conv_out, line_shift(d_conv_out[: CONV - 1], -1)], 0)
    d_conv_in = sum(taps[k : k + 1] * d_after[CONV - 1 - k : CONV - 1 - k + TOK] for k in range(CONV))
    small_grads = jnp.stack(
        [jnp.sum(d_conv_out * padded_in[tap : tap + TOK], axis=0) for tap in range(CONV)]
        + [jnp.sum(d_conv_out, axis=0), jnp.sum(d_step_pre, axis=0), jnp.sum(dy * mixer_in, axis=0)],
        0,
    )
    small_grads = jnp.concatenate([small_grads, grad_decay], 0).T
    d_conv_low = low(d_conv_in)
    grad_conv = low(tn(d_conv_low, x1))

    d_x1 = nt(d_qkv, w_attn[:, : QW + 2 * HEAD]) + nn(d_conv_low, w_conv) + nn(d_gate_low, w_gate)
    d_in_g = jnp.sum(rms(line_in.astype(F32), 1.0) * d_x1, axis=0)
    gain_grads = jnp.stack([d_in_g, d_attn_g, d_ssm_g, d_mlp_g]).reshape(4, LINES, ROWS_PAD)[:, :, :ROWS]
    gain_grads = jnp.pad(jnp.swapaxes(gain_grads, 0, 1), ((0, 0), (PIECE, CH_PAD - PIECE - 4), (GAIN_AT, 0)))
    small_grads = jnp.pad(small_grads, ((0, 0), (0, SMALL - SMALL_USED))) + gain_grads.reshape(CH, SMALL)
    grad_late = jnp.concatenate(
        [
            grad_conv,
            low(jnp.pad(grad_x, ((0, 0), (0, 256 - XROWS)))),
            low(jnp.pad(grad_d, ((0, 0), (0, 128 - DTR)))),
            low(small_grads),
        ],
        1,
    )
    with jax.named_scope("reduce_rest"):
        grads = reduce_lines(late_grads(grad_late, grads))
    grad_early, grad_late = grads[:, : 2 * DP], grads[:, PARTS[2] :].astype(F32)
    grad_attn = jnp.swapaxes(grads[:, PARTS[1] : PARTS[2]].reshape(CH_PAD, RING, ATT_COLS), 0, 1)
    grad_attn = grad_attn.reshape(RING * CH_PAD, ATT_COLS)
    d_x1, _ = scatter_tokens(low(d_x1))
    d_norm, _ = rms_back(own_in, in_g, d_x1)
    grad_in = d_hidden + d_norm
    mlp_out, _ = scatter_tokens(low(nt(tie(mlp_act, d_conv_low), w_dn)))
    block_out = low(hidden + mlp_out)

    first = core == 0

    def both_cores(own):
        other = swap_core(own)
        return jnp.concatenate([jnp.where(first, own, other), jnp.where(first, other, own)], 0)

    block_out = drop_features(both_cores(block_out))
    grad_in = drop_features(both_cores(grad_in))

    def to_owner(grads):
        return exchange(low(grads[:ROWS]).reshape(RING, PIECE, grads.shape[1]), "z").astype(F32)

    grad_ff = to_owner(grad_ff).reshape(RING, PIECE, 3, FF_PAD)[..., :FF_PIECE]
    grad_ff = jnp.transpose(grad_ff, (1, 2, 0, 3)).reshape(PIECE, 3, RING * FF_PIECE)
    grad_gateup, grad_down = grad_ff[:, :2], grad_ff[:, 2].T

    grad_attn = to_owner(grad_attn)
    other = swap_core(grad_attn)
    grad_attn = jnp.stack([jnp.where(first, grad_attn, other), jnp.where(first, other, grad_attn)], 1)
    grad_attn = jnp.transpose(grad_attn, (2, 0, 1, 3)).reshape(PIECE, 2 * RING, ATT_COLS)[:, :KV_HEADS]
    grad_query = grad_attn[..., :QW].reshape(PIECE, HEADS * HEAD)
    grad_keyval = grad_attn[..., QW : QW + 2 * HEAD].reshape(PIECE, KV_HEADS, 2, HEAD)
    grad_keyval = jnp.swapaxes(grad_keyval, 1, 2).reshape(PIECE, 2, KV_HEADS * HEAD)
    grad_out = grad_attn[..., QW + 2 * HEAD :].reshape(PIECE, HEADS * HEAD).T

    gain_grads = grad_late[PIECE : PIECE + 4, DP + 384 + GAIN_AT :]
    grad_early, grad_late = grad_early[:PIECE, : 2 * DP].astype(F32), grad_late[:PIECE]
    grad_inner = jnp.stack([grad_late[:, :DP], grad_early[:, :DP]], 1)
    grad_inner = jnp.transpose(drop_features(grad_inner), (2, 1, 0))
    grad_ssmout = drop_features(grad_early[:, DP : 2 * DP])
    grad_xproj = grad_late[:, DP : DP + XROWS]
    grad_xproj = jnp.concatenate([grad_xproj[:, :DTR], grad_xproj[:, RANK_PAD:]], 1)
    grad_delta = grad_late[:, DP + 256 : DP + 256 + DTR].T
    small_grads = grad_late[:, DP + 384 : DP + 384 + SMALL_USED].T

    gain_grads = gain_grads + swap_core(gain_grads)
    gain_grads = sum(around(gain_grads, "z"))
    gain_grads = lax.dynamic_slice_in_dim(gain_grads, depth * PIECE, PIECE, 1)

    return (
        block_out, grad_in, gain_grads[0], grad_query, grad_keyval, grad_out, gain_grads[1], gain_grads[2],
        grad_inner, small_grads[:CONV], small_grads[4], grad_xproj, grad_delta, small_grads[5],
        small_grads[7 : 7 + STATE], small_grads[6], grad_ssmout, gain_grads[3], grad_gateup, grad_down,
    )


def solution(mesh):
    fine = Mesh(mesh.devices.reshape(RING, RING, RING, 2), ("y", "x", "z", "wt"))
    both = SEQ + ("wt",)
    weights = (
        P(SEQ),
        P(SEQ, None),
        P(SEQ, None, None),
        P(None, SEQ),
        P(SEQ),
        P(SEQ),
        P(None, None, both),
        P(None, both),
        P(both),
        P(both, None),
        P(None, both),
        P(both),
        P(None, both),
        P(both),
        P(both, None),
        P(SEQ),
        P(SEQ, None, "wt"),
        P("wt", SEQ),
    )
    rows = P(SEQ, None)
    return jax.shard_map(
        per_device, mesh=fine, in_specs=(rows,) + weights + (rows,), out_specs=(rows, rows) + weights, check_vma=False
    )
```

```python
import functools
import math

import jax
import jax.numpy as jnp
from jax import lax
from jax.experimental import pallas as pl
from jax.experimental.pallas import tpu as pltpu
from jax.sharding import Mesh
from jax.sharding import PartitionSpec as P

F32 = jnp.float32
BF16 = jnp.bfloat16

HEADS = 25
KV_HEADS = 5
GROUP = HEADS // KV_HEADS
HEAD = 64
STATE = 16
DTR = 100
CONV = 4
WINDOW = 1024
D = 1600
QW = GROUP * HEAD
EPS = 1e-06
LOG2E = math.log2(math.e)

YX = ("y", "x")
SEQ = ("y", "x", "z")
RING = 4
LINES = 16
PIECE = 25
ROWS = RING * PIECE
ROWS_PAD = 104
DP = LINES * ROWS_PAD
CH_PAD = 32
CH = LINES * CH_PAD
SPAN = 64
CHUNKS = 8
TOK = SPAN * CHUNKS
FF_PIECE = 688
FF_PAD = 768
ATT_COLS = 768
RANK_PAD = 104
XROWS = RANK_PAD + 2 * STATE
PAY = STATE + 8
SMALL = 128
SMALL_USED = CONV + 3 + STATE
COLS = (0, DP, 2 * DP, 2 * DP + 256, 2 * DP + 384, 2 * DP + 512)


def dot(left, right, dims):
    return lax.dot_general(left, right, (dims, ((), ())), preferred_element_type=F32)


def nn(left, right):
    return dot(left, right, ((1,), (0,)))


def nt(left, right):
    return dot(left, right, ((1,), (1,)))


def tn(left, right):
    return dot(left, right, ((0,), (0,)))


def low(value):
    return value.astype(BF16)


def pad_features(value):
    lead = value.shape[:-1]
    value = value.reshape(lead + (LINES, ROWS))
    value = jnp.pad(value, [(0, 0)] * (len(lead) + 1) + [(0, ROWS_PAD - ROWS)])
    return value.reshape(lead + (DP,))


def drop_features(value):
    lead = value.shape[:-1]
    return value.reshape(lead + (LINES, ROWS_PAD))[..., :ROWS].reshape(lead + (D,))


def step_to(axis, distance):
    return [(i, (i + distance) % RING) for i in range(RING)]


def around(value, axis):
    return [value] + [lax.ppermute(value, axis, step_to(axis, RING - d)) for d in range(1, RING)]


def copy_kernel(plan, count, *refs):
    ins, outs, sems = refs[:count], refs[count:-1], refs[-1]
    copies = [pltpu.make_async_copy(src, dst, sems.at[k]) for k, (src, dst) in enumerate(plan(ins, outs))]
    for copy in copies:
        copy.start()
    for copy in copies:
        copy.wait()


def copy_call(plan, number, arrays, shapes, near=False):
    anywhere = pl.BlockSpec(memory_space=pl.ANY)
    return pl.pallas_call(
        functools.partial(copy_kernel, plan, len(arrays)),
        in_specs=[anywhere] * len(arrays),
        out_specs=[pl.BlockSpec(memory_space=pltpu.VMEM) if near else anywhere] * len(shapes),
        out_shape=[
            pltpu.VMEM(shape, arrays[0].dtype) if near else jax.ShapeDtypeStruct(shape, arrays[0].dtype)
            for shape in shapes
        ],
        scratch_shapes=[pltpu.SemaphoreType.DMA((number,))],
        compiler_params=pltpu.CompilerParams(vmem_limit_bytes=8 * 1024 * 1024),
        cost_estimate=cost(1),
    )(*arrays)


def spot(axis, k):
    return lax.rem(lax.axis_index(axis) + k, RING)


def in_order(blocks, axis):
    def plan(ins, outs):
        return [(block, outs[0].at[spot(axis, k)]) for k, block in enumerate(ins)]

    return copy_call(plan, RING, blocks, [(RING,) + blocks[0].shape])[0]


def swap_core(value):
    return lax.ppermute(value, "wt", [(0, 1), (1, 0)])


def sent_along(pieces, axis):
    here = lax.axis_index(axis)
    got = [lax.dynamic_index_in_dim(pieces, here, 0, False)]
    for d in range(1, RING):
        piece = lax.dynamic_index_in_dim(pieces, (here + RING - d) % RING, 0, False)
        got.append(lax.ppermute(piece, axis, step_to(axis, RING - d)))
    return got


def exchange(pieces, axis):
    return in_order(sent_along(pieces, axis), axis)


def gather_tokens(own):
    return merge_cores(in_order(around(own, "z"), "z"))


def merge_cores(mine):
    wide, rows = mine.shape[2], pl.ds(0, SPAN)

    def plan(ins, outs):
        core = lax.axis_index("wt")
        return [(part.at[:, rows], outs[0].at[:, place]) for place, part in ((core, ins[0]), (1 - core, ins[1]))]

    return copy_call(plan, 2, [mine, swap_core(mine)], [(RING, 2, SPAN, wide)], True)[0].reshape(TOK, wide)


def add_cores(partial):
    core = lax.axis_index("wt")
    parts = partial.reshape(RING, 2, SPAN, partial.shape[1])
    mine = lax.dynamic_index_in_dim(parts, core, 1, False)
    theirs = lax.dynamic_index_in_dim(parts, 1 - core, 1, False)
    return mine.astype(F32) + swap_core(theirs).astype(F32)


def add_ring(mine):
    here = lax.axis_index("z")
    total, parts = lax.dynamic_index_in_dim(mine, here, 0, False), []
    for d in range(1, RING):
        piece = lax.dynamic_index_in_dim(mine, (here + d) % RING, 0, False)
        parts.append(lax.ppermute(low(piece), "z", step_to("z", d)))
        total = total + parts[-1].astype(F32)
    return total, parts[0]


def scatter_tokens(partial):
    return add_ring(add_cores(partial))


def sum_line(value):
    value = value + swap_core(value)
    parts = around(low(value), "z")
    return value + (parts[1].astype(F32) + parts[2].astype(F32) + parts[3].astype(F32)), parts[1]


def line_shift(value, distance):
    route = [(i, i + distance) for i in range(LINES) if 0 <= i + distance < LINES]
    return lax.ppermute(value, YX, route)


def rms(value, gain):
    scale = lax.rsqrt(jnp.sum(value * value, axis=-1, keepdims=True) / D + EPS)
    return value * scale * gain


def rms_back(value, gain, dy):
    r = lax.rsqrt(jnp.sum(value * value, axis=-1, keepdims=True) / D + EPS)
    inner = jnp.sum(value * gain * dy, axis=-1, keepdims=True) / D
    return r * gain * dy - value * (r * r * r) * inner, jnp.sum(value * r * dy, axis=0)


def silu_grad(value):
    sig = jax.nn.sigmoid(value)
    return sig * (1.0 + value * (1.0 - sig))


def rows_at(ref, tau):
    return ref[pl.ds(tau, CHUNKS, stride=SPAN), :]


def spread(rows):
    rows = jnp.transpose(rows.reshape(STATE, CHUNKS, SPAN), (2, 0, 1))
    return jnp.broadcast_to(rows[..., None], (SPAN, STATE, CHUNKS, 128))


def rate_rows(rate_ref):
    return [jnp.broadcast_to(rate_ref[n : n + 1, :], (CHUNKS, 128)) for n in range(STATE)]


def zeros():
    return jnp.zeros((CHUNKS, 128), F32)


def walk(start, ends_ref, spans_ref, rate_ref, starts_ref=None, backward=False):
    state, order = start, range(CHUNKS)
    for chunk in reversed(order) if backward else order:
        rows = pl.ds(chunk, STATE, stride=CHUNKS)
        if starts_ref is not None:
            starts_ref[rows, :] = state
        state = jnp.exp2(rate_ref[...] * spans_ref[chunk : chunk + 1, :]) * state + ends_ref[rows, :]
    return state


def chunk_rows(n):
    return slice(CHUNKS * n, CHUNKS * n + CHUNKS)


def report(pay_ref, state, spans_ref):
    pay_ref[:STATE, :] = state
    total = jnp.sum(spans_ref[...], axis=0, keepdims=True)
    pay_ref[STATE:, :] = jnp.broadcast_to(total, (PAY - STATE, 128))


def ends_kernel(step_ref, in_ref, b_ref, rate_ref, end_ref, span_ref, pay_ref):
    rates = rate_rows(rate_ref)

    def token(tau, carry):
        states, total = carry
        step = rows_at(step_ref, tau)
        push = step * rows_at(in_ref, tau)
        states = [jnp.exp2(step * rates[n]) * states[n] + push * b_ref[tau, n] for n in range(STATE)]
        return states, total + step

    states, total = lax.fori_loop(0, SPAN, token, ([zeros()] * STATE, zeros()), unroll=8)
    for n in range(STATE):
        end_ref[chunk_rows(n), :] = states[n]
    span_ref[...] = total
    report(pay_ref, walk(jnp.zeros((STATE, 128), F32), end_ref, span_ref, rate_ref), span_ref)


def outputs_kernel(step_ref, in_ref, b_ref, c_ref, rate_ref, end_ref, span_ref, enter_ref, y_ref, init_ref):
    rates = rate_rows(rate_ref)
    walk(enter_ref[...], end_ref, span_ref, rate_ref, init_ref)

    def token(tau, states):
        step = rows_at(step_ref, tau)
        push = step * rows_at(in_ref, tau)
        states = [jnp.exp2(step * rates[n]) * states[n] + push * b_ref[tau, n] for n in range(STATE)]
        y_ref[pl.ds(tau, CHUNKS, stride=SPAN), :] = sum(c_ref[tau, n] * states[n] for n in range(STATE))
        return states

    lax.fori_loop(0, SPAN, token, [init_ref[chunk_rows(n), :] for n in range(STATE)], unroll=8)


def heads_kernel(step_ref, dy_ref, c_ref, rate_ref, span_ref, head_ref, pay_ref):
    rates = rate_rows(rate_ref)

    def token(back, carry):
        tau = SPAN - 1 - back
        step = rows_at(step_ref, tau)
        dy = rows_at(dy_ref, tau)
        return [jnp.exp2(step * rates[n]) * (c_ref[tau, n] * dy + carry[n]) for n in range(STATE)]

    carry = lax.fori_loop(0, SPAN, token, [zeros()] * STATE, unroll=8)
    for n in range(STATE):
        head_ref[chunk_rows(n), :] = carry[n]
    state = walk(jnp.zeros((STATE, 128), F32), head_ref, span_ref, rate_ref, backward=True)
    report(pay_ref, state, span_ref)


def backward_kernel(
    step_ref, in_ref, dy_ref, b_ref, c_ref, rate_ref, end_ref, span_ref, enter_ref, head_ref, enter_back_ref,
    dstep_ref, lamb_ref, ddecay_ref, dmix_ref,
    a_ref, h_ref, din_ref, dout_ref, init_ref, lam_ref,
):
    rates = rate_rows(rate_ref)

    @pl.when(pl.program_id(0) == 0)
    def _():
        @pl.loop(0, SPAN)
        def _(tau):
            din_ref[tau] = jnp.zeros((STATE, CHUNKS, 128), F32)
            dout_ref[tau] = jnp.zeros((STATE, CHUNKS, 128), F32)

    walk(enter_ref[...], end_ref, span_ref, rate_ref, init_ref)
    walk(enter_back_ref[...], head_ref, span_ref, rate_ref, lam_ref, backward=True)
    for n in range(STATE):
        h_ref[0, n] = init_ref[chunk_rows(n), :]

    def forth(tau, states):
        step = rows_at(step_ref, tau)
        push = step * rows_at(in_ref, tau)
        states = list(states)
        for n in range(STATE):
            decay = jnp.exp2(step * rates[n])
            a_ref[tau, n] = decay
            states[n] = decay * states[n] + push * b_ref[tau, n]
            h_ref[tau + 1, n] = states[n]
        return states

    lax.fori_loop(0, SPAN, forth, [init_ref[chunk_rows(n), :] for n in range(STATE)], unroll=4)

    def back(backwards, carry):
        tau = SPAN - 1 - backwards
        lams, decays = list(carry[0]), list(carry[1])
        step = rows_at(step_ref, tau)
        push = step * rows_at(in_ref, tau)
        dy = rows_at(dy_ref, tau)
        dstep, lamb = zeros(), zeros()
        for n in range(STATE):
            lam = c_ref[tau, n] * dy + lams[n]
            lams[n] = a_ref[tau, n] * lam
            along = lams[n] * h_ref[tau, n]
            dstep = dstep + along * rates[n]
            lamb = lamb + lam * b_ref[tau, n]
            decays[n] = decays[n] + along * step
            din_ref[tau, n] += lam * push
            dout_ref[tau, n] += dy * h_ref[tau + 1, n]
        dstep_ref[pl.ds(tau, CHUNKS, stride=SPAN), :] = dstep * (1.0 / LOG2E)
        lamb_ref[pl.ds(tau, CHUNKS, stride=SPAN), :] = lamb
        return lams, decays

    start = ([lam_ref[chunk_rows(n), :] for n in range(STATE)], [zeros()] * STATE)
    _, decays = lax.fori_loop(0, SPAN, back, start, unroll=4)
    total = jnp.concatenate([jnp.sum(decays[n], axis=0, keepdims=True) for n in range(STATE)], 0)
    ddecay_ref[...] = total * rate_ref[...] * (1.0 / LOG2E)

    @pl.when(pl.program_id(0) == pl.num_programs(0) - 1)
    def _():
        lane = lax.broadcasted_iota(jnp.int32, (CHUNKS, 128), 1)

        def fold(tau, carry):
            rows = zeros()
            for n in range(STATE):
                rows = jnp.where(lane == n, jnp.sum(din_ref[tau, n], axis=1, keepdims=True), rows)
                total = jnp.sum(dout_ref[tau, n], axis=1, keepdims=True)
                rows = jnp.where(lane == STATE + n, total, rows)
            dmix_ref[pl.ds(tau, CHUNKS, stride=SPAN), :] = rows
            return carry

        lax.fori_loop(0, SPAN, fold, 0, unroll=8)


def cost(micros):
    return pl.CostEstimate(flops=int(micros * 1e9), bytes_accessed=int(micros * 3e6), transcendentals=0)


def scan_call(kernel, ins, outs, scratch, micros):
    wide = (SPAN, STATE, CHUNKS, 128)
    once = pl.BlockSpec(wide, lambda i: (0, 0, 0, 0), pipeline_mode=pl.Buffered(1))

    def lanes(rows):
        return (rows, CH), pl.BlockSpec((rows, 128), lambda i: (0, i))

    kinds = {
        "tok": lanes(TOK),
        "mix": ((TOK, 128), pl.BlockSpec((TOK, 128), lambda i: (0, 0))),
        "state": lanes(STATE),
        "states": lanes(STATE * CHUNKS),
        "chunk": lanes(CHUNKS),
        "pay": lanes(PAY),
        "wide": (wide, once),
    }
    return pl.pallas_call(
        kernel,
        grid=(CH // 128,),
        in_specs=[kinds[kind][1] for kind in ins],
        out_specs=[kinds[kind][1] for kind in outs],
        out_shape=[jax.ShapeDtypeStruct(kinds[kind][0], F32) for kind in outs],
        scratch_shapes=[pltpu.VMEM(shape, F32) for shape in scratch],
        compiler_params=pltpu.CompilerParams(
            dimension_semantics=("arbitrary",), vmem_limit_bytes=36 * 1024 * 1024
        ),
        cost_estimate=cost(micros),
    )


WALK = (STATE * CHUNKS, 128)


def scan_ends(*args):
    ins = ("tok", "tok", "wide", "state")
    return scan_call(ends_kernel, ins, ("states", "chunk", "pay"), (), 5)(*args)


def scan_outputs(*args):
    ins = ("tok", "tok", "wide", "wide", "state", "states", "chunk", "state")
    return scan_call(outputs_kernel, ins, ("tok",), (WALK,), 7)(*args)[0]


def scan_heads(*args):
    ins = ("tok", "tok", "wide", "state", "chunk")
    return scan_call(heads_kernel, ins, ("states", "pay"), (), 5)(*args)


def scan_backward(*args):
    ins = ("tok", "tok", "tok", "wide", "wide", "state", "states", "chunk", "state", "states", "state")
    outs = ("tok", "tok", "state", "mix")
    wide = [(SPAN + extra, STATE, CHUNKS, 128) for extra in (0, 1, 0, 0)]
    return scan_call(backward_kernel, ins, outs, wide + [WALK, WALK], 20)(*args)


def nearer(value, axis, backward):
    here = lax.axis_index(axis)
    if backward:
        here = RING - 1 - here
    steps = ((d, lax.ppermute(value, axis, step_to(axis, -d if backward else d))) for d in (3, 2, 1))
    return here, list(steps)


def fold(rate2, blocks, keep):
    state, span = jnp.zeros_like(rate2), jnp.zeros_like(rate2[:1])
    for d, block in blocks:
        block_span = block[STATE : STATE + 1]
        longer = jnp.exp2(rate2 * block_span) * state + block[:STATE]
        state = jnp.where(keep(d), longer, state)
        span = jnp.where(keep(d), span + block_span, span)
    return state, span


def state_along_x(rate2, pay, backward):
    here, blocks = nearer(pay, "x", backward)
    before = fold(rate2, blocks, lambda d: d <= here)
    after, after_span = fold(rate2, blocks, lambda d: d > here)
    own_span = pay[STATE : STATE + 1]
    whole = jnp.exp2(rate2 * own_span) * before[0] + pay[:STATE]
    whole = jnp.exp2(rate2 * after_span) * whole + after
    rows = jnp.concatenate([whole, jnp.broadcast_to(before[1] + own_span + after_span, (PAY - STATE, CH))], 0)
    return before, rows


def state_along_y(rate2, before, rows, backward):
    here, blocks = nearer(rows, "y", backward)
    above, _ = fold(rate2, blocks, lambda d: d <= here)
    return jnp.exp2(rate2 * before[1]) * above + before[0], blocks[-1][1]


QBLOCK = 128
SCALE = HEAD ** (-0.5)
SEEN = WINDOW + QBLOCK


def head_cols(g):
    return slice(HEAD * g, HEAD * g + HEAD)


def fill_bias(first_ref, bias_ref):
    row = lax.broadcasted_iota(jnp.int32, (QBLOCK, SEEN), 0)
    col = lax.broadcasted_iota(jnp.int32, (QBLOCK, SEEN), 1)
    first = first_ref[0] - pl.program_id(0) * QBLOCK
    bias_ref[...] = jnp.where((col > row) & (col <= row + WINDOW) & (col >= first), 0.0, -1e30)


def attend_kernel(first_ref, q_ref, kv_ref, out_ref, lse_ref, bias_ref):
    fill_bias(first_ref, bias_ref)
    keyval = kv_ref[pl.ds(pl.program_id(0) * QBLOCK, SEEN), :]
    keys = keyval[:, :HEAD]
    lane = lax.broadcasted_iota(jnp.int32, (QBLOCK, 128), 1)
    lses = jnp.zeros((QBLOCK, 128), F32)
    outs = []
    for g in range(GROUP):
        scores = nt(q_ref[:, head_cols(g)] * BF16(SCALE), keys) + bias_ref[...]
        peak = jnp.max(scores, axis=1, keepdims=True)
        probs = jnp.exp(scores - peak)
        total = jnp.sum(probs, axis=1, keepdims=True)
        outs.append(low(nn(low(probs), keyval)[:, HEAD:] / total))
        lses = jnp.where(lane == g, peak + jnp.log(total), lses)
    out_ref[...] = jnp.concatenate(outs, 1)
    lse_ref[...] = lses


def attend_back_kernel(
    first_ref, q_ref, kv_ref, dout_ref, lse_ref, dq_ref, dkv_ref, bias_ref, probs_ref, dscores_ref
):
    block = pl.program_id(0)
    fill_bias(first_ref, bias_ref)

    @pl.when(block == 0)
    def _():
        dkv_ref[...] = jnp.zeros(dkv_ref.shape, F32)

    here = pl.ds(block * QBLOCK, SEEN)
    keyval = kv_ref[here, :]
    keys, values = keyval[:, :HEAD], keyval[:, HEAD:]
    lses = lse_ref[...]
    queries = [q_ref[:, head_cols(g)] * BF16(SCALE) for g in range(GROUP)]
    d_outs = [dout_ref[:, head_cols(g)] for g in range(GROUP)]
    d_queries = []
    for g in range(GROUP):
        rows = slice(g * QBLOCK, (g + 1) * QBLOCK)
        probs = jnp.exp(nt(queries[g], keys) + bias_ref[...] - lses[:, g : g + 1])
        weighted = probs * nt(d_outs[g], values)
        d_scores = low(weighted - probs * jnp.sum(weighted, axis=1, keepdims=True))
        probs_ref[rows, :] = low(probs)
        dscores_ref[rows, :] = d_scores
        d_queries.append(low(nn(d_scores, keys) * SCALE))
    dq_ref[...] = jnp.concatenate(d_queries, 1)
    d_keys = tn(dscores_ref[...], jnp.concatenate(queries, 0))
    d_values = tn(probs_ref[...], jnp.concatenate(d_outs, 0))
    dkv_ref[here, :] += jnp.concatenate([d_keys, d_values], 1)


def attention_call(kernel, ins, outs, scratch, micros):
    kinds = {
        "first": pl.BlockSpec(memory_space=pltpu.SMEM),
        "heads": pl.BlockSpec((QBLOCK, QW), lambda i: (i, 0)),
        "keys": pl.BlockSpec((WINDOW + TOK, 128), lambda i: (0, 0)),
        "lse": pl.BlockSpec((QBLOCK, 128), lambda i: (i, 0)),
    }
    shapes = {"heads": ((TOK, QW), BF16), "keys": ((WINDOW + TOK, 128), F32), "lse": ((TOK, 128), F32)}
    return pl.pallas_call(
        kernel,
        grid=(TOK // QBLOCK,),
        in_specs=[kinds[kind] for kind in ins],
        out_specs=[kinds[kind] for kind in outs],
        out_shape=[jax.ShapeDtypeStruct(*shapes[kind]) for kind in outs],
        scratch_shapes=[pltpu.VMEM((QBLOCK, SEEN), F32)] + [pltpu.VMEM((GROUP * QBLOCK, SEEN), BF16)] * scratch,
        compiler_params=pltpu.CompilerParams(
            dimension_semantics=("arbitrary",), vmem_limit_bytes=28 * 1024 * 1024
        ),
        cost_estimate=cost(micros),
    )


def first_key(line):
    return (WINDOW - line * TOK).reshape(1).astype(jnp.int32)


def attention_forward(query, keyval, line):
    call = attention_call(attend_kernel, ("first", "heads", "keys"), ("heads", "lse"), 0, 9)
    return call(first_key(line), query, keyval)


def attention_backward(query, keyval, lse, d_out, line):
    ins = ("first", "heads", "keys", "heads", "lse")
    call = attention_call(attend_back_kernel, ins, ("heads", "keys"), 2, 14)
    return call(first_key(line), query, keyval, d_out, lse)


def by_group(pieces):
    rows, _, cols = pieces.shape
    pieces = jnp.pad(pieces, ((0, 0), (0, 2 * RING - KV_HEADS), (0, 0)))
    pieces = pieces.reshape(rows, RING, 2, cols)
    mine = lax.dynamic_index_in_dim(pieces, lax.axis_index("wt"), 2, False)
    return jnp.swapaxes(mine, 0, 1)


def gather_lines(block):
    return lax.all_gather(block, YX, axis=0, tiled=True)


def reduce_lines(grads):
    return lax.psum_scatter(grads, YX, scatter_dimension=0, tiled=True)


TURNED = ROWS_PAD * (LINES - 1) + 128


def turn_features(x_ref, out_ref, first):
    for tile in range(DP // 128):
        cols = slice(128 * tile, 128 * tile + 128)
        out_ref[cols, first : first + TOK] = x_ref[:, cols].T.astype(F32)
    out_ref[DP:, first : first + TOK] = jnp.zeros((TURNED - DP, TOK), F32)


def two_blocks(turned_ref, pair):
    starts = [pl.multiple_of(ROWS_PAD * (2 * pair + k), 8) for k in range(2)]
    return jnp.concatenate([low(turned_ref[pl.ds(start, 128), :]) for start in starts], 0)


def ff_grads_kernel(x2_ref, cot_ref, d_gu_ref, act_ref, done_ref, out_ref, turned_ref):
    part = pl.program_id(0)

    def fill(right_ref):
        @pl.loop(0, LINES // 2)
        def _(pair):
            rows = pl.ds(pl.multiple_of(256 * pair, 256), 256)
            out_ref[rows, :] = low(nn(two_blocks(turned_ref, pair), right_ref[...]))

    @pl.when(part == 0)
    def _():
        turn_features(x2_ref, turned_ref, 0)

    @pl.when(part < 2)
    def _():
        fill(d_gu_ref)

    @pl.when(part == 2)
    def _():
        turn_features(cot_ref, turned_ref, 0)
        fill(act_ref)


def ff_grads(x2, cot, d_gate_up, act, done):
    def whole(cols):
        return pl.BlockSpec((TOK, cols), lambda i: (0, 0))

    return pl.pallas_call(
        ff_grads_kernel,
        grid=(3,),
        in_specs=[
            whole(DP),
            whole(DP),
            pl.BlockSpec((TOK, FF_PAD), lambda i: (0, jnp.minimum(i, 1))),
            whole(FF_PAD),
            pl.BlockSpec(memory_space=pl.ANY),
        ],
        out_specs=pl.BlockSpec((LINES * 128, FF_PAD), lambda i: (0, i)),
        out_shape=pltpu.HBM((LINES * 128, 3 * FF_PAD), BF16),
        scratch_shapes=[pltpu.VMEM((TURNED, TOK), F32)],
        compiler_params=pltpu.CompilerParams(
            dimension_semantics=("arbitrary",), vmem_limit_bytes=36 * 1024 * 1024
        ),
        cost_estimate=cost(11),
    )(x2, cot, d_gate_up, act, done)


LATE = DP + 512
PARTS = (0, 2 * DP, 2 * DP + RING * ATT_COLS, 2 * DP + RING * ATT_COLS + LATE)


def put(source_ref, out_ref, part, sem):
    copy = pltpu.make_async_copy(source_ref, out_ref.at[:, PARTS[part] : PARTS[part + 1]], sem)
    copy.start()
    copy.wait()


def channel_grads_kernel(x1_ref, d_mixer_ref, d_gate_ref, act_ref, out_ref, left_ref, got_ref, sem):
    def channels(source_ref, right_ref, cols):
        left_ref[...] = source_ref[...].T

        @pl.loop(0, CH // 256)
        def _(part):
            rows = pl.ds(pl.multiple_of(256 * part, 256), 256)
            got_ref[rows, cols] = low(nn(left_ref[rows, :], right_ref[...]))

    channels(d_gate_ref, x1_ref, slice(0, DP))
    channels(act_ref, d_mixer_ref, slice(DP, 2 * DP))
    put(got_ref, out_ref, 0, sem)


def attention_grads_kernel(x1_ref, d_attn_ref, right_ref, grads_ref, out_ref, turned_ref, got_ref, sem):
    turn_features(x1_ref, turned_ref, 0)
    turn_features(d_attn_ref, turned_ref, TOK)

    @pl.loop(0, LINES // 2)
    def _(pair):
        got = low(nn(two_blocks(turned_ref, pair), right_ref[...]))
        for block in range(2):
            rows = pl.ds(pl.multiple_of((2 * pair + block) * CH_PAD, CH_PAD), CH_PAD)
            for q in range(RING):
                first = 128 * block + CH_PAD * q
                got_ref[rows, ATT_COLS * q : ATT_COLS * (q + 1)] = got[first : first + CH_PAD, :]

    put(got_ref, out_ref, 1, sem)


def late_grads_kernel(late_ref, grads_ref, out_ref, sem):
    put(late_ref, out_ref, 2, sem)


def grads_call(kernel, arrays, grads, scratch, micros):
    whole, far = pl.BlockSpec(memory_space=pltpu.VMEM), pl.BlockSpec(memory_space=pltpu.HBM)
    given = [] if grads is None else [grads]
    return pl.pallas_call(
        kernel,
        in_specs=[whole] * len(arrays) + [far] * len(given),
        out_specs=far,
        out_shape=pltpu.HBM((CH, PARTS[3]), BF16),
        input_output_aliases={len(arrays): 0} if given else {},
        scratch_shapes=scratch + [pltpu.SemaphoreType.DMA(())],
        compiler_params=pltpu.CompilerParams(vmem_limit_bytes=36 * 1024 * 1024),
        cost_estimate=cost(micros),
    )(*arrays, *given)


def channel_grads(x1, d_mixer, d_gate, act):
    scratch = [pltpu.VMEM((CH, TOK), BF16), pltpu.VMEM((CH, 2 * DP), BF16)]
    return grads_call(channel_grads_kernel, (x1, d_mixer, d_gate, act), None, scratch, 5)


def attention_grads(x1, d_attn, d_qkv, attended, grads):
    right = [jnp.pad(d_qkv, ((0, 0), (0, QW))), jnp.pad(attended, ((0, 0), (ATT_COLS - QW, 0)))]
    scratch = [pltpu.VMEM((TURNED, 2 * TOK), F32), pltpu.VMEM((CH, RING * ATT_COLS), BF16)]
    return grads_call(attention_grads_kernel, (x1, d_attn, jnp.concatenate(right, 0)), grads, scratch, 8)


def late_grads(late, grads):
    return grads_call(late_grads_kernel, (late,), grads, [], 2)


def nothing_kernel(value_ref, done_ref, out_ref):
    pass


def tie(value, done):
    anywhere = pl.BlockSpec(memory_space=pl.ANY)
    return pl.pallas_call(
        nothing_kernel,
        in_specs=[anywhere, anywhere],
        out_specs=anywhere,
        out_shape=jax.ShapeDtypeStruct(value.shape, value.dtype),
        input_output_aliases={0: 0},
        compiler_params=pltpu.CompilerParams(vmem_limit_bytes=8 * 1024 * 1024),
        cost_estimate=cost(0),
    )(value, done)


def corner(value):
    return value[:8, :128]


def per_device(
    block_in, in_gain, w_query, w_keyval, w_out, attn_gain, ssm_gain, inner_weight, conv_weight, conv_bias,
    w_xproj, w_delta, delta_bias, log_decay, skip_gain, w_ssmout, mlp_gain, w_gateup, w_down, cotangent,
):
    core = lax.axis_index("wt")
    depth = lax.axis_index("z")
    line = lax.axis_index("y") * RING + lax.axis_index("x")

    inner_rows = jnp.transpose(inner_weight, (2, 1, 0))
    small = jnp.concatenate(
        [conv_weight.T, conv_bias[:, None], delta_bias[:, None], skip_gain[:, None], log_decay.T], 1
    )
    channel = jnp.concatenate(
        [
            pad_features(inner_rows).reshape(PIECE, 2 * DP),
            jnp.pad(w_xproj[:, :DTR], ((0, 0), (0, RANK_PAD - DTR))),
            jnp.pad(w_xproj[:, DTR:], ((0, 0), (0, 256 - XROWS))),
            jnp.pad(w_delta.T, ((0, 0), (0, 128 - DTR))),
            jnp.pad(small, ((0, 0), (0, SMALL - SMALL_USED))),
        ],
        1,
    )
    channel = jnp.pad(channel, ((0, CH_PAD - PIECE), (0, 0)))

    own_in = lax.dynamic_slice_in_dim(pad_features(block_in), core * SPAN, SPAN, 0)
    own_cot = lax.dynamic_slice_in_dim(pad_features(cotangent), core * SPAN, SPAN, 0)
    gains = jnp.pad(jnp.stack([in_gain, attn_gain, ssm_gain, mlp_gain]), ((0, 12), (0, 128 - PIECE)))
    gains = in_order(around(tie(gains, corner(channel)), "z"), "z")[:, :4, :PIECE]
    gains = jnp.swapaxes(gains, 0, 1).reshape(4, ROWS)
    gains = jnp.pad(gains, ((0, 12), (0, 128 - ROWS)))
    gains_rows = in_order(around(in_order(around(gains, "x"), "x"), "y"), "y")
    gains = gains_rows.reshape(LINES, 16, 128)[:, :4, :ROWS].astype(F32)
    gains = jnp.pad(jnp.swapaxes(gains, 0, 1), ((0, 0), (0, 0), (0, ROWS_PAD - ROWS))).reshape(4, DP)
    in_g, attn_g, ssm_g, mlp_g = (gains[k : k + 1] for k in range(4))
    mine = in_order(around(own_in, "z"), "z")
    line_in = merge_cores(mine)
    own_in = own_in.astype(F32)
    x1 = low(rms(line_in.astype(F32), in_g))

    attn_piece = jnp.concatenate(
        [
            by_group(w_query.reshape(PIECE, KV_HEADS, QW)),
            by_group(w_keyval[:, 0].reshape(PIECE, KV_HEADS, HEAD)),
            by_group(w_keyval[:, 1].reshape(PIECE, KV_HEADS, HEAD)),
            by_group(w_out.T.reshape(PIECE, KV_HEADS, QW)),
        ],
        2,
    )
    ff_piece = jnp.concatenate([w_gateup, w_down.T[:, None]], 1).reshape(PIECE, 3, RING, FF_PIECE)
    ff_piece = jnp.pad(ff_piece, ((0, 0), (0, 0), (0, 0), (0, FF_PAD - FF_PIECE)))
    ff_piece = jnp.transpose(ff_piece, (2, 0, 1, 3)).reshape(RING, PIECE, 3 * FF_PAD)
    parts = jnp.pad(jnp.concatenate([attn_piece, ff_piece], 2), ((0, 0), (0, CH_PAD - PIECE), (0, 0)))
    halves = jnp.concatenate([own_cot[:CH_PAD], own_cot[CH_PAD:]], 1)
    parts = jnp.concatenate([parts, jnp.broadcast_to(halves, (RING,) + halves.shape)], 2)
    parts = sent_along(tie(parts, mine), "z")
    cols = ATT_COLS + 3 * FF_PAD

    def plan(ins, outs):
        pairs = []
        for k, part in enumerate(ins[:RING]):
            pairs.append((part.at[:, :cols], outs[0].at[spot("z", k)]))
            for half in range(2):
                source = part.at[:, cols + DP * half : cols + DP * (half + 1)]
                pairs.append((source, outs[1].at[spot("z", k), CH_PAD * half : CH_PAD * (half + 1)]))
        return pairs

    piece, mine_cot = copy_call(plan, 3 * RING, parts + [gains_rows], [(RING, CH_PAD, cols), (RING, SPAN, DP)])
    line_cot = merge_cores(mine_cot)
    piece = piece[:, :PIECE].reshape(ROWS, cols)
    piece = jnp.pad(piece, ((0, ROWS_PAD - ROWS), (0, 0)))
    attn_piece, ff_piece = piece[:, :ATT_COLS], piece[:, ATT_COLS:]
    out_piece = jnp.pad(pad_features(w_ssmout), ((0, CH_PAD - PIECE), (0, 0))).reshape(4, 8, DP // 128, 128)
    out_piece = jnp.transpose(out_piece, (2, 1, 0, 3)).reshape(ROWS_PAD, 512)
    attn_piece = jnp.concatenate([attn_piece, out_piece], 1)

    with jax.named_scope("gather_channels"):
        channel = gather_lines(channel)
    with jax.named_scope("gather_attention"):
        w_attn = gather_lines(attn_piece)
    with jax.named_scope("gather_ff"):
        w_ff = gather_lines(ff_piece)
    w_so = w_attn[:, ATT_COLS:].reshape(LINES, DP // 128, 8, 4, 128)
    w_so = jnp.transpose(w_so, (0, 3, 2, 1, 4)).reshape(CH, DP)

    w_conv, w_gate = channel[:, :DP], channel[:, COLS[1] : COLS[2]]
    w_x = channel[:, COLS[2] : COLS[2] + XROWS]
    w_d = channel[:, COLS[3] : COLS[3] + DTR]
    small = channel[:, COLS[4] : COLS[5]].astype(F32)
    small_rows = small[:, :32].T
    taps, c_bias, d_bias, skip = small_rows[:CONV], small_rows[4:5], small_rows[5:6], small_rows[6:7]
    rate2 = -jnp.exp(small_rows[7 : 7 + STATE]) * LOG2E
    conv_in = low(nt(x1, w_conv))
    gate_z = low(nt(x1, w_gate)).astype(F32)
    edge = line_shift(conv_in[TOK - (CONV - 1) :], 1)
    padded_in = jnp.concatenate([edge, conv_in], 0).astype(F32)
    conv_out = c_bias
    for tap in range(CONV):
        conv_out = conv_out + taps[tap : tap + 1] * padded_in[tap : tap + TOK]
    mixer_low = low(jax.nn.silu(conv_out))
    mixer_in = mixer_low.astype(F32)
    xproj, _ = sum_line(dot(w_x, mixer_low, ((0,), (1,))))
    step_low = low(xproj[:DTR])
    in_mix, out_mix = spread(xproj[RANK_PAD : RANK_PAD + STATE]), spread(xproj[RANK_PAD + STATE :])
    step_pre = dot(step_low, w_d, ((0,), (1,))) + d_bias
    step = jax.nn.softplus(step_pre)
    ends, spans, pay = scan_ends(step, mixer_in, in_mix, rate2)
    before, rows = state_along_x(rate2, pay, False)

    qkv = low(nn(x1, w_attn[:, : QW + 2 * HEAD]))
    enter, _ = state_along_y(rate2, before, rows, False)
    query, keyval = qkv[:, :QW], qkv[:, QW:]
    keyval = jnp.concatenate([line_shift(keyval, 2), line_shift(keyval, 1), keyval], 0)
    attended, lse = attention_forward(query, keyval, line)
    w_o = w_attn[:, QW + 2 * HEAD : ATT_COLS]
    attn_part = low(nt(attended, w_o))

    ssm_y = scan_outputs(step, mixer_in, in_mix, out_mix, rate2, ends, spans, enter) + skip * mixer_in
    silu_z = jax.nn.silu(gate_z)
    mixer_act = low(ssm_y * silu_z)
    branches, _ = scatter_tokens(jnp.concatenate([attn_part, low(nn(mixer_act, w_so))], 1))
    attn_out, mixer_out = branches[:, :DP], branches[:, DP:]

    hidden = own_in + 0.5 * (rms(attn_out, attn_g) + rms(mixer_out, ssm_g))
    x2 = gather_tokens(low(rms(hidden, mlp_g)))
    w_gu, w_dn = w_ff[:, : 2 * FF_PAD], w_ff[:, 2 * FF_PAD :]
    gate_up = low(nn(x2, w_gu)).astype(F32)
    gate, upper = gate_up[:, :FF_PAD], gate_up[:, FF_PAD:]
    silu_gate = jax.nn.silu(gate)
    mlp_act = low(silu_gate * upper)
    d_act = nn(line_cot, w_dn)
    d_gate_up = low(jnp.concatenate([d_act * upper * silu_grad(gate), d_act * silu_gate], 1))
    d_x2 = add_cores(low(nt(d_gate_up, w_gu)))
    d_x2, arrived = add_ring(d_x2)
    grad_ff = ff_grads(x2, line_cot, d_gate_up, mlp_act, arrived)
    with jax.named_scope("reduce_ff"):
        grad_ff = reduce_lines(grad_ff)

    d_norm, d_mlp_g = rms_back(hidden, mlp_g, d_x2)
    d_hidden = own_cot.astype(F32) + d_norm
    d_attn, d_attn_g = rms_back(attn_out, attn_g, 0.5 * d_hidden)
    d_mixer, d_ssm_g = rms_back(mixer_out, ssm_g, 0.5 * d_hidden)
    blocks = around(low(d_mixer), "z")
    d_mixer = merge_cores(in_order(blocks, "z"))
    blocks = around(tie(low(d_attn), blocks[2]), "z")
    d_attn = merge_cores(in_order(blocks, "z"))

    d_mact = nt(d_mixer, w_so)
    dy = d_mact * silu_z
    d_gate_low = low(d_mact * ssm_y * silu_grad(gate_z))
    heads, pay = scan_heads(step, dy, out_mix, tie(rate2, blocks[1]), spans)
    before, rows = state_along_x(rate2, pay, True)
    enter_back, _ = state_along_y(rate2, before, rows, True)

    d_step, lam_b, grad_decay, d_mixes = scan_backward(
        step, mixer_in, dy, in_mix, out_mix, rate2, ends, spans, enter, heads, enter_back
    )
    d_step_pre = (d_step + lam_b * mixer_in) * jax.nn.sigmoid(step_pre)
    d_step_low = low(d_step_pre)
    grad_d = tn(d_step_low, step_low.T)
    d_rank = dot(w_d, d_step_low, ((0,), (1,)))
    d_xproj = jnp.concatenate([jnp.pad(d_rank, ((0, RANK_PAD - DTR), (0, 0))), d_mixes[:, : 2 * STATE].T], 0)
    d_xproj, arrived = sum_line(d_xproj)
    d_xproj = low(d_xproj)
    d_attended = low(nn(d_attn, w_o))
    d_query, d_keyval = attention_backward(query, keyval, tie(lse, arrived), d_attended, line)
    d_keyval = (
        d_keyval[2 * TOK :]
        + line_shift(low(d_keyval[TOK : 2 * TOK]), -1).astype(F32)
        + line_shift(low(d_keyval[:TOK]), -2).astype(F32)
    )
    d_qkv = jnp.concatenate([d_query, low(d_keyval)], 1)
    grads = channel_grads(x1, d_mixer, d_gate_low, mixer_act)
    grads = attention_grads(x1, d_attn, d_qkv, attended, grads)

    grad_x = dot(mixer_low, d_xproj, ((0,), (1,)))
    d_mixer_in = dy * skip + step * lam_b + dot(d_xproj, w_x, ((0,), (1,)))
    d_conv_out = d_mixer_in * silu_grad(conv_out)
    d_after = jnp.concatenate([d_conv_out, line_shift(d_conv_out[: CONV - 1], -1)], 0)
    d_conv_in = sum(taps[k : k + 1] * d_after[CONV - 1 - k : CONV - 1 - k + TOK] for k in range(CONV))
    small_grads = jnp.stack(
        [jnp.sum(d_conv_out * padded_in[tap : tap + TOK], axis=0) for tap in range(CONV)]
        + [jnp.sum(d_conv_out, axis=0), jnp.sum(d_step_pre, axis=0), jnp.sum(dy * mixer_in, axis=0)],
        0,
    )
    small_grads = jnp.concatenate([small_grads, grad_decay], 0).T
    d_conv_low = low(d_conv_in)
    grad_conv = low(tn(d_conv_low, x1))

    d_x1 = nt(d_qkv, w_attn[:, : QW + 2 * HEAD]) + nn(d_conv_low, w_conv) + nn(d_gate_low, w_gate)
    small_grads = jnp.pad(small_grads, ((0, 0), (0, SMALL - SMALL_USED)))
    grad_late = jnp.concatenate(
        [
            grad_conv,
            low(jnp.pad(grad_x, ((0, 0), (0, 256 - XROWS)))),
            low(jnp.pad(grad_d, ((0, 0), (0, 128 - DTR)))),
            low(small_grads),
        ],
        1,
    )
    with jax.named_scope("reduce_rest"):
        grads = reduce_lines(late_grads(grad_late, grads))
    grad_early, grad_late = grads[:, : 2 * DP], grads[:, PARTS[2] :].astype(F32)
    grad_attn = jnp.swapaxes(grads[:, PARTS[1] : PARTS[2]].reshape(CH_PAD, RING, ATT_COLS), 0, 1)
    grad_attn = grad_attn.reshape(RING * CH_PAD, ATT_COLS)
    d_x1, _ = scatter_tokens(low(d_x1))
    d_norm, d_in_g = rms_back(own_in, in_g, d_x1)
    grad_in = d_hidden + d_norm
    mlp_out, _ = scatter_tokens(low(nt(tie(mlp_act, d_conv_low), w_dn)))
    block_out = low(hidden + mlp_out)

    first = core == 0

    def both_cores(own):
        other = swap_core(own)
        return jnp.concatenate([jnp.where(first, own, other), jnp.where(first, other, own)], 0)

    block_out = drop_features(both_cores(block_out))
    grad_in = drop_features(both_cores(grad_in))

    def to_owner(grads):
        return exchange(low(grads[:ROWS]).reshape(RING, PIECE, grads.shape[1]), "z").astype(F32)

    grad_ff = to_owner(grad_ff).reshape(RING, PIECE, 3, FF_PAD)[..., :FF_PIECE]
    grad_ff = jnp.transpose(grad_ff, (1, 2, 0, 3)).reshape(PIECE, 3, RING * FF_PIECE)
    grad_gateup, grad_down = grad_ff[:, :2], grad_ff[:, 2].T

    grad_attn = to_owner(grad_attn)
    other = swap_core(grad_attn)
    grad_attn = jnp.stack([jnp.where(first, grad_attn, other), jnp.where(first, other, grad_attn)], 1)
    grad_attn = jnp.transpose(grad_attn, (2, 0, 1, 3)).reshape(PIECE, 2 * RING, ATT_COLS)[:, :KV_HEADS]
    grad_query = grad_attn[..., :QW].reshape(PIECE, HEADS * HEAD)
    grad_keyval = grad_attn[..., QW : QW + 2 * HEAD].reshape(PIECE, KV_HEADS, 2, HEAD)
    grad_keyval = jnp.swapaxes(grad_keyval, 1, 2).reshape(PIECE, 2, KV_HEADS * HEAD)
    grad_out = grad_attn[..., QW + 2 * HEAD :].reshape(PIECE, HEADS * HEAD).T

    grad_early, grad_late = grad_early[:PIECE, : 2 * DP].astype(F32), grad_late[:PIECE]
    grad_inner = jnp.stack([grad_late[:, :DP], grad_early[:, :DP]], 1)
    grad_inner = jnp.transpose(drop_features(grad_inner), (2, 1, 0))
    grad_ssmout = drop_features(grad_early[:, DP : 2 * DP])
    grad_xproj = grad_late[:, DP : DP + XROWS]
    grad_xproj = jnp.concatenate([grad_xproj[:, :DTR], grad_xproj[:, RANK_PAD:]], 1)
    grad_delta = grad_late[:, DP + 256 : DP + 256 + DTR].T
    small_grads = grad_late[:, DP + 384 : DP + 384 + SMALL_USED].T

    gain_grads = jnp.pad(jnp.stack([d_in_g, d_attn_g, d_ssm_g, d_mlp_g]), ((0, 4), (0, 0)))
    gain_grads = gain_grads + swap_core(gain_grads)
    for axis in SEQ:
        gain_grads = sum(around(gain_grads, axis))
    gain_grads = lax.dynamic_slice_in_dim(gain_grads, line * ROWS_PAD + depth * PIECE, PIECE, 1)

    return (
        block_out, grad_in, gain_grads[0], grad_query, grad_keyval, grad_out, gain_grads[1], gain_grads[2],
        grad_inner, small_grads[:CONV], small_grads[4], grad_xproj, grad_delta, small_grads[5],
        small_grads[7 : 7 + STATE], small_grads[6], grad_ssmout, gain_grads[3], grad_gateup, grad_down,
    )


def solution(mesh):
    fine = Mesh(mesh.devices.reshape(RING, RING, RING, 2), ("y", "x", "z", "wt"))
    both = SEQ + ("wt",)
    weights = (
        P(SEQ),
        P(SEQ, None),
        P(SEQ, None, None),
        P(None, SEQ),
        P(SEQ),
        P(SEQ),
        P(None, None, both),
        P(None, both),
        P(both),
        P(both, None),
        P(None, both),
        P(both),
        P(None, both),
        P(both),
        P(both, None),
        P(SEQ),
        P(SEQ, None, "wt"),
        P("wt", SEQ),
    )
    rows = P(SEQ, None)
    return jax.shard_map(
        per_device, mesh=fine, in_specs=(rows,) + weights + (rows,), out_specs=(rows, rows) + weights, check_vma=False
    )
```

```python
import functools
import math

import jax
import jax.numpy as jnp
from jax import lax
from jax.experimental import pallas as pl
from jax.experimental.pallas import tpu as pltpu
from jax.sharding import Mesh
from jax.sharding import PartitionSpec as P

F32 = jnp.float32
BF16 = jnp.bfloat16

HEADS = 25
KV_HEADS = 5
GROUP = HEADS // KV_HEADS
HEAD = 64
STATE = 16
DTR = 100
CONV = 4
WINDOW = 1024
D = 1600
QW = GROUP * HEAD
EPS = 1e-06
LOG2E = math.log2(math.e)

YX = ("y", "x")
SEQ = ("y", "x", "z")
RING = 4
LINES = 16
PIECE = 25
ROWS = RING * PIECE
ROWS_PAD = 104
DP = LINES * ROWS_PAD
CH_PAD = 32
CH = LINES * CH_PAD
SPAN = 64
CHUNKS = 8
TOK = SPAN * CHUNKS
FF_PIECE = 688
FF_PAD = 768
ATT_COLS = 768
RANK_PAD = 104
XROWS = RANK_PAD + 2 * STATE
PAY = STATE + 8
SMALL = 128
SMALL_USED = CONV + 3 + STATE
COLS = (0, DP, 2 * DP, 2 * DP + 256, 2 * DP + 384, 2 * DP + 512)


def dot(left, right, dims):
    return lax.dot_general(left, right, (dims, ((), ())), preferred_element_type=F32)


def nn(left, right):
    return dot(left, right, ((1,), (0,)))


def nt(left, right):
    return dot(left, right, ((1,), (1,)))


def tn(left, right):
    return dot(left, right, ((0,), (0,)))


def low(value):
    return value.astype(BF16)


def pad_features(value):
    lead = value.shape[:-1]
    value = value.reshape(lead + (LINES, ROWS))
    value = jnp.pad(value, [(0, 0)] * (len(lead) + 1) + [(0, ROWS_PAD - ROWS)])
    return value.reshape(lead + (DP,))


def drop_features(value):
    lead = value.shape[:-1]
    return value.reshape(lead + (LINES, ROWS_PAD))[..., :ROWS].reshape(lead + (D,))


def step_to(axis, distance):
    return [(i, (i + distance) % RING) for i in range(RING)]


def around(value, axis):
    return [value] + [lax.ppermute(value, axis, step_to(axis, RING - d)) for d in range(1, RING)]


def copy_kernel(plan, count, *refs):
    ins, outs, sems = refs[:count], refs[count:-1], refs[-1]
    copies = [pltpu.make_async_copy(src, dst, sems.at[k]) for k, (src, dst) in enumerate(plan(ins, outs))]
    for copy in copies:
        copy.start()
    for copy in copies:
        copy.wait()


def copy_call(plan, number, arrays, shapes, near=False):
    anywhere = pl.BlockSpec(memory_space=pl.ANY)
    return pl.pallas_call(
        functools.partial(copy_kernel, plan, len(arrays)),
        in_specs=[pl.BlockSpec(memory_space=pltpu.HBM)] * len(arrays),
        out_specs=[pl.BlockSpec(memory_space=pltpu.VMEM) if near else anywhere] * len(shapes),
        out_shape=[
            pltpu.VMEM(shape, arrays[0].dtype) if near else jax.ShapeDtypeStruct(shape, arrays[0].dtype)
            for shape in shapes
        ],
        scratch_shapes=[pltpu.SemaphoreType.DMA((number,))],
        compiler_params=pltpu.CompilerParams(vmem_limit_bytes=8 * 1024 * 1024),
        cost_estimate=cost(1),
    )(*arrays)


def spot(axis, k):
    return lax.rem(lax.axis_index(axis) + k, RING)


def in_order(blocks, axis):
    def plan(ins, outs):
        return [(block, outs[0].at[spot(axis, k)]) for k, block in enumerate(ins)]

    return copy_call(plan, RING, blocks, [(RING,) + blocks[0].shape])[0]


def swap_core(value):
    return lax.ppermute(value, "wt", [(0, 1), (1, 0)])


def sent_along(pieces, axis):
    here = lax.axis_index(axis)
    got = [lax.dynamic_index_in_dim(pieces, here, 0, False)]
    for d in range(1, RING):
        piece = lax.dynamic_index_in_dim(pieces, (here + RING - d) % RING, 0, False)
        got.append(lax.ppermute(piece, axis, step_to(axis, RING - d)))
    return got


def exchange(pieces, axis):
    return in_order(sent_along(pieces, axis), axis)


def gather_tokens(own):
    return merge_cores(in_order(around(own, "z"), "z"))


def merge_cores(mine):
    wide, rows = mine.shape[2], pl.ds(0, SPAN)

    def plan(ins, outs):
        core = lax.axis_index("wt")
        return [(part.at[:, rows], outs[0].at[:, place]) for place, part in ((core, ins[0]), (1 - core, ins[1]))]

    return copy_call(plan, 2, [mine, swap_core(mine)], [(RING, 2, SPAN, wide)], True)[0].reshape(TOK, wide)


def add_cores(partial):
    core = lax.axis_index("wt")
    parts = partial.reshape(RING, 2, SPAN, partial.shape[1])
    mine = lax.dynamic_index_in_dim(parts, core, 1, False)
    theirs = lax.dynamic_index_in_dim(parts, 1 - core, 1, False)
    return mine.astype(F32) + swap_core(theirs).astype(F32)


def add_ring(mine):
    here = lax.axis_index("z")
    total, parts = lax.dynamic_index_in_dim(mine, here, 0, False), []
    for d in range(1, RING):
        piece = lax.dynamic_index_in_dim(mine, (here + d) % RING, 0, False)
        parts.append(lax.ppermute(low(piece), "z", step_to("z", d)))
        total = total + parts[-1].astype(F32)
    return total, parts[0]


def scatter_tokens(partial):
    return add_ring(add_cores(partial))


def sum_line(value):
    value = value + swap_core(value)
    parts = around(low(value), "z")
    return value + (parts[1].astype(F32) + parts[2].astype(F32) + parts[3].astype(F32)), parts[1]


def line_shift(value, distance):
    route = [(i, i + distance) for i in range(LINES) if 0 <= i + distance < LINES]
    return lax.ppermute(value, YX, route)


def rms(value, gain):
    scale = lax.rsqrt(jnp.sum(value * value, axis=-1, keepdims=True) / D + EPS)
    return value * scale * gain


def rms_back(value, gain, dy):
    r = lax.rsqrt(jnp.sum(value * value, axis=-1, keepdims=True) / D + EPS)
    inner = jnp.sum(value * gain * dy, axis=-1, keepdims=True) / D
    return r * gain * dy - value * (r * r * r) * inner, jnp.sum(value * r * dy, axis=0)


def silu_grad(value):
    sig = jax.nn.sigmoid(value)
    return sig * (1.0 + value * (1.0 - sig))


def rows_at(ref, tau):
    return ref[pl.ds(tau, CHUNKS, stride=SPAN), :]


def spread(rows):
    rows = jnp.transpose(rows.reshape(STATE, CHUNKS, SPAN), (2, 0, 1))
    return jnp.broadcast_to(rows[..., None], (SPAN, STATE, CHUNKS, 128))


def rate_rows(rate_ref):
    return [jnp.broadcast_to(rate_ref[n : n + 1, :], (CHUNKS, 128)) for n in range(STATE)]


def zeros():
    return jnp.zeros((CHUNKS, 128), F32)


def walk(start, ends_ref, spans_ref, rate_ref, starts_ref=None, backward=False):
    state, order = start, range(CHUNKS)
    for chunk in reversed(order) if backward else order:
        rows = pl.ds(chunk, STATE, stride=CHUNKS)
        if starts_ref is not None:
            starts_ref[rows, :] = state
        state = jnp.exp2(rate_ref[...] * spans_ref[chunk : chunk + 1, :]) * state + ends_ref[rows, :]
    return state


def chunk_rows(n):
    return slice(CHUNKS * n, CHUNKS * n + CHUNKS)


def report(pay_ref, state, spans_ref):
    pay_ref[:STATE, :] = state
    total = jnp.sum(spans_ref[...], axis=0, keepdims=True)
    pay_ref[STATE:, :] = jnp.broadcast_to(total, (PAY - STATE, 128))


def ends_kernel(step_ref, in_ref, b_ref, rate_ref, end_ref, span_ref, pay_ref):
    rates = rate_rows(rate_ref)

    def token(tau, carry):
        states, total = carry
        step = rows_at(step_ref, tau)
        push = step * rows_at(in_ref, tau)
        states = [jnp.exp2(step * rates[n]) * states[n] + push * b_ref[tau, n] for n in range(STATE)]
        return states, total + step

    states, total = lax.fori_loop(0, SPAN, token, ([zeros()] * STATE, zeros()), unroll=8)
    for n in range(STATE):
        end_ref[chunk_rows(n), :] = states[n]
    span_ref[...] = total
    report(pay_ref, walk(jnp.zeros((STATE, 128), F32), end_ref, span_ref, rate_ref), span_ref)


def outputs_kernel(step_ref, in_ref, b_ref, c_ref, rate_ref, end_ref, span_ref, enter_ref, y_ref, init_ref):
    rates = rate_rows(rate_ref)
    walk(enter_ref[...], end_ref, span_ref, rate_ref, init_ref)

    def token(tau, states):
        step = rows_at(step_ref, tau)
        push = step * rows_at(in_ref, tau)
        states = [jnp.exp2(step * rates[n]) * states[n] + push * b_ref[tau, n] for n in range(STATE)]
        y_ref[pl.ds(tau, CHUNKS, stride=SPAN), :] = sum(c_ref[tau, n] * states[n] for n in range(STATE))
        return states

    lax.fori_loop(0, SPAN, token, [init_ref[chunk_rows(n), :] for n in range(STATE)], unroll=8)


def heads_kernel(step_ref, dy_ref, c_ref, rate_ref, span_ref, head_ref, pay_ref):
    rates = rate_rows(rate_ref)

    def token(back, carry):
        tau = SPAN - 1 - back
        step = rows_at(step_ref, tau)
        dy = rows_at(dy_ref, tau)
        return [jnp.exp2(step * rates[n]) * (c_ref[tau, n] * dy + carry[n]) for n in range(STATE)]

    carry = lax.fori_loop(0, SPAN, token, [zeros()] * STATE, unroll=8)
    for n in range(STATE):
        head_ref[chunk_rows(n), :] = carry[n]
    state = walk(jnp.zeros((STATE, 128), F32), head_ref, span_ref, rate_ref, backward=True)
    report(pay_ref, state, span_ref)


def backward_kernel(
    step_ref, in_ref, dy_ref, b_ref, c_ref, rate_ref, end_ref, span_ref, enter_ref, head_ref, enter_back_ref,
    dstep_ref, lamb_ref, ddecay_ref, dmix_ref,
    a_ref, h_ref, din_ref, dout_ref, init_ref, lam_ref,
):
    rates = rate_rows(rate_ref)

    @pl.when(pl.program_id(0) == 0)
    def _():
        @pl.loop(0, SPAN)
        def _(tau):
            din_ref[tau] = jnp.zeros((STATE, CHUNKS, 128), F32)
            dout_ref[tau] = jnp.zeros((STATE, CHUNKS, 128), F32)

    walk(enter_ref[...], end_ref, span_ref, rate_ref, init_ref)
    walk(enter_back_ref[...], head_ref, span_ref, rate_ref, lam_ref, backward=True)
    for n in range(STATE):
        h_ref[0, n] = init_ref[chunk_rows(n), :]

    def forth(tau, states):
        step = rows_at(step_ref, tau)
        push = step * rows_at(in_ref, tau)
        states = list(states)
        for n in range(STATE):
            decay = jnp.exp2(step * rates[n])
            a_ref[tau, n] = decay
            states[n] = decay * states[n] + push * b_ref[tau, n]
            h_ref[tau + 1, n] = states[n]
        return states

    lax.fori_loop(0, SPAN, forth, [init_ref[chunk_rows(n), :] for n in range(STATE)], unroll=4)

    def back(backwards, carry):
        tau = SPAN - 1 - backwards
        lams, decays = list(carry[0]), list(carry[1])
        step = rows_at(step_ref, tau)
        push = step * rows_at(in_ref, tau)
        dy = rows_at(dy_ref, tau)
        dstep, lamb = zeros(), zeros()
        for n in range(STATE):
            lam = c_ref[tau, n] * dy + lams[n]
            lams[n] = a_ref[tau, n] * lam
            along = lams[n] * h_ref[tau, n]
            dstep = dstep + along * rates[n]
            lamb = lamb + lam * b_ref[tau, n]
            decays[n] = decays[n] + along * step
            din_ref[tau, n] += lam * push
            dout_ref[tau, n] += dy * h_ref[tau + 1, n]
        dstep_ref[pl.ds(tau, CHUNKS, stride=SPAN), :] = dstep * (1.0 / LOG2E)
        lamb_ref[pl.ds(tau, CHUNKS, stride=SPAN), :] = lamb
        return lams, decays

    start = ([lam_ref[chunk_rows(n), :] for n in range(STATE)], [zeros()] * STATE)
    _, decays = lax.fori_loop(0, SPAN, back, start, unroll=4)
    total = jnp.concatenate([jnp.sum(decays[n], axis=0, keepdims=True) for n in range(STATE)], 0)
    ddecay_ref[...] = total * rate_ref[...] * (1.0 / LOG2E)

    @pl.when(pl.program_id(0) == pl.num_programs(0) - 1)
    def _():
        lane = lax.broadcasted_iota(jnp.int32, (CHUNKS, 128), 1)

        def fold(tau, carry):
            rows = zeros()
            for n in range(STATE):
                rows = jnp.where(lane == n, jnp.sum(din_ref[tau, n], axis=1, keepdims=True), rows)
                total = jnp.sum(dout_ref[tau, n], axis=1, keepdims=True)
                rows = jnp.where(lane == STATE + n, total, rows)
            dmix_ref[pl.ds(tau, CHUNKS, stride=SPAN), :] = rows
            return carry

        lax.fori_loop(0, SPAN, fold, 0, unroll=8)


def cost(micros):
    return pl.CostEstimate(flops=int(micros * 1e9), bytes_accessed=int(micros * 3e6), transcendentals=0)


def scan_call(kernel, ins, outs, scratch, micros):
    wide = (SPAN, STATE, CHUNKS, 128)
    once = pl.BlockSpec(wide, lambda i: (0, 0, 0, 0), pipeline_mode=pl.Buffered(1))

    def lanes(rows):
        return (rows, CH), pl.BlockSpec((rows, 128), lambda i: (0, i))

    kinds = {
        "tok": lanes(TOK),
        "mix": ((TOK, 128), pl.BlockSpec((TOK, 128), lambda i: (0, 0))),
        "state": lanes(STATE),
        "states": lanes(STATE * CHUNKS),
        "chunk": lanes(CHUNKS),
        "pay": lanes(PAY),
        "wide": (wide, once),
    }
    return pl.pallas_call(
        kernel,
        grid=(CH // 128,),
        in_specs=[kinds[kind][1] for kind in ins],
        out_specs=[kinds[kind][1] for kind in outs],
        out_shape=[jax.ShapeDtypeStruct(kinds[kind][0], F32) for kind in outs],
        scratch_shapes=[pltpu.VMEM(shape, F32) for shape in scratch],
        compiler_params=pltpu.CompilerParams(
            dimension_semantics=("arbitrary",), vmem_limit_bytes=36 * 1024 * 1024
        ),
        cost_estimate=cost(micros),
    )


WALK = (STATE * CHUNKS, 128)


def scan_ends(*args):
    ins = ("tok", "tok", "wide", "state")
    return scan_call(ends_kernel, ins, ("states", "chunk", "pay"), (), 5)(*args)


def scan_outputs(*args):
    ins = ("tok", "tok", "wide", "wide", "state", "states", "chunk", "state")
    return scan_call(outputs_kernel, ins, ("tok",), (WALK,), 7)(*args)[0]


def scan_heads(*args):
    ins = ("tok", "tok", "wide", "state", "chunk")
    return scan_call(heads_kernel, ins, ("states", "pay"), (), 5)(*args)


def scan_backward(*args):
    ins = ("tok", "tok", "tok", "wide", "wide", "state", "states", "chunk", "state", "states", "state")
    outs = ("tok", "tok", "state", "mix")
    wide = [(SPAN + extra, STATE, CHUNKS, 128) for extra in (0, 1, 0, 0)]
    return scan_call(backward_kernel, ins, outs, wide + [WALK, WALK], 20)(*args)


def nearer(value, axis, backward):
    here = lax.axis_index(axis)
    if backward:
        here = RING - 1 - here
    steps = ((d, lax.ppermute(value, axis, step_to(axis, -d if backward else d))) for d in (3, 2, 1))
    return here, list(steps)


def fold(rate2, blocks, keep):
    state, span = jnp.zeros_like(rate2), jnp.zeros_like(rate2[:1])
    for d, block in blocks:
        block_span = block[STATE : STATE + 1]
        longer = jnp.exp2(rate2 * block_span) * state + block[:STATE]
        state = jnp.where(keep(d), longer, state)
        span = jnp.where(keep(d), span + block_span, span)
    return state, span


def state_along_x(rate2, pay, backward):
    here, blocks = nearer(pay, "x", backward)
    before = fold(rate2, blocks, lambda d: d <= here)
    after, after_span = fold(rate2, blocks, lambda d: d > here)
    own_span = pay[STATE : STATE + 1]
    whole = jnp.exp2(rate2 * own_span) * before[0] + pay[:STATE]
    whole = jnp.exp2(rate2 * after_span) * whole + after
    rows = jnp.concatenate([whole, jnp.broadcast_to(before[1] + own_span + after_span, (PAY - STATE, CH))], 0)
    return before, rows


def state_along_y(rate2, before, rows, backward):
    here, blocks = nearer(rows, "y", backward)
    above, _ = fold(rate2, blocks, lambda d: d <= here)
    return jnp.exp2(rate2 * before[1]) * above + before[0], blocks[-1][1]


QBLOCK = 128
SCALE = HEAD ** (-0.5)
SEEN = WINDOW + QBLOCK


def head_cols(g):
    return slice(HEAD * g, HEAD * g + HEAD)


def fill_bias(first_ref, bias_ref):
    row = lax.broadcasted_iota(jnp.int32, (QBLOCK, SEEN), 0)
    col = lax.broadcasted_iota(jnp.int32, (QBLOCK, SEEN), 1)
    first = first_ref[0] - pl.program_id(0) * QBLOCK
    bias_ref[...] = jnp.where((col > row) & (col <= row + WINDOW) & (col >= first), 0.0, -1e30)


def attend_kernel(first_ref, q_ref, kv_ref, out_ref, lse_ref, bias_ref):
    fill_bias(first_ref, bias_ref)
    keyval = kv_ref[pl.ds(pl.program_id(0) * QBLOCK, SEEN), :]
    keys = keyval[:, :HEAD]
    lane = lax.broadcasted_iota(jnp.int32, (QBLOCK, 128), 1)
    lses = jnp.zeros((QBLOCK, 128), F32)
    outs = []
    for g in range(GROUP):
        scores = nt(q_ref[:, head_cols(g)] * BF16(SCALE), keys) + bias_ref[...]
        peak = jnp.max(scores, axis=1, keepdims=True)
        probs = jnp.exp(scores - peak)
        total = jnp.sum(probs, axis=1, keepdims=True)
        outs.append(low(nn(low(probs), keyval)[:, HEAD:] / total))
        lses = jnp.where(lane == g, peak + jnp.log(total), lses)
    out_ref[...] = jnp.concatenate(outs, 1)
    lse_ref[...] = lses


def attend_back_kernel(
    first_ref, q_ref, kv_ref, dout_ref, lse_ref, dq_ref, dkv_ref, bias_ref, probs_ref, dscores_ref
):
    block = pl.program_id(0)
    fill_bias(first_ref, bias_ref)

    @pl.when(block == 0)
    def _():
        dkv_ref[...] = jnp.zeros(dkv_ref.shape, F32)

    here = pl.ds(block * QBLOCK, SEEN)
    keyval = kv_ref[here, :]
    keys, values = keyval[:, :HEAD], keyval[:, HEAD:]
    lses = lse_ref[...]
    queries = [q_ref[:, head_cols(g)] * BF16(SCALE) for g in range(GROUP)]
    d_outs = [dout_ref[:, head_cols(g)] for g in range(GROUP)]
    d_queries = []
    for g in range(GROUP):
        rows = slice(g * QBLOCK, (g + 1) * QBLOCK)
        probs = jnp.exp(nt(queries[g], keys) + bias_ref[...] - lses[:, g : g + 1])
        weighted = probs * nt(d_outs[g], values)
        d_scores = low(weighted - probs * jnp.sum(weighted, axis=1, keepdims=True))
        probs_ref[rows, :] = low(probs)
        dscores_ref[rows, :] = d_scores
        d_queries.append(low(nn(d_scores, keys) * SCALE))
    dq_ref[...] = jnp.concatenate(d_queries, 1)
    d_keys = tn(dscores_ref[...], jnp.concatenate(queries, 0))
    d_values = tn(probs_ref[...], jnp.concatenate(d_outs, 0))
    dkv_ref[here, :] += jnp.concatenate([d_keys, d_values], 1)


def attention_call(kernel, ins, outs, scratch, micros):
    kinds = {
        "first": pl.BlockSpec(memory_space=pltpu.SMEM),
        "heads": pl.BlockSpec((QBLOCK, QW), lambda i: (i, 0)),
        "keys": pl.BlockSpec((WINDOW + TOK, 128), lambda i: (0, 0)),
        "lse": pl.BlockSpec((QBLOCK, 128), lambda i: (i, 0)),
    }
    shapes = {"heads": ((TOK, QW), BF16), "keys": ((WINDOW + TOK, 128), F32), "lse": ((TOK, 128), F32)}
    return pl.pallas_call(
        kernel,
        grid=(TOK // QBLOCK,),
        in_specs=[kinds[kind] for kind in ins],
        out_specs=[kinds[kind] for kind in outs],
        out_shape=[jax.ShapeDtypeStruct(*shapes[kind]) for kind in outs],
        scratch_shapes=[pltpu.VMEM((QBLOCK, SEEN), F32)] + [pltpu.VMEM((GROUP * QBLOCK, SEEN), BF16)] * scratch,
        compiler_params=pltpu.CompilerParams(
            dimension_semantics=("arbitrary",), vmem_limit_bytes=28 * 1024 * 1024
        ),
        cost_estimate=cost(micros),
    )


def first_key(line):
    return (WINDOW - line * TOK).reshape(1).astype(jnp.int32)


def attention_forward(query, keyval, line):
    call = attention_call(attend_kernel, ("first", "heads", "keys"), ("heads", "lse"), 0, 9)
    return call(first_key(line), query, keyval)


def attention_backward(query, keyval, lse, d_out, line):
    ins = ("first", "heads", "keys", "heads", "lse")
    call = attention_call(attend_back_kernel, ins, ("heads", "keys"), 2, 14)
    return call(first_key(line), query, keyval, d_out, lse)


def by_group(pieces):
    rows, _, cols = pieces.shape
    pieces = jnp.pad(pieces, ((0, 0), (0, 2 * RING - KV_HEADS), (0, 0)))
    pieces = pieces.reshape(rows, RING, 2, cols)
    mine = lax.dynamic_index_in_dim(pieces, lax.axis_index("wt"), 2, False)
    return jnp.swapaxes(mine, 0, 1)


def gather_lines(block):
    return lax.all_gather(block, YX, axis=0, tiled=True)


def reduce_lines(grads):
    return lax.psum_scatter(grads, YX, scatter_dimension=0, tiled=True)


TURNED = ROWS_PAD * (LINES - 1) + 128


def turn_features(x_ref, out_ref, first):
    for tile in range(DP // 128):
        cols = slice(128 * tile, 128 * tile + 128)
        out_ref[cols, first : first + TOK] = x_ref[:, cols].T.astype(F32)
    out_ref[DP:, first : first + TOK] = jnp.zeros((TURNED - DP, TOK), F32)


def two_blocks(turned_ref, pair):
    starts = [pl.multiple_of(ROWS_PAD * (2 * pair + k), 8) for k in range(2)]
    return jnp.concatenate([low(turned_ref[pl.ds(start, 128), :]) for start in starts], 0)


def ff_grads_kernel(x2_ref, cot_ref, d_gu_ref, act_ref, done_ref, out_ref, turned_ref):
    part = pl.program_id(0)

    def fill(right_ref):
        @pl.loop(0, LINES // 2)
        def _(pair):
            rows = pl.ds(pl.multiple_of(256 * pair, 256), 256)
            out_ref[rows, :] = low(nn(two_blocks(turned_ref, pair), right_ref[...]))

    @pl.when(part == 0)
    def _():
        turn_features(x2_ref, turned_ref, 0)

    @pl.when(part < 2)
    def _():
        fill(d_gu_ref)

    @pl.when(part == 2)
    def _():
        turn_features(cot_ref, turned_ref, 0)
        fill(act_ref)


def ff_grads(x2, cot, d_gate_up, act, done):
    def whole(cols):
        return pl.BlockSpec((TOK, cols), lambda i: (0, 0))

    return pl.pallas_call(
        ff_grads_kernel,
        grid=(3,),
        in_specs=[
            whole(DP),
            whole(DP),
            pl.BlockSpec((TOK, FF_PAD), lambda i: (0, jnp.minimum(i, 1))),
            whole(FF_PAD),
            pl.BlockSpec(memory_space=pl.ANY),
        ],
        out_specs=pl.BlockSpec((LINES * 128, FF_PAD), lambda i: (0, i)),
        out_shape=pltpu.HBM((LINES * 128, 3 * FF_PAD), BF16),
        scratch_shapes=[pltpu.VMEM((TURNED, TOK), F32)],
        compiler_params=pltpu.CompilerParams(
            dimension_semantics=("arbitrary",), vmem_limit_bytes=36 * 1024 * 1024
        ),
        cost_estimate=cost(11),
    )(x2, cot, d_gate_up, act, done)


LATE = DP + 512
PARTS = (0, 2 * DP, 2 * DP + RING * ATT_COLS, 2 * DP + RING * ATT_COLS + LATE)


def put(source_ref, out_ref, part, sem):
    copy = pltpu.make_async_copy(source_ref, out_ref.at[:, PARTS[part] : PARTS[part + 1]], sem)
    copy.start()
    copy.wait()


def channel_grads_kernel(x1_ref, d_mixer_ref, d_gate_ref, act_ref, out_ref, left_ref, got_ref, sem):
    def channels(source_ref, right_ref, cols):
        left_ref[...] = source_ref[...].T

        @pl.loop(0, CH // 256)
        def _(part):
            rows = pl.ds(pl.multiple_of(256 * part, 256), 256)
            got_ref[rows, cols] = low(nn(left_ref[rows, :], right_ref[...]))

    channels(d_gate_ref, x1_ref, slice(0, DP))
    channels(act_ref, d_mixer_ref, slice(DP, 2 * DP))
    put(got_ref, out_ref, 0, sem)


def attention_grads_kernel(x1_ref, d_attn_ref, right_ref, grads_ref, out_ref, turned_ref, got_ref, sem):
    turn_features(x1_ref, turned_ref, 0)
    turn_features(d_attn_ref, turned_ref, TOK)

    @pl.loop(0, LINES // 2)
    def _(pair):
        got = low(nn(two_blocks(turned_ref, pair), right_ref[...]))
        for block in range(2):
            rows = pl.ds(pl.multiple_of((2 * pair + block) * CH_PAD, CH_PAD), CH_PAD)
            for q in range(RING):
                first = 128 * block + CH_PAD * q
                got_ref[rows, ATT_COLS * q : ATT_COLS * (q + 1)] = got[first : first + CH_PAD, :]

    put(got_ref, out_ref, 1, sem)


def late_grads_kernel(late_ref, grads_ref, out_ref, sem):
    put(late_ref, out_ref, 2, sem)


def grads_call(kernel, arrays, grads, scratch, micros):
    whole, far = pl.BlockSpec(memory_space=pltpu.VMEM), pl.BlockSpec(memory_space=pltpu.HBM)
    given = [] if grads is None else [grads]
    return pl.pallas_call(
        kernel,
        in_specs=[whole] * len(arrays) + [far] * len(given),
        out_specs=far,
        out_shape=pltpu.HBM((CH, PARTS[3]), BF16),
        input_output_aliases={len(arrays): 0} if given else {},
        scratch_shapes=scratch + [pltpu.SemaphoreType.DMA(())],
        compiler_params=pltpu.CompilerParams(vmem_limit_bytes=36 * 1024 * 1024),
        cost_estimate=cost(micros),
    )(*arrays, *given)


def channel_grads(x1, d_mixer, d_gate, act):
    scratch = [pltpu.VMEM((CH, TOK), BF16), pltpu.VMEM((CH, 2 * DP), BF16)]
    return grads_call(channel_grads_kernel, (x1, d_mixer, d_gate, act), None, scratch, 5)


def attention_grads(x1, d_attn, d_qkv, attended, grads):
    right = [jnp.pad(d_qkv, ((0, 0), (0, QW))), jnp.pad(attended, ((0, 0), (ATT_COLS - QW, 0)))]
    scratch = [pltpu.VMEM((TURNED, 2 * TOK), F32), pltpu.VMEM((CH, RING * ATT_COLS), BF16)]
    return grads_call(attention_grads_kernel, (x1, d_attn, jnp.concatenate(right, 0)), grads, scratch, 8)


def late_grads(late, grads):
    return grads_call(late_grads_kernel, (late,), grads, [], 2)


def nothing_kernel(value_ref, done_ref, out_ref):
    pass


def tie(value, done):
    anywhere = pl.BlockSpec(memory_space=pl.ANY)
    return pl.pallas_call(
        nothing_kernel,
        in_specs=[anywhere, anywhere],
        out_specs=anywhere,
        out_shape=jax.ShapeDtypeStruct(value.shape, value.dtype),
        input_output_aliases={0: 0},
        compiler_params=pltpu.CompilerParams(vmem_limit_bytes=8 * 1024 * 1024),
        cost_estimate=cost(0),
    )(value, done)


def corner(value):
    return value[:8, :128]


def per_device(
    block_in, in_gain, w_query, w_keyval, w_out, attn_gain, ssm_gain, inner_weight, conv_weight, conv_bias,
    w_xproj, w_delta, delta_bias, log_decay, skip_gain, w_ssmout, mlp_gain, w_gateup, w_down, cotangent,
):
    core = lax.axis_index("wt")
    depth = lax.axis_index("z")
    line = lax.axis_index("y") * RING + lax.axis_index("x")

    inner_rows = jnp.transpose(inner_weight, (2, 1, 0))
    small = [conv_weight, conv_bias[None], delta_bias[None], skip_gain[None], log_decay]
    small = [w_delta, jnp.zeros((128 - DTR, PIECE), BF16)] + small + [jnp.zeros((SMALL - SMALL_USED, PIECE), BF16)]
    small = jnp.concatenate(small, 0).T
    channel = jnp.concatenate(
        [
            pad_features(inner_rows).reshape(PIECE, 2 * DP),
            jnp.pad(w_xproj[:, :DTR], ((0, 0), (0, RANK_PAD - DTR))),
            jnp.pad(w_xproj[:, DTR:], ((0, 0), (0, 256 - XROWS))),
            small,
        ],
        1,
    )
    channel = jnp.pad(channel, ((0, CH_PAD - PIECE), (0, 0)))

    own_in = lax.dynamic_slice_in_dim(pad_features(block_in), core * SPAN, SPAN, 0)
    own_cot = lax.dynamic_slice_in_dim(pad_features(cotangent), core * SPAN, SPAN, 0)
    gains = jnp.pad(jnp.stack([in_gain, attn_gain, ssm_gain, mlp_gain]), ((0, 12), (0, 128 - PIECE)))
    gains = in_order(around(tie(gains, corner(channel)), "z"), "z")[:, :4, :PIECE]
    gains = jnp.swapaxes(gains, 0, 1).reshape(4, ROWS)
    gains = jnp.pad(gains, ((0, 12), (0, 128 - ROWS)))
    gains_rows = in_order(around(in_order(around(gains, "x"), "x"), "y"), "y")
    gains = gains_rows.reshape(LINES, 16, 128)[:, :4, :ROWS].astype(F32)
    gains = jnp.pad(jnp.swapaxes(gains, 0, 1), ((0, 0), (0, 0), (0, ROWS_PAD - ROWS))).reshape(4, DP)
    in_g, attn_g, ssm_g, mlp_g = (gains[k : k + 1] for k in range(4))
    mine = in_order(around(own_in, "z"), "z")
    line_in = merge_cores(mine)
    own_in = own_in.astype(F32)
    x1 = low(rms(line_in.astype(F32), in_g))

    attn_piece = jnp.concatenate(
        [
            by_group(w_query.reshape(PIECE, KV_HEADS, QW)),
            by_group(w_keyval[:, 0].reshape(PIECE, KV_HEADS, HEAD)),
            by_group(w_keyval[:, 1].reshape(PIECE, KV_HEADS, HEAD)),
            by_group(w_out.T.reshape(PIECE, KV_HEADS, QW)),
        ],
        2,
    )
    ff_piece = jnp.concatenate([w_gateup, w_down.T[:, None]], 1).reshape(PIECE, 3, RING, FF_PIECE)
    ff_piece = jnp.pad(ff_piece, ((0, 0), (0, 0), (0, 0), (0, FF_PAD - FF_PIECE)))
    ff_piece = jnp.transpose(ff_piece, (2, 0, 1, 3)).reshape(RING, PIECE, 3 * FF_PAD)
    parts = jnp.pad(jnp.concatenate([attn_piece, ff_piece], 2), ((0, 0), (0, CH_PAD - PIECE), (0, 0)))
    halves = jnp.concatenate([own_cot[:CH_PAD], own_cot[CH_PAD:]], 1)
    parts = jnp.concatenate([parts, jnp.broadcast_to(halves, (RING,) + halves.shape)], 2)
    parts = sent_along(tie(parts, corner(line_in)), "z")
    cols = ATT_COLS + 3 * FF_PAD

    def plan(ins, outs):
        pairs = []
        for k, part in enumerate(ins[:RING]):
            pairs.append((part.at[:, :cols], outs[0].at[spot("z", k)]))
            for half in range(2):
                source = part.at[:, cols + DP * half : cols + DP * (half + 1)]
                pairs.append((source, outs[1].at[spot("z", k), CH_PAD * half : CH_PAD * (half + 1)]))
        return pairs

    piece, mine_cot = copy_call(plan, 3 * RING, parts + [gains_rows], [(RING, CH_PAD, cols), (RING, SPAN, DP)])
    line_cot = merge_cores(mine_cot)
    piece = piece[:, :PIECE].reshape(ROWS, cols)
    piece = jnp.pad(piece, ((0, ROWS_PAD - ROWS), (0, 0)))
    attn_piece, ff_piece = piece[:, :ATT_COLS], piece[:, ATT_COLS:]
    out_piece = jnp.pad(pad_features(w_ssmout), ((0, CH_PAD - PIECE), (0, 0))).reshape(4, 8, DP // 128, 128)
    out_piece = jnp.transpose(out_piece, (2, 1, 0, 3)).reshape(ROWS_PAD, 512)
    attn_piece = jnp.concatenate([attn_piece, out_piece], 1)

    with jax.named_scope("gather_channels"):
        channel = gather_lines(channel)
    with jax.named_scope("gather_attention"):
        w_attn = gather_lines(attn_piece)
    with jax.named_scope("gather_ff"):
        w_ff = gather_lines(ff_piece)
    w_so = w_attn[:, ATT_COLS:].reshape(LINES, DP // 128, 8, 4, 128)
    w_so = jnp.transpose(w_so, (0, 3, 2, 1, 4)).reshape(CH, DP)

    w_conv, w_gate = channel[:, :DP], channel[:, COLS[1] : COLS[2]]
    w_x = channel[:, COLS[2] : COLS[2] + XROWS]
    w_d = channel[:, COLS[3] : COLS[3] + DTR]
    small = channel[:, COLS[4] : COLS[5]].astype(F32)
    small_rows = small[:, :32].T
    taps, c_bias, d_bias, skip = small_rows[:CONV], small_rows[4:5], small_rows[5:6], small_rows[6:7]
    rate2 = -jnp.exp(small_rows[7 : 7 + STATE]) * LOG2E
    conv_in = low(nt(x1, w_conv))
    gate_z = low(nt(x1, w_gate)).astype(F32)
    edge = line_shift(conv_in[TOK - (CONV - 1) :], 1)
    padded_in = jnp.concatenate([edge, conv_in], 0).astype(F32)
    conv_out = c_bias
    for tap in range(CONV):
        conv_out = conv_out + taps[tap : tap + 1] * padded_in[tap : tap + TOK]
    mixer_low = low(jax.nn.silu(conv_out))
    mixer_in = mixer_low.astype(F32)
    xproj, _ = sum_line(dot(w_x, mixer_low, ((0,), (1,))))
    step_low = low(xproj[:DTR])
    in_mix, out_mix = spread(xproj[RANK_PAD : RANK_PAD + STATE]), spread(xproj[RANK_PAD + STATE :])
    step_pre = dot(step_low, w_d, ((0,), (1,))) + d_bias
    step = jax.nn.softplus(step_pre)
    ends, spans, pay = scan_ends(step, mixer_in, in_mix, rate2)
    before, rows = state_along_x(rate2, pay, False)

    qkv = low(nn(x1, w_attn[:, : QW + 2 * HEAD]))
    enter, _ = state_along_y(rate2, before, rows, False)
    query, keyval = qkv[:, :QW], qkv[:, QW:]
    keyval = jnp.concatenate([line_shift(keyval, 2), line_shift(keyval, 1), keyval], 0)
    attended, lse = attention_forward(query, keyval, line)
    w_o = w_attn[:, QW + 2 * HEAD : ATT_COLS]
    attn_part = low(nt(attended, w_o))

    ssm_y = scan_outputs(step, mixer_in, in_mix, out_mix, rate2, ends, spans, enter) + skip * mixer_in
    silu_z = jax.nn.silu(gate_z)
    mixer_act = low(ssm_y * silu_z)
    branches, _ = scatter_tokens(jnp.concatenate([attn_part, low(nn(mixer_act, w_so))], 1))
    attn_out, mixer_out = branches[:, :DP], branches[:, DP:]

    hidden = own_in + 0.5 * (rms(attn_out, attn_g) + rms(mixer_out, ssm_g))
    x2 = gather_tokens(low(rms(hidden, mlp_g)))
    w_gu, w_dn = w_ff[:, : 2 * FF_PAD], w_ff[:, 2 * FF_PAD :]
    gate_up = low(nn(x2, w_gu)).astype(F32)
    gate, upper = gate_up[:, :FF_PAD], gate_up[:, FF_PAD:]
    silu_gate = jax.nn.silu(gate)
    mlp_act = low(silu_gate * upper)
    d_act = nn(line_cot, w_dn)
    d_gate_up = low(jnp.concatenate([d_act * upper * silu_grad(gate), d_act * silu_gate], 1))
    d_x2 = add_cores(low(nt(d_gate_up, w_gu)))
    d_x2, _ = add_ring(d_x2)
    grad_ff = ff_grads(x2, line_cot, d_gate_up, mlp_act, corner(d_x2))
    with jax.named_scope("reduce_ff"):
        grad_ff = reduce_lines(grad_ff)

    d_norm, d_mlp_g = rms_back(hidden, mlp_g, d_x2)
    d_hidden = own_cot.astype(F32) + d_norm
    d_attn, d_attn_g = rms_back(attn_out, attn_g, 0.5 * d_hidden)
    d_mixer, d_ssm_g = rms_back(mixer_out, ssm_g, 0.5 * d_hidden)
    blocks = around(low(d_mixer), "z")
    d_mixer = merge_cores(in_order(blocks, "z"))
    blocks = around(tie(low(d_attn), blocks[2]), "z")
    d_attn = merge_cores(in_order(blocks, "z"))

    d_mact = nt(d_mixer, w_so)
    dy = d_mact * silu_z
    d_gate_low = low(d_mact * ssm_y * silu_grad(gate_z))
    heads, pay = scan_heads(step, dy, out_mix, rate2, spans)
    before, rows = state_along_x(rate2, pay, True)
    enter_back, _ = state_along_y(rate2, before, rows, True)

    d_step, lam_b, grad_decay, d_mixes = scan_backward(
        step, mixer_in, dy, in_mix, out_mix, rate2, ends, spans, enter, heads, enter_back
    )
    d_step_pre = (d_step + lam_b * mixer_in) * jax.nn.sigmoid(step_pre)
    d_step_low = low(d_step_pre)
    grad_d = tn(d_step_low, step_low.T)
    d_rank = dot(w_d, d_step_low, ((0,), (1,)))
    d_xproj = jnp.concatenate([jnp.pad(d_rank, ((0, RANK_PAD - DTR), (0, 0))), d_mixes[:, : 2 * STATE].T], 0)
    d_xproj, arrived = sum_line(d_xproj)
    d_xproj = low(d_xproj)
    d_attended = low(nn(d_attn, w_o))
    d_query, d_keyval = attention_backward(query, keyval, tie(lse, arrived), d_attended, line)
    d_keyval = (
        d_keyval[2 * TOK :]
        + line_shift(low(d_keyval[TOK : 2 * TOK]), -1).astype(F32)
        + line_shift(low(d_keyval[:TOK]), -2).astype(F32)
    )
    d_qkv = jnp.concatenate([d_query, low(d_keyval)], 1)
    grads = channel_grads(x1, d_mixer, d_gate_low, mixer_act)
    grads = attention_grads(x1, d_attn, d_qkv, attended, grads)

    grad_x = dot(mixer_low, d_xproj, ((0,), (1,)))
    d_mixer_in = dy * skip + step * lam_b + dot(d_xproj, w_x, ((0,), (1,)))
    d_conv_out = d_mixer_in * silu_grad(conv_out)
    d_after = jnp.concatenate([d_conv_out, line_shift(d_conv_out[: CONV - 1], -1)], 0)
    d_conv_in = sum(taps[k : k + 1] * d_after[CONV - 1 - k : CONV - 1 - k + TOK] for k in range(CONV))
    small_grads = jnp.stack(
        [jnp.sum(d_conv_out * padded_in[tap : tap + TOK], axis=0) for tap in range(CONV)]
        + [jnp.sum(d_conv_out, axis=0), jnp.sum(d_step_pre, axis=0), jnp.sum(dy * mixer_in, axis=0)],
        0,
    )
    small_grads = jnp.concatenate([small_grads, grad_decay], 0).T
    d_conv_low = low(d_conv_in)
    grad_conv = low(tn(d_conv_low, x1))

    d_x1 = nt(d_qkv, w_attn[:, : QW + 2 * HEAD]) + nn(d_conv_low, w_conv) + nn(d_gate_low, w_gate)
    small_grads = jnp.pad(small_grads, ((0, 0), (0, SMALL - SMALL_USED)))
    grad_late = jnp.concatenate(
        [
            grad_conv,
            low(jnp.pad(grad_x, ((0, 0), (0, 256 - XROWS)))),
            low(jnp.pad(grad_d, ((0, 0), (0, 128 - DTR)))),
            low(small_grads),
        ],
        1,
    )
    with jax.named_scope("reduce_rest"):
        grads = reduce_lines(late_grads(grad_late, grads))
    grad_early, grad_late = grads[:, : 2 * DP], grads[:, PARTS[2] :].astype(F32)
    grad_attn = jnp.swapaxes(grads[:, PARTS[1] : PARTS[2]].reshape(CH_PAD, RING, ATT_COLS), 0, 1)
    grad_attn = grad_attn.reshape(RING * CH_PAD, ATT_COLS)
    d_x1, _ = scatter_tokens(low(d_x1))
    d_norm, d_in_g = rms_back(own_in, in_g, d_x1)
    grad_in = d_hidden + d_norm
    mlp_out, _ = scatter_tokens(low(nt(tie(mlp_act, d_conv_low), w_dn)))
    block_out = low(hidden + mlp_out)

    first = core == 0

    def both_cores(own):
        other = swap_core(own)
        return jnp.concatenate([jnp.where(first, own, other), jnp.where(first, other, own)], 0)

    block_out = drop_features(both_cores(block_out))
    grad_in = drop_features(both_cores(grad_in))

    def to_owner(grads):
        return exchange(low(grads[:ROWS]).reshape(RING, PIECE, grads.shape[1]), "z").astype(F32)

    grad_ff = to_owner(grad_ff).reshape(RING, PIECE, 3, FF_PAD)[..., :FF_PIECE]
    grad_ff = jnp.transpose(grad_ff, (1, 2, 0, 3)).reshape(PIECE, 3, RING * FF_PIECE)
    grad_gateup, grad_down = grad_ff[:, :2], grad_ff[:, 2].T

    grad_attn = to_owner(grad_attn)
    other = swap_core(grad_attn)
    grad_attn = jnp.stack([jnp.where(first, grad_attn, other), jnp.where(first, other, grad_attn)], 1)
    grad_attn = jnp.transpose(grad_attn, (2, 0, 1, 3)).reshape(PIECE, 2 * RING, ATT_COLS)[:, :KV_HEADS]
    grad_query = grad_attn[..., :QW].reshape(PIECE, HEADS * HEAD)
    grad_keyval = grad_attn[..., QW : QW + 2 * HEAD].reshape(PIECE, KV_HEADS, 2, HEAD)
    grad_keyval = jnp.swapaxes(grad_keyval, 1, 2).reshape(PIECE, 2, KV_HEADS * HEAD)
    grad_out = grad_attn[..., QW + 2 * HEAD :].reshape(PIECE, HEADS * HEAD).T

    grad_early, grad_late = grad_early[:PIECE, : 2 * DP].astype(F32), grad_late[:PIECE]
    grad_inner = jnp.stack([grad_late[:, :DP], grad_early[:, :DP]], 1)
    grad_inner = jnp.transpose(drop_features(grad_inner), (2, 1, 0))
    grad_ssmout = drop_features(grad_early[:, DP : 2 * DP])
    grad_xproj = grad_late[:, DP : DP + XROWS]
    grad_xproj = jnp.concatenate([grad_xproj[:, :DTR], grad_xproj[:, RANK_PAD:]], 1)
    grad_delta = grad_late[:, DP + 256 : DP + 256 + DTR].T
    small_grads = grad_late[:, DP + 384 : DP + 384 + SMALL_USED].T

    gain_grads = jnp.pad(jnp.stack([d_in_g, d_attn_g, d_ssm_g, d_mlp_g]), ((0, 4), (0, 0)))
    gain_grads = gain_grads + swap_core(gain_grads)
    for axis in SEQ:
        gain_grads = sum(around(gain_grads, axis))
    gain_grads = lax.dynamic_slice_in_dim(gain_grads, line * ROWS_PAD + depth * PIECE, PIECE, 1)

    return (
        block_out, grad_in, gain_grads[0], grad_query, grad_keyval, grad_out, gain_grads[1], gain_grads[2],
        grad_inner, small_grads[:CONV], small_grads[4], grad_xproj, grad_delta, small_grads[5],
        small_grads[7 : 7 + STATE], small_grads[6], grad_ssmout, gain_grads[3], grad_gateup, grad_down,
    )


def solution(mesh):
    fine = Mesh(mesh.devices.reshape(RING, RING, RING, 2), ("y", "x", "z", "wt"))
    both = SEQ + ("wt",)
    weights = (
        P(SEQ),
        P(SEQ, None),
        P(SEQ, None, None),
        P(None, SEQ),
        P(SEQ),
        P(SEQ),
        P(None, None, both),
        P(None, both),
        P(both),
        P(both, None),
        P(None, both),
        P(both),
        P(None, both),
        P(both),
        P(both, None),
        P(SEQ),
        P(SEQ, None, "wt"),
        P("wt", SEQ),
    )
    rows = P(SEQ, None)
    return jax.shard_map(
        per_device, mesh=fine, in_specs=(rows,) + weights + (rows,), out_specs=(rows, rows) + weights, check_vma=False
    )
```

```python
import functools
import math

import jax
import jax.numpy as jnp
from jax import lax
from jax.experimental import pallas as pl
from jax.experimental.pallas import tpu as pltpu
from jax.sharding import Mesh
from jax.sharding import PartitionSpec as P

F32 = jnp.float32
BF16 = jnp.bfloat16

HEADS = 25
KV_HEADS = 5
GROUP = HEADS // KV_HEADS
HEAD = 64
STATE = 16
DTR = 100
CONV = 4
WINDOW = 1024
D = 1600
QW = GROUP * HEAD
EPS = 1e-06
LOG2E = math.log2(math.e)

YX = ("y", "x")
SEQ = ("y", "x", "z")
RING = 4
LINES = 16
PIECE = 25
ROWS = RING * PIECE
ROWS_PAD = 104
DP = LINES * ROWS_PAD
CH_PAD = 32
CH = LINES * CH_PAD
SPAN = 64
CHUNKS = 8
TOK = SPAN * CHUNKS
FF_PIECE = 688
FF_PAD = 768
ATT_COLS = 768
RANK_PAD = 104
XROWS = RANK_PAD + 2 * STATE
PAY = STATE + 8
SMALL = 128
SMALL_USED = CONV + 3 + STATE
COLS = (0, DP, 2 * DP, 2 * DP + 256, 2 * DP + 384, 2 * DP + 512)


def dot(left, right, dims):
    return lax.dot_general(left, right, (dims, ((), ())), preferred_element_type=F32)


def nn(left, right):
    return dot(left, right, ((1,), (0,)))


def nt(left, right):
    return dot(left, right, ((1,), (1,)))


def tn(left, right):
    return dot(left, right, ((0,), (0,)))


def low(value):
    return value.astype(BF16)


def pad_features(value):
    lead = value.shape[:-1]
    value = value.reshape(lead + (LINES, ROWS))
    value = jnp.pad(value, [(0, 0)] * (len(lead) + 1) + [(0, ROWS_PAD - ROWS)])
    return value.reshape(lead + (DP,))


def drop_features(value):
    lead = value.shape[:-1]
    return value.reshape(lead + (LINES, ROWS_PAD))[..., :ROWS].reshape(lead + (D,))


def step_to(axis, distance):
    return [(i, (i + distance) % RING) for i in range(RING)]


def around(value, axis):
    return [value] + [lax.ppermute(value, axis, step_to(axis, RING - d)) for d in range(1, RING)]


def copy_kernel(plan, count, *refs):
    ins, outs, sems = refs[:count], refs[count:-1], refs[-1]
    copies = [pltpu.make_async_copy(src, dst, sems.at[k]) for k, (src, dst) in enumerate(plan(ins, outs))]
    for copy in copies:
        copy.start()
    for copy in copies:
        copy.wait()


def copy_call(plan, number, arrays, shapes, near=False):
    anywhere = pl.BlockSpec(memory_space=pl.ANY)
    return pl.pallas_call(
        functools.partial(copy_kernel, plan, len(arrays)),
        in_specs=[pl.BlockSpec(memory_space=pltpu.HBM)] * len(arrays),
        out_specs=[pl.BlockSpec(memory_space=pltpu.VMEM) if near else anywhere] * len(shapes),
        out_shape=[
            pltpu.VMEM(shape, arrays[0].dtype) if near else jax.ShapeDtypeStruct(shape, arrays[0].dtype)
            for shape in shapes
        ],
        scratch_shapes=[pltpu.SemaphoreType.DMA((number,))],
        compiler_params=pltpu.CompilerParams(vmem_limit_bytes=8 * 1024 * 1024),
        cost_estimate=cost(1),
    )(*arrays)


def spot(axis, k):
    return lax.rem(lax.axis_index(axis) + k, RING)


def in_order(blocks, axis):
    def plan(ins, outs):
        return [(block, outs[0].at[spot(axis, k)]) for k, block in enumerate(ins)]

    return copy_call(plan, RING, blocks, [(RING,) + blocks[0].shape])[0]


def swap_core(value):
    return lax.ppermute(value, "wt", [(0, 1), (1, 0)])


def sent_along(pieces, axis):
    here = lax.axis_index(axis)
    got = [lax.dynamic_index_in_dim(pieces, here, 0, False)]
    for d in range(1, RING):
        piece = lax.dynamic_index_in_dim(pieces, (here + RING - d) % RING, 0, False)
        got.append(lax.ppermute(piece, axis, step_to(axis, RING - d)))
    return got


def exchange(pieces, axis):
    return in_order(sent_along(pieces, axis), axis)


def gather_tokens(own):
    return merge_cores(in_order(around(own, "z"), "z"))


def merge_cores(mine, near=True):
    wide, rows = mine.shape[2], pl.ds(0, SPAN)

    def plan(ins, outs):
        core = lax.axis_index("wt")
        return [(part.at[:, rows], outs[0].at[:, place]) for place, part in ((core, ins[0]), (1 - core, ins[1]))]

    return copy_call(plan, 2, [mine, swap_core(mine)], [(RING, 2, SPAN, wide)], near)[0].reshape(TOK, wide)


def add_cores(partial):
    core = lax.axis_index("wt")
    parts = partial.reshape(RING, 2, SPAN, partial.shape[1])
    mine = lax.dynamic_index_in_dim(parts, core, 1, False)
    theirs = lax.dynamic_index_in_dim(parts, 1 - core, 1, False)
    return mine.astype(F32) + swap_core(theirs).astype(F32)


def add_ring(mine):
    here = lax.axis_index("z")
    total, parts = lax.dynamic_index_in_dim(mine, here, 0, False), []
    for d in range(1, RING):
        piece = lax.dynamic_index_in_dim(mine, (here + d) % RING, 0, False)
        parts.append(lax.ppermute(low(piece), "z", step_to("z", d)))
        total = total + parts[-1].astype(F32)
    return total, parts[0]


def scatter_tokens(partial):
    return add_ring(add_cores(partial))


def sum_line(value):
    value = value + swap_core(value)
    parts = around(low(value), "z")
    return value + (parts[1].astype(F32) + parts[2].astype(F32) + parts[3].astype(F32)), parts[1]


def line_shift(value, distance):
    route = [(i, i + distance) for i in range(LINES) if 0 <= i + distance < LINES]
    return lax.ppermute(value, YX, route)


def rms(value, gain):
    scale = lax.rsqrt(jnp.sum(value * value, axis=-1, keepdims=True) / D + EPS)
    return value * scale * gain


def rms_back(value, gain, dy):
    r = lax.rsqrt(jnp.sum(value * value, axis=-1, keepdims=True) / D + EPS)
    inner = jnp.sum(value * gain * dy, axis=-1, keepdims=True) / D
    return r * gain * dy - value * (r * r * r) * inner, jnp.sum(value * r * dy, axis=0)


def silu_grad(value):
    sig = jax.nn.sigmoid(value)
    return sig * (1.0 + value * (1.0 - sig))


def rows_at(ref, tau):
    return ref[pl.ds(tau, CHUNKS, stride=SPAN), :]


def spread(rows):
    rows = jnp.transpose(rows.reshape(STATE, CHUNKS, SPAN), (2, 0, 1))
    return jnp.broadcast_to(rows[..., None], (SPAN, STATE, CHUNKS, 128))


def rate_rows(rate_ref):
    return [jnp.broadcast_to(rate_ref[n : n + 1, :], (CHUNKS, 128)) for n in range(STATE)]


def zeros():
    return jnp.zeros((CHUNKS, 128), F32)


def walk(start, ends_ref, spans_ref, rate_ref, starts_ref=None, backward=False):
    state, order = start, range(CHUNKS)
    for chunk in reversed(order) if backward else order:
        rows = pl.ds(chunk, STATE, stride=CHUNKS)
        if starts_ref is not None:
            starts_ref[rows, :] = state
        state = jnp.exp2(rate_ref[...] * spans_ref[chunk : chunk + 1, :]) * state + ends_ref[rows, :]
    return state


def chunk_rows(n):
    return slice(CHUNKS * n, CHUNKS * n + CHUNKS)


def report(pay_ref, state, spans_ref):
    pay_ref[:STATE, :] = state
    total = jnp.sum(spans_ref[...], axis=0, keepdims=True)
    pay_ref[STATE:, :] = jnp.broadcast_to(total, (PAY - STATE, 128))


def ends_kernel(step_ref, in_ref, b_ref, rate_ref, end_ref, span_ref, pay_ref):
    rates = rate_rows(rate_ref)

    def token(tau, carry):
        states, total = carry
        step = rows_at(step_ref, tau)
        push = step * rows_at(in_ref, tau)
        states = [jnp.exp2(step * rates[n]) * states[n] + push * b_ref[tau, n] for n in range(STATE)]
        return states, total + step

    states, total = lax.fori_loop(0, SPAN, token, ([zeros()] * STATE, zeros()), unroll=8)
    for n in range(STATE):
        end_ref[chunk_rows(n), :] = states[n]
    span_ref[...] = total
    report(pay_ref, walk(jnp.zeros((STATE, 128), F32), end_ref, span_ref, rate_ref), span_ref)


def outputs_kernel(step_ref, in_ref, b_ref, c_ref, rate_ref, end_ref, span_ref, enter_ref, y_ref, init_ref):
    rates = rate_rows(rate_ref)
    walk(enter_ref[...], end_ref, span_ref, rate_ref, init_ref)

    def token(tau, states):
        step = rows_at(step_ref, tau)
        push = step * rows_at(in_ref, tau)
        states = [jnp.exp2(step * rates[n]) * states[n] + push * b_ref[tau, n] for n in range(STATE)]
        y_ref[pl.ds(tau, CHUNKS, stride=SPAN), :] = sum(c_ref[tau, n] * states[n] for n in range(STATE))
        return states

    lax.fori_loop(0, SPAN, token, [init_ref[chunk_rows(n), :] for n in range(STATE)], unroll=8)


def heads_kernel(step_ref, dy_ref, c_ref, rate_ref, span_ref, head_ref, pay_ref):
    rates = rate_rows(rate_ref)

    def token(back, carry):
        tau = SPAN - 1 - back
        step = rows_at(step_ref, tau)
        dy = rows_at(dy_ref, tau)
        return [jnp.exp2(step * rates[n]) * (c_ref[tau, n] * dy + carry[n]) for n in range(STATE)]

    carry = lax.fori_loop(0, SPAN, token, [zeros()] * STATE, unroll=8)
    for n in range(STATE):
        head_ref[chunk_rows(n), :] = carry[n]
    state = walk(jnp.zeros((STATE, 128), F32), head_ref, span_ref, rate_ref, backward=True)
    report(pay_ref, state, span_ref)


def backward_kernel(
    step_ref, in_ref, dy_ref, b_ref, c_ref, rate_ref, end_ref, span_ref, enter_ref, head_ref, enter_back_ref,
    dstep_ref, lamb_ref, ddecay_ref, dmix_ref,
    a_ref, h_ref, din_ref, dout_ref, init_ref, lam_ref,
):
    rates = rate_rows(rate_ref)

    @pl.when(pl.program_id(0) == 0)
    def _():
        @pl.loop(0, SPAN)
        def _(tau):
            din_ref[tau] = jnp.zeros((STATE, CHUNKS, 128), F32)
            dout_ref[tau] = jnp.zeros((STATE, CHUNKS, 128), F32)

    walk(enter_ref[...], end_ref, span_ref, rate_ref, init_ref)
    walk(enter_back_ref[...], head_ref, span_ref, rate_ref, lam_ref, backward=True)
    for n in range(STATE):
        h_ref[0, n] = init_ref[chunk_rows(n), :]

    def forth(tau, states):
        step = rows_at(step_ref, tau)
        push = step * rows_at(in_ref, tau)
        states = list(states)
        for n in range(STATE):
            decay = jnp.exp2(step * rates[n])
            a_ref[tau, n] = decay
            states[n] = decay * states[n] + push * b_ref[tau, n]
            h_ref[tau + 1, n] = states[n]
        return states

    lax.fori_loop(0, SPAN, forth, [init_ref[chunk_rows(n), :] for n in range(STATE)], unroll=8)

    def back(backwards, carry):
        tau = SPAN - 1 - backwards
        lams, decays = list(carry[0]), list(carry[1])
        step = rows_at(step_ref, tau)
        push = step * rows_at(in_ref, tau)
        dy = rows_at(dy_ref, tau)
        dstep, lamb = zeros(), zeros()
        for n in range(STATE):
            lam = c_ref[tau, n] * dy + lams[n]
            lams[n] = a_ref[tau, n] * lam
            along = lams[n] * h_ref[tau, n]
            dstep = dstep + along * rates[n]
            lamb = lamb + lam * b_ref[tau, n]
            decays[n] = decays[n] + along * step
            din_ref[tau, n] += lam * push
            dout_ref[tau, n] += dy * h_ref[tau + 1, n]
        dstep_ref[pl.ds(tau, CHUNKS, stride=SPAN), :] = dstep * (1.0 / LOG2E)
        lamb_ref[pl.ds(tau, CHUNKS, stride=SPAN), :] = lamb
        return lams, decays

    start = ([lam_ref[chunk_rows(n), :] for n in range(STATE)], [zeros()] * STATE)
    _, decays = lax.fori_loop(0, SPAN, back, start, unroll=8)
    total = jnp.concatenate([jnp.sum(decays[n], axis=0, keepdims=True) for n in range(STATE)], 0)
    ddecay_ref[...] = total * rate_ref[...] * (1.0 / LOG2E)

    @pl.when(pl.program_id(0) == pl.num_programs(0) - 1)
    def _():
        lane = lax.broadcasted_iota(jnp.int32, (CHUNKS, 128), 1)

        def fold(tau, carry):
            rows = zeros()
            for n in range(STATE):
                rows = jnp.where(lane == n, jnp.sum(din_ref[tau, n], axis=1, keepdims=True), rows)
                total = jnp.sum(dout_ref[tau, n], axis=1, keepdims=True)
                rows = jnp.where(lane == STATE + n, total, rows)
            dmix_ref[pl.ds(tau, CHUNKS, stride=SPAN), :] = rows
            return carry

        lax.fori_loop(0, SPAN, fold, 0, unroll=16)


def cost(micros):
    return pl.CostEstimate(flops=int(micros * 1e9), bytes_accessed=int(micros * 3e6), transcendentals=0)


def scan_call(kernel, ins, outs, scratch, micros):
    wide = (SPAN, STATE, CHUNKS, 128)
    once = pl.BlockSpec(wide, lambda i: (0, 0, 0, 0), pipeline_mode=pl.Buffered(1))

    def lanes(rows):
        return (rows, CH), pl.BlockSpec((rows, 128), lambda i: (0, i))

    kinds = {
        "tok": lanes(TOK),
        "mix": ((TOK, 128), pl.BlockSpec((TOK, 128), lambda i: (0, 0))),
        "state": lanes(STATE),
        "states": lanes(STATE * CHUNKS),
        "chunk": lanes(CHUNKS),
        "pay": lanes(PAY),
        "wide": (wide, once),
    }
    return pl.pallas_call(
        kernel,
        grid=(CH // 128,),
        in_specs=[kinds[kind][1] for kind in ins],
        out_specs=[kinds[kind][1] for kind in outs],
        out_shape=[jax.ShapeDtypeStruct(kinds[kind][0], F32) for kind in outs],
        scratch_shapes=[pltpu.VMEM(shape, F32) for shape in scratch],
        compiler_params=pltpu.CompilerParams(
            dimension_semantics=("arbitrary",), vmem_limit_bytes=36 * 1024 * 1024
        ),
        cost_estimate=cost(micros),
    )


WALK = (STATE * CHUNKS, 128)


def scan_ends(*args):
    ins = ("tok", "tok", "wide", "state")
    return scan_call(ends_kernel, ins, ("states", "chunk", "pay"), (), 5)(*args)


def scan_outputs(*args):
    ins = ("tok", "tok", "wide", "wide", "state", "states", "chunk", "state")
    return scan_call(outputs_kernel, ins, ("tok",), (WALK,), 7)(*args)[0]


def scan_heads(*args):
    ins = ("tok", "tok", "wide", "state", "chunk")
    return scan_call(heads_kernel, ins, ("states", "pay"), (), 5)(*args)


def scan_backward(*args):
    ins = ("tok", "tok", "tok", "wide", "wide", "state", "states", "chunk", "state", "states", "state")
    outs = ("tok", "tok", "state", "mix")
    wide = [(SPAN + extra, STATE, CHUNKS, 128) for extra in (0, 1, 0, 0)]
    return scan_call(backward_kernel, ins, outs, wide + [WALK, WALK], 20)(*args)


def nearer(value, axis, backward):
    here = lax.axis_index(axis)
    if backward:
        here = RING - 1 - here
    steps = ((d, lax.ppermute(value, axis, step_to(axis, -d if backward else d))) for d in (3, 2, 1))
    return here, list(steps)


def fold(rate2, blocks, keep):
    state, span = jnp.zeros_like(rate2), jnp.zeros_like(rate2[:1])
    for d, block in blocks:
        block_span = block[STATE : STATE + 1]
        longer = jnp.exp2(rate2 * block_span) * state + block[:STATE]
        state = jnp.where(keep(d), longer, state)
        span = jnp.where(keep(d), span + block_span, span)
    return state, span


def state_along_x(rate2, pay, backward):
    here, blocks = nearer(pay, "x", backward)
    before = fold(rate2, blocks, lambda d: d <= here)
    after, after_span = fold(rate2, blocks, lambda d: d > here)
    own_span = pay[STATE : STATE + 1]
    whole = jnp.exp2(rate2 * own_span) * before[0] + pay[:STATE]
    whole = jnp.exp2(rate2 * after_span) * whole + after
    rows = jnp.concatenate([whole, jnp.broadcast_to(before[1] + own_span + after_span, (PAY - STATE, CH))], 0)
    return before, rows


def state_along_y(rate2, before, rows, backward):
    here, blocks = nearer(rows, "y", backward)
    above, _ = fold(rate2, blocks, lambda d: d <= here)
    return jnp.exp2(rate2 * before[1]) * above + before[0], blocks[-1][1]


QBLOCK = 128
SCALE = HEAD ** (-0.5)
SEEN = WINDOW + QBLOCK


def head_cols(g):
    return slice(HEAD * g, HEAD * g + HEAD)


def fill_bias(first_ref, bias_ref):
    row = lax.broadcasted_iota(jnp.int32, (QBLOCK, SEEN), 0)
    col = lax.broadcasted_iota(jnp.int32, (QBLOCK, SEEN), 1)
    first = first_ref[0] - pl.program_id(0) * QBLOCK
    bias_ref[...] = jnp.where((col > row) & (col <= row + WINDOW) & (col >= first), 0.0, -1e30)


def attend_kernel(first_ref, q_ref, kv_ref, out_ref, lse_ref, bias_ref):
    fill_bias(first_ref, bias_ref)
    keyval = kv_ref[pl.ds(pl.program_id(0) * QBLOCK, SEEN), :]
    keys = keyval[:, :HEAD]
    lane = lax.broadcasted_iota(jnp.int32, (QBLOCK, 128), 1)
    lses = jnp.zeros((QBLOCK, 128), F32)
    outs = []
    for g in range(GROUP):
        scores = nt(q_ref[:, head_cols(g)] * BF16(SCALE), keys) + bias_ref[...]
        peak = jnp.max(scores, axis=1, keepdims=True)
        probs = jnp.exp(scores - peak)
        total = jnp.sum(probs, axis=1, keepdims=True)
        outs.append(low(nn(low(probs), keyval)[:, HEAD:] / total))
        lses = jnp.where(lane == g, peak + jnp.log(total), lses)
    out_ref[...] = jnp.concatenate(outs, 1)
    lse_ref[...] = lses


def attend_back_kernel(
    first_ref, q_ref, kv_ref, dout_ref, lse_ref, dq_ref, dkv_ref, bias_ref, probs_ref, dscores_ref
):
    block = pl.program_id(0)
    fill_bias(first_ref, bias_ref)

    @pl.when(block == 0)
    def _():
        dkv_ref[...] = jnp.zeros(dkv_ref.shape, F32)

    here = pl.ds(block * QBLOCK, SEEN)
    keyval = kv_ref[here, :]
    keys, values = keyval[:, :HEAD], keyval[:, HEAD:]
    lses = lse_ref[...]
    queries = [q_ref[:, head_cols(g)] * BF16(SCALE) for g in range(GROUP)]
    d_outs = [dout_ref[:, head_cols(g)] for g in range(GROUP)]
    d_queries = []
    for g in range(GROUP):
        rows = slice(g * QBLOCK, (g + 1) * QBLOCK)
        probs = jnp.exp(nt(queries[g], keys) + bias_ref[...] - lses[:, g : g + 1])
        weighted = probs * nt(d_outs[g], values)
        d_scores = low(weighted - probs * jnp.sum(weighted, axis=1, keepdims=True))
        probs_ref[rows, :] = low(probs)
        dscores_ref[rows, :] = d_scores
        d_queries.append(low(nn(d_scores, keys) * SCALE))
    dq_ref[...] = jnp.concatenate(d_queries, 1)
    d_keys = tn(dscores_ref[...], jnp.concatenate(queries, 0))
    d_values = tn(probs_ref[...], jnp.concatenate(d_outs, 0))
    dkv_ref[here, :] += jnp.concatenate([d_keys, d_values], 1)


def attention_call(kernel, ins, outs, scratch, micros):
    kinds = {
        "first": pl.BlockSpec(memory_space=pltpu.SMEM),
        "heads": pl.BlockSpec((QBLOCK, QW), lambda i: (i, 0)),
        "keys": pl.BlockSpec((WINDOW + TOK, 128), lambda i: (0, 0)),
        "lse": pl.BlockSpec((QBLOCK, 128), lambda i: (i, 0)),
    }
    shapes = {"heads": ((TOK, QW), BF16), "keys": ((WINDOW + TOK, 128), F32), "lse": ((TOK, 128), F32)}
    return pl.pallas_call(
        kernel,
        grid=(TOK // QBLOCK,),
        in_specs=[kinds[kind] for kind in ins],
        out_specs=[kinds[kind] for kind in outs],
        out_shape=[jax.ShapeDtypeStruct(*shapes[kind]) for kind in outs],
        scratch_shapes=[pltpu.VMEM((QBLOCK, SEEN), F32)] + [pltpu.VMEM((GROUP * QBLOCK, SEEN), BF16)] * scratch,
        compiler_params=pltpu.CompilerParams(
            dimension_semantics=("arbitrary",), vmem_limit_bytes=28 * 1024 * 1024
        ),
        cost_estimate=cost(micros),
    )


def first_key(line):
    return (WINDOW - line * TOK).reshape(1).astype(jnp.int32)


def attention_forward(query, keyval, line):
    call = attention_call(attend_kernel, ("first", "heads", "keys"), ("heads", "lse"), 0, 9)
    return call(first_key(line), query, keyval)


def attention_backward(query, keyval, lse, d_out, line):
    ins = ("first", "heads", "keys", "heads", "lse")
    call = attention_call(attend_back_kernel, ins, ("heads", "keys"), 2, 14)
    return call(first_key(line), query, keyval, d_out, lse)


def by_group(pieces):
    rows, _, cols = pieces.shape
    pieces = jnp.pad(pieces, ((0, 0), (0, 2 * RING - KV_HEADS), (0, 0)))
    pieces = pieces.reshape(rows, RING, 2, cols)
    mine = lax.dynamic_index_in_dim(pieces, lax.axis_index("wt"), 2, False)
    return jnp.swapaxes(mine, 0, 1)


def gather_lines(block):
    return lax.all_gather(block, YX, axis=0, tiled=True)


def reduce_lines(grads):
    return lax.psum_scatter(grads, YX, scatter_dimension=0, tiled=True)


TURNED = ROWS_PAD * (LINES - 1) + 128


def turn_features(x_ref, out_ref, first):
    for tile in range(DP // 128):
        cols = slice(128 * tile, 128 * tile + 128)
        out_ref[cols, first : first + TOK] = x_ref[:, cols].T.astype(F32)
    out_ref[DP:, first : first + TOK] = jnp.zeros((TURNED - DP, TOK), F32)


def two_blocks(turned_ref, pair):
    starts = [pl.multiple_of(ROWS_PAD * (2 * pair + k), 8) for k in range(2)]
    return jnp.concatenate([low(turned_ref[pl.ds(start, 128), :]) for start in starts], 0)


def ff_grads_kernel(x2_ref, cot_ref, d_gu_ref, act_ref, done_ref, out_ref, turned_ref):
    part = pl.program_id(0)

    def fill(right_ref):
        @pl.loop(0, LINES // 2)
        def _(pair):
            rows = pl.ds(pl.multiple_of(256 * pair, 256), 256)
            out_ref[rows, :] = low(nn(two_blocks(turned_ref, pair), right_ref[...]))

    @pl.when(part == 0)
    def _():
        turn_features(x2_ref, turned_ref, 0)

    @pl.when(part < 2)
    def _():
        fill(d_gu_ref)

    @pl.when(part == 2)
    def _():
        turn_features(cot_ref, turned_ref, 0)
        fill(act_ref)


def ff_grads(x2, cot, d_gate_up, act, done):
    def whole(cols):
        return pl.BlockSpec((TOK, cols), lambda i: (0, 0))

    return pl.pallas_call(
        ff_grads_kernel,
        grid=(3,),
        in_specs=[
            whole(DP),
            whole(DP),
            pl.BlockSpec((TOK, FF_PAD), lambda i: (0, jnp.minimum(i, 1))),
            whole(FF_PAD),
            pl.BlockSpec(memory_space=pl.ANY),
        ],
        out_specs=pl.BlockSpec((LINES * 128, FF_PAD), lambda i: (0, i)),
        out_shape=pltpu.HBM((LINES * 128, 3 * FF_PAD), BF16),
        scratch_shapes=[pltpu.VMEM((TURNED, TOK), F32)],
        compiler_params=pltpu.CompilerParams(
            dimension_semantics=("arbitrary",), vmem_limit_bytes=36 * 1024 * 1024
        ),
        cost_estimate=cost(11),
    )(x2, cot, d_gate_up, act, done)


LATE = DP + 512
PARTS = (0, 2 * DP, 2 * DP + RING * ATT_COLS, 2 * DP + RING * ATT_COLS + LATE)


def put(source_ref, out_ref, part, sem):
    copy = pltpu.make_async_copy(source_ref, out_ref.at[:, PARTS[part] : PARTS[part + 1]], sem)
    copy.start()
    copy.wait()


def channel_grads_kernel(x1_ref, d_mixer_ref, d_gate_ref, act_ref, out_ref, left_ref, got_ref, sem):
    def channels(source_ref, right_ref, cols):
        left_ref[...] = source_ref[...].T

        @pl.loop(0, CH // 256)
        def _(part):
            rows = pl.ds(pl.multiple_of(256 * part, 256), 256)
            got_ref[rows, cols] = low(nn(left_ref[rows, :], right_ref[...]))

    channels(d_gate_ref, x1_ref, slice(0, DP))
    channels(act_ref, d_mixer_ref, slice(DP, 2 * DP))
    put(got_ref, out_ref, 0, sem)


def attention_grads_kernel(x1_ref, d_attn_ref, right_ref, grads_ref, out_ref, turned_ref, got_ref, sem):
    turn_features(x1_ref, turned_ref, 0)
    turn_features(d_attn_ref, turned_ref, TOK)

    @pl.loop(0, LINES // 2)
    def _(pair):
        got = low(nn(two_blocks(turned_ref, pair), right_ref[...]))
        for block in range(2):
            rows = pl.ds(pl.multiple_of((2 * pair + block) * CH_PAD, CH_PAD), CH_PAD)
            for q in range(RING):
                first = 128 * block + CH_PAD * q
                got_ref[rows, ATT_COLS * q : ATT_COLS * (q + 1)] = got[first : first + CH_PAD, :]

    put(got_ref, out_ref, 1, sem)


def late_grads_kernel(late_ref, grads_ref, out_ref, sem):
    put(late_ref, out_ref, 2, sem)


def grads_call(kernel, arrays, grads, scratch, micros):
    whole, far = pl.BlockSpec(memory_space=pltpu.VMEM), pl.BlockSpec(memory_space=pltpu.HBM)
    given = [] if grads is None else [grads]
    return pl.pallas_call(
        kernel,
        in_specs=[whole] * len(arrays) + [far] * len(given),
        out_specs=far,
        out_shape=pltpu.HBM((CH, PARTS[3]), BF16),
        input_output_aliases={len(arrays): 0} if given else {},
        scratch_shapes=scratch + [pltpu.SemaphoreType.DMA(())],
        compiler_params=pltpu.CompilerParams(vmem_limit_bytes=36 * 1024 * 1024),
        cost_estimate=cost(micros),
    )(*arrays, *given)


def channel_grads(x1, d_mixer, d_gate, act):
    scratch = [pltpu.VMEM((CH, TOK), BF16), pltpu.VMEM((CH, 2 * DP), BF16)]
    return grads_call(channel_grads_kernel, (x1, d_mixer, d_gate, act), None, scratch, 5)


def attention_grads(x1, d_attn, d_qkv, attended, grads):
    right = [jnp.pad(d_qkv, ((0, 0), (0, QW))), jnp.pad(attended, ((0, 0), (ATT_COLS - QW, 0)))]
    scratch = [pltpu.VMEM((TURNED, 2 * TOK), F32), pltpu.VMEM((CH, RING * ATT_COLS), BF16)]
    return grads_call(attention_grads_kernel, (x1, d_attn, jnp.concatenate(right, 0)), grads, scratch, 8)


def late_grads(late, grads):
    return grads_call(late_grads_kernel, (late,), grads, [], 2)


def nothing_kernel(value_ref, done_ref, out_ref):
    pass


def tie(value, done):
    anywhere = pl.BlockSpec(memory_space=pl.ANY)
    return pl.pallas_call(
        nothing_kernel,
        in_specs=[anywhere, anywhere],
        out_specs=anywhere,
        out_shape=jax.ShapeDtypeStruct(value.shape, value.dtype),
        input_output_aliases={0: 0},
        compiler_params=pltpu.CompilerParams(vmem_limit_bytes=8 * 1024 * 1024),
        cost_estimate=cost(0),
    )(value, done)


def corner(value):
    return value[:8, :128]


def per_device(
    block_in, in_gain, w_query, w_keyval, w_out, attn_gain, ssm_gain, inner_weight, conv_weight, conv_bias,
    w_xproj, w_delta, delta_bias, log_decay, skip_gain, w_ssmout, mlp_gain, w_gateup, w_down, cotangent,
):
    core = lax.axis_index("wt")
    depth = lax.axis_index("z")
    line = lax.axis_index("y") * RING + lax.axis_index("x")

    inner_rows = jnp.transpose(inner_weight, (2, 1, 0))
    small = [conv_weight, conv_bias[None], delta_bias[None], skip_gain[None], log_decay]
    small = [w_delta, jnp.zeros((128 - DTR, PIECE), BF16)] + small + [jnp.zeros((SMALL - SMALL_USED, PIECE), BF16)]
    small = jnp.concatenate(small, 0).T
    channel = jnp.concatenate(
        [
            pad_features(inner_rows).reshape(PIECE, 2 * DP),
            jnp.pad(w_xproj[:, :DTR], ((0, 0), (0, RANK_PAD - DTR))),
            jnp.pad(w_xproj[:, DTR:], ((0, 0), (0, 256 - XROWS))),
            small,
        ],
        1,
    )
    channel = jnp.pad(channel, ((0, CH_PAD - PIECE), (0, 0)))

    own_in = lax.dynamic_slice_in_dim(pad_features(block_in), core * SPAN, SPAN, 0)
    own_cot = lax.dynamic_slice_in_dim(pad_features(cotangent), core * SPAN, SPAN, 0)
    gains = jnp.pad(jnp.stack([in_gain, attn_gain, ssm_gain, mlp_gain]), ((0, 12), (0, 128 - PIECE)))
    gains = in_order(around(tie(gains, corner(channel)), "z"), "z")[:, :4, :PIECE]
    gains = jnp.swapaxes(gains, 0, 1).reshape(4, ROWS)
    gains = jnp.pad(gains, ((0, 12), (0, 128 - ROWS)))
    gains_rows = in_order(around(in_order(around(gains, "x"), "x"), "y"), "y")
    gains = gains_rows.reshape(LINES, 16, 128)[:, :4, :ROWS].astype(F32)
    gains = jnp.pad(jnp.swapaxes(gains, 0, 1), ((0, 0), (0, 0), (0, ROWS_PAD - ROWS))).reshape(4, DP)
    in_g, attn_g, ssm_g, mlp_g = (gains[k : k + 1] for k in range(4))
    mine = in_order(around(own_in, "z"), "z")
    line_in = merge_cores(mine)
    own_in = own_in.astype(F32)
    x1 = low(rms(line_in.astype(F32), in_g))

    attn_piece = jnp.concatenate(
        [
            by_group(w_query.reshape(PIECE, KV_HEADS, QW)),
            by_group(w_keyval[:, 0].reshape(PIECE, KV_HEADS, HEAD)),
            by_group(w_keyval[:, 1].reshape(PIECE, KV_HEADS, HEAD)),
            by_group(w_out.T.reshape(PIECE, KV_HEADS, QW)),
        ],
        2,
    )
    ff_piece = jnp.concatenate([w_gateup, w_down.T[:, None]], 1).reshape(PIECE, 3, RING, FF_PIECE)
    ff_piece = jnp.pad(ff_piece, ((0, 0), (0, 0), (0, 0), (0, FF_PAD - FF_PIECE)))
    ff_piece = jnp.transpose(ff_piece, (2, 0, 1, 3)).reshape(RING, PIECE, 3 * FF_PAD)
    parts = jnp.pad(jnp.concatenate([attn_piece, ff_piece], 2), ((0, 0), (0, CH_PAD - PIECE), (0, 0)))
    halves = jnp.concatenate([own_cot[:CH_PAD], own_cot[CH_PAD:]], 1)
    parts = jnp.concatenate([parts, jnp.broadcast_to(halves, (RING,) + halves.shape)], 2)
    parts = sent_along(tie(parts, corner(line_in)), "z")
    cols = ATT_COLS + 3 * FF_PAD

    def plan(ins, outs):
        pairs = []
        for k, part in enumerate(ins[:RING]):
            pairs.append((part.at[:, :cols], outs[0].at[spot("z", k)]))
            for half in range(2):
                source = part.at[:, cols + DP * half : cols + DP * (half + 1)]
                pairs.append((source, outs[1].at[spot("z", k), CH_PAD * half : CH_PAD * (half + 1)]))
        return pairs

    piece, mine_cot = copy_call(plan, 3 * RING, parts + [gains_rows], [(RING, CH_PAD, cols), (RING, SPAN, DP)])
    line_cot = merge_cores(mine_cot, False)
    piece = piece[:, :PIECE].reshape(ROWS, cols)
    piece = jnp.pad(piece, ((0, ROWS_PAD - ROWS), (0, 0)))
    attn_piece, ff_piece = piece[:, :ATT_COLS], piece[:, ATT_COLS:]
    out_piece = jnp.pad(pad_features(w_ssmout), ((0, CH_PAD - PIECE), (0, 0))).reshape(4, 8, DP // 128, 128)
    out_piece = jnp.transpose(out_piece, (2, 1, 0, 3)).reshape(ROWS_PAD, 512)
    attn_piece = jnp.concatenate([attn_piece, out_piece], 1)

    with jax.named_scope("gather_channels"):
        channel = gather_lines(channel)
    with jax.named_scope("gather_attention"):
        w_attn = gather_lines(attn_piece)
    with jax.named_scope("gather_ff"):
        w_ff = gather_lines(ff_piece)
    w_so = w_attn[:, ATT_COLS:].reshape(LINES, DP // 128, 8, 4, 128)
    w_so = jnp.transpose(w_so, (0, 3, 2, 1, 4)).reshape(CH, DP)

    w_conv, w_gate = channel[:, :DP], channel[:, COLS[1] : COLS[2]]
    w_x = channel[:, COLS[2] : COLS[2] + XROWS]
    w_d = channel[:, COLS[3] : COLS[3] + DTR]
    small = channel[:, COLS[4] : COLS[5]].astype(F32)
    small_rows = small[:, :32].T
    taps, c_bias, d_bias, skip = small_rows[:CONV], small_rows[4:5], small_rows[5:6], small_rows[6:7]
    rate2 = -jnp.exp(small_rows[7 : 7 + STATE]) * LOG2E
    conv_in = low(nt(x1, w_conv))
    gate_z = low(nt(x1, w_gate)).astype(F32)
    edge = line_shift(conv_in[TOK - (CONV - 1) :], 1)
    padded_in = jnp.concatenate([edge, conv_in], 0).astype(F32)
    conv_out = c_bias
    for tap in range(CONV):
        conv_out = conv_out + taps[tap : tap + 1] * padded_in[tap : tap + TOK]
    mixer_low = low(jax.nn.silu(conv_out))
    mixer_in = mixer_low.astype(F32)
    xproj, _ = sum_line(dot(w_x, mixer_low, ((0,), (1,))))
    step_low = low(xproj[:DTR])
    in_mix, out_mix = spread(xproj[RANK_PAD : RANK_PAD + STATE]), spread(xproj[RANK_PAD + STATE :])
    step_pre = dot(step_low, w_d, ((0,), (1,))) + d_bias
    step = jax.nn.softplus(step_pre)
    ends, spans, pay = scan_ends(step, mixer_in, in_mix, rate2)
    before, rows = state_along_x(rate2, pay, False)

    qkv = low(nn(x1, w_attn[:, : QW + 2 * HEAD]))
    enter, _ = state_along_y(rate2, before, rows, False)
    query, keyval = qkv[:, :QW], qkv[:, QW:]
    keyval = jnp.concatenate([line_shift(keyval, 2), line_shift(keyval, 1), keyval], 0)
    attended, lse = attention_forward(query, keyval, line)
    w_o = w_attn[:, QW + 2 * HEAD : ATT_COLS]
    attn_part = low(nt(attended, w_o))

    ssm_y = scan_outputs(step, mixer_in, in_mix, out_mix, rate2, ends, spans, enter) + skip * mixer_in
    silu_z = jax.nn.silu(gate_z)
    mixer_act = low(ssm_y * silu_z)
    branches, _ = scatter_tokens(jnp.concatenate([attn_part, low(nn(mixer_act, w_so))], 1))
    attn_out, mixer_out = branches[:, :DP], branches[:, DP:]

    hidden = own_in + 0.5 * (rms(attn_out, attn_g) + rms(mixer_out, ssm_g))
    x2 = gather_tokens(low(rms(hidden, mlp_g)))
    w_gu, w_dn = w_ff[:, : 2 * FF_PAD], w_ff[:, 2 * FF_PAD :]
    gate_up = low(nn(x2, w_gu)).astype(F32)
    gate, upper = gate_up[:, :FF_PAD], gate_up[:, FF_PAD:]
    silu_gate = jax.nn.silu(gate)
    mlp_act = low(silu_gate * upper)
    d_act = nn(line_cot, w_dn)
    d_gate_up = low(jnp.concatenate([d_act * upper * silu_grad(gate), d_act * silu_gate], 1))
    d_x2 = add_cores(low(nt(d_gate_up, w_gu)))
    d_x2, _ = add_ring(d_x2)
    grad_ff = ff_grads(x2, line_cot, d_gate_up, mlp_act, corner(d_x2))
    with jax.named_scope("reduce_ff"):
        grad_ff = reduce_lines(grad_ff)

    d_norm, d_mlp_g = rms_back(hidden, mlp_g, d_x2)
    d_hidden = own_cot.astype(F32) + d_norm
    d_attn, d_attn_g = rms_back(attn_out, attn_g, 0.5 * d_hidden)
    d_mixer, d_ssm_g = rms_back(mixer_out, ssm_g, 0.5 * d_hidden)
    blocks = around(low(d_mixer), "z")
    d_mixer = merge_cores(in_order(blocks, "z"))
    blocks = around(tie(low(d_attn), blocks[2]), "z")
    d_attn = merge_cores(in_order(blocks, "z"))

    d_mact = nt(d_mixer, w_so)
    dy = d_mact * silu_z
    d_gate_low = low(d_mact * ssm_y * silu_grad(gate_z))
    heads, pay = scan_heads(step, dy, out_mix, rate2, spans)
    before, rows = state_along_x(rate2, pay, True)
    enter_back, _ = state_along_y(rate2, before, rows, True)

    d_step, lam_b, grad_decay, d_mixes = scan_backward(
        step, mixer_in, dy, in_mix, out_mix, rate2, ends, spans, enter, heads, enter_back
    )
    d_step_pre = (d_step + lam_b * mixer_in) * jax.nn.sigmoid(step_pre)
    d_step_low = low(d_step_pre)
    grad_d = tn(d_step_low, step_low.T)
    d_rank = dot(w_d, d_step_low, ((0,), (1,)))
    d_xproj = jnp.concatenate([jnp.pad(d_rank, ((0, RANK_PAD - DTR), (0, 0))), d_mixes[:, : 2 * STATE].T], 0)
    d_xproj, arrived = sum_line(d_xproj)
    d_xproj = low(d_xproj)
    d_attended = low(nn(d_attn, w_o))
    d_query, d_keyval = attention_backward(query, keyval, tie(lse, arrived), d_attended, line)
    d_keyval = (
        d_keyval[2 * TOK :]
        + line_shift(low(d_keyval[TOK : 2 * TOK]), -1).astype(F32)
        + line_shift(low(d_keyval[:TOK]), -2).astype(F32)
    )
    d_qkv = jnp.concatenate([d_query, low(d_keyval)], 1)
    grads = channel_grads(x1, d_mixer, d_gate_low, mixer_act)
    grads = attention_grads(x1, d_attn, d_qkv, attended, grads)

    grad_x = dot(mixer_low, d_xproj, ((0,), (1,)))
    d_mixer_in = dy * skip + step * lam_b + dot(d_xproj, w_x, ((0,), (1,)))
    d_conv_out = d_mixer_in * silu_grad(conv_out)
    d_after = jnp.concatenate([d_conv_out, line_shift(d_conv_out[: CONV - 1], -1)], 0)
    d_conv_in = sum(taps[k : k + 1] * d_after[CONV - 1 - k : CONV - 1 - k + TOK] for k in range(CONV))
    small_grads = jnp.stack(
        [jnp.sum(d_conv_out * padded_in[tap : tap + TOK], axis=0) for tap in range(CONV)]
        + [jnp.sum(d_conv_out, axis=0), jnp.sum(d_step_pre, axis=0), jnp.sum(dy * mixer_in, axis=0)],
        0,
    )
    small_grads = jnp.concatenate([small_grads, grad_decay], 0).T
    d_conv_low = low(d_conv_in)
    grad_conv = low(tn(d_conv_low, x1))

    d_x1 = nt(d_qkv, w_attn[:, : QW + 2 * HEAD]) + nn(d_conv_low, w_conv) + nn(d_gate_low, w_gate)
    small_grads = jnp.pad(small_grads, ((0, 0), (0, SMALL - SMALL_USED)))
    grad_late = jnp.concatenate(
        [
            grad_conv,
            low(jnp.pad(grad_x, ((0, 0), (0, 256 - XROWS)))),
            low(jnp.pad(grad_d, ((0, 0), (0, 128 - DTR)))),
            low(small_grads),
        ],
        1,
    )
    with jax.named_scope("reduce_rest"):
        grads = reduce_lines(late_grads(grad_late, grads))
    grad_early, grad_late = grads[:, : 2 * DP], grads[:, PARTS[2] :].astype(F32)
    grad_attn = jnp.swapaxes(grads[:, PARTS[1] : PARTS[2]].reshape(CH_PAD, RING, ATT_COLS), 0, 1)
    grad_attn = grad_attn.reshape(RING * CH_PAD, ATT_COLS)
    d_x1, _ = scatter_tokens(low(d_x1))
    d_norm, d_in_g = rms_back(own_in, in_g, d_x1)
    grad_in = d_hidden + d_norm
    mlp_out, _ = scatter_tokens(low(nt(tie(mlp_act, d_conv_low), w_dn)))
    block_out = low(hidden + mlp_out)

    first = core == 0

    def both_cores(own):
        other = swap_core(own)
        return jnp.concatenate([jnp.where(first, own, other), jnp.where(first, other, own)], 0)

    block_out = drop_features(both_cores(block_out))
    grad_in = drop_features(both_cores(grad_in))

    def to_owner(grads):
        return exchange(low(grads[:ROWS]).reshape(RING, PIECE, grads.shape[1]), "z")

    grad_ff = to_owner(grad_ff).astype(F32).reshape(RING, PIECE, 3, FF_PAD)[..., :FF_PIECE]
    grad_ff = jnp.transpose(grad_ff, (1, 2, 0, 3)).reshape(PIECE, 3, RING * FF_PIECE)
    grad_gateup, grad_down = grad_ff[:, :2], grad_ff[:, 2].T

    grad_attn = to_owner(grad_attn)
    other = swap_core(grad_attn)
    grad_attn = jnp.stack([jnp.where(first, grad_attn, other), jnp.where(first, other, grad_attn)], 1)
    grad_attn = jnp.transpose(grad_attn.astype(F32), (2, 0, 1, 3)).reshape(PIECE, 2 * RING, ATT_COLS)[:, :KV_HEADS]
    grad_query = grad_attn[..., :QW].reshape(PIECE, HEADS * HEAD)
    grad_keyval = grad_attn[..., QW : QW + 2 * HEAD].reshape(PIECE, KV_HEADS, 2, HEAD)
    grad_keyval = jnp.swapaxes(grad_keyval, 1, 2).reshape(PIECE, 2, KV_HEADS * HEAD)
    grad_out = grad_attn[..., QW + 2 * HEAD :].reshape(PIECE, HEADS * HEAD).T

    grad_early, grad_late = grad_early[:PIECE, : 2 * DP].astype(F32), grad_late[:PIECE]
    grad_inner = jnp.stack([grad_late[:, :DP], grad_early[:, :DP]], 1)
    grad_inner = jnp.transpose(drop_features(grad_inner), (2, 1, 0))
    grad_ssmout = drop_features(grad_early[:, DP : 2 * DP])
    grad_xproj = grad_late[:, DP : DP + XROWS]
    grad_xproj = jnp.concatenate([grad_xproj[:, :DTR], grad_xproj[:, RANK_PAD:]], 1)
    grad_delta = grad_late[:, DP + 256 : DP + 256 + DTR].T
    small_grads = grad_late[:, DP + 384 : DP + 384 + SMALL_USED].T

    gain_grads = jnp.pad(jnp.stack([d_in_g, d_attn_g, d_ssm_g, d_mlp_g]), ((0, 4), (0, 0)))
    gain_grads = gain_grads + swap_core(gain_grads)
    for axis in SEQ:
        gain_grads = sum(around(gain_grads, axis))
    gain_grads = lax.dynamic_slice_in_dim(gain_grads, line * ROWS_PAD + depth * PIECE, PIECE, 1)

    return (
        block_out, grad_in, gain_grads[0], grad_query, grad_keyval, grad_out, gain_grads[1], gain_grads[2],
        grad_inner, small_grads[:CONV], small_grads[4], grad_xproj, grad_delta, small_grads[5],
        small_grads[7 : 7 + STATE], small_grads[6], grad_ssmout, gain_grads[3], grad_gateup, grad_down,
    )


def solution(mesh):
    fine = Mesh(mesh.devices.reshape(RING, RING, RING, 2), ("y", "x", "z", "wt"))
    both = SEQ + ("wt",)
    weights = (
        P(SEQ),
        P(SEQ, None),
        P(SEQ, None, None),
        P(None, SEQ),
        P(SEQ),
        P(SEQ),
        P(None, None, both),
        P(None, both),
        P(both),
        P(both, None),
        P(None, both),
        P(both),
        P(None, both),
        P(both),
        P(both, None),
        P(SEQ),
        P(SEQ, None, "wt"),
        P("wt", SEQ),
    )
    rows = P(SEQ, None)
    return jax.shard_map(
        per_device, mesh=fine, in_specs=(rows,) + weights + (rows,), out_specs=(rows, rows) + weights, check_vma=False
    )
```
